32 devices in a mesh: expert: 8 (over z, x), seq: 4 (over y, core).
Axes of the slice: x: 2, y: 2, z: 4, core: 2. Of those that a mesh axis runs over, the one named last changes fastest.
Arguments:
- tokens: bfloat16 [4096, 2048], P(('expert', 'seq')), may hold values from -6 to 6
- out_grad: bfloat16 [4096, 2048], P(('expert', 'seq')), may hold values from -6 to 6
- expert_ids: int32 [4096, 8], P(('expert', 'seq')), may hold values from 0 to 127, all different within a row; in each aligned block of 128 rows (0 to 127, 128 to 255, ...) at most 12 rows name the same one
- combine: float32 [4096, 8], P(('expert', 'seq')), may hold values from 0.05 to 1
- w_gate: bfloat16 [8, 2048, 192], P('expert'), may hold values from -0.125 to 0.125
- w_up: bfloat16 [8, 2048, 192], P('expert'), may hold values from -0.125 to 0.125
- w_down: bfloat16 [8, 192, 2048], P('expert'), may hold values from -0.21875 to 0.21875
Outputs:
- grad_tokens: bfloat16 [4096, 2048], P(('expert', 'seq'))
- grad_combine: float32 [4096, 8], P(('expert', 'seq'))
- weight_grads: bfloat16 [8, 2048, 3, 192], P('expert', 'seq')
The draws below stay inside these ranges and needn't reach their ends.
Inputs may be any that keep to these rules, and one draw needn't show every extreme that they name: `expert_ids`: each token names 8 different experts. Among the tokens of one device no expert is named by more than 12. Slice j of the weights belongs to index j of the expert axis; only experts below 2 are held.
All inputs are finite; a program needn't handle non-finite values.
Results may differ from the reference program's by a relative error of at most 0.025.
Values may be sent and summed in bfloat16 or wider, within the bound.
A program may use at most 64 MiB of HBM per device.

```python
import math
import jax
import jax.numpy as jnp
import numpy as np
from jax import lax

D = 2048
HID = 768
E_ALL = 128
TOP = 8
HSPLIT = 4
TOK_DEV = 128
CAP = 12
HPART = 192
TOKENS = 4096
N_EXPERT = 8
N_SEQ = 4


def raised(drawn, own_key, source, target, parts, factor):
    owner, partner = [(jnp.arange(drawn.shape[dim]) // (drawn.shape[dim] // parts)).reshape([-1 if axis == dim else 1 for axis in range(drawn.ndim)]) for dim in (source, target)]
    chosen = jax.random.permutation(own_key, parts)[partner]
    strong = (owner == chosen) | (owner == (partner + parts // 2) % parts)
    return jnp.where(strong, factor * drawn, drawn)


def block_scale(stream_key, dims, cuts, low, largest):
    def one(dim, blocks):
        heights = jax.random.uniform(jax.random.fold_in(jax.random.fold_in(stream_key, 6), dim), (blocks,), jnp.float32, low / len(cuts), largest / len(cuts))
        return jnp.repeat(jnp.exp(heights), dims[dim] // blocks).reshape((-1,) + (1,) * (len(dims) - dim - 1))

    loudness = one(*cuts[0])
    for cut in cuts[1:]:
        loudness = loudness * one(*cut)
    return loudness


def deal_out(stream_key, own, number, rows, number_of, top, limit, skew):
    order = jax.random.permutation(stream_key, number_of)
    crowded, ordinary = shares(number_of, rows * top, limit, skew, True), shares(number_of, rows * top, limit, skew, False)
    places = jnp.arange(number_of)

    def named(lengths, rotation):
        used = int((lengths > 0).sum())
        fixed = max(1, used // 4)
        shifted = fixed + (places - fixed + rotation * (used - fixed)) % max(1, number_of - fixed)
        return jnp.zeros((number_of,), jnp.int32).at[order[jnp.where(places < fixed, places, shifted)]].set(jnp.asarray(lengths, jnp.int32))

    lengths = jnp.where(number % 4 == 0, named(crowded, number // 4), named(ordinary, number - number // 4 - 1))
    mixed = jax.random.permutation(jax.random.fold_in(own, 3), number_of)
    donor, sink = mixed[0:number_of // 2 * 2:2], mixed[1:number_of // 2 * 2:2]
    margin = jnp.minimum(lengths[donor] - 1, limit - lengths[sink]) // 2
    margin = jnp.where((donor == order[0]) | (sink == order[0]) | (lengths[sink] == 0), 0, jnp.maximum(margin, 0))
    shifted = jax.random.randint(jax.random.fold_in(own, 4), (number_of // 2,), 0, 1 << 20) % (margin + 1)
    lengths = lengths.at[donor].add(-shifted).at[sink].add(shifted)
    items = jnp.searchsorted(jnp.cumsum(lengths), jnp.arange(rows * top), side="right").astype(jnp.int32)
    grid = items.reshape(top, rows).T
    grid = grid[jax.random.permutation(jax.random.fold_in(own, 1), rows)]
    rotation = jax.random.randint(jax.random.fold_in(own, 2), (rows, 1), 0, top)
    return jnp.take_along_axis(grid, (jnp.arange(top)[None, :] + rotation) % top, axis=1)


def shares(number_of, total, most, slope, full):
    weights = [(1 << 20) // math.isqrt(standing ** slope) + 1 for standing in range(1, number_of + 1)]
    largest = most if full else min(most, max(-(-total // number_of), total * weights[0] // sum(weights)))
    least = 1 if total - largest >= number_of - 1 else 0
    holding, spare = [largest] + [least] * (number_of - 1), total - largest - least * (number_of - 1)
    while spare > 0:
        movable = [i for i in range(1, number_of) if holding[i] < largest] or [i for i in range(1, number_of) if holding[i] < most]
        pool, budget = sum([weights[i] for i in movable]), spare
        for i in movable:
            addition = min(most - holding[i], max(1, budget * weights[i] // pool), spare)
            holding[i] = holding[i] + addition
            spare = spare - addition
    return np.array(holding)


def centred(key, shape, scale, limit, cuts=(), kind=jnp.bfloat16):
    result = jax.random.normal(key, shape, jnp.float32) * scale
    if len(cuts) > 0:
        result = block_scale(key, shape, cuts, -0.22, 0.18) * result
    return jnp.clip(result, min=-limit, max=limit).astype(kind)


def heavy_noise(stream_key, dims, scale, bound, shards, heavy, kind=jnp.bfloat16):
    entries = scale * jax.random.normal(stream_key, dims, jnp.float32)
    if shards:
        entries = entries * block_scale(stream_key, dims, shards, -0.22, 0.18)
    return jnp.clip(raised(entries, jax.random.fold_in(stream_key, 3), *heavy), -bound, bound).astype(kind)


def setup_inputs(seed: int = 0) -> dict:
    splits = jax.random.split(jax.random.key(seed), 8)
    tokens = heavy_noise(splits[0], (TOKENS, D), 1.0, 6.0, ((0, 32),), (0, 1, 32, 2.75))
    out_grad = centred(splits[1], (TOKENS, D), 1.0, 6.0, ((0, 32),))
    expert_ids_keys = jax.random.split(jax.random.fold_in(splits[2], 1), TOKENS // TOK_DEV)
    expert_ids_turns = jax.random.permutation(jax.random.fold_in(splits[2], 3), TOKENS // TOK_DEV)
    expert_ids = jax.vmap(lambda own, number: deal_out(jax.random.fold_in(splits[2], 2), own, number, TOK_DEV, E_ALL, TOP, CAP, 1))(expert_ids_keys, expert_ids_turns).reshape((TOKENS, TOP))
    combine = jnp.clip(jnp.exp(math.log(1.0) - 2.9957323 * jax.random.uniform(splits[3], (TOKENS, TOP), jnp.float32) ** block_scale(splits[3], (TOKENS, TOP), ((0, 32),), -0.2, 0.2)), 0.05, 1.0)
    w_gate = centred(splits[4], (N_EXPERT, D, HPART), D ** -0.5, 0.125, ((0, 8),))
    w_up = centred(splits[5], (N_EXPERT, D, HPART), D ** -0.5, 0.125, ((0, 8),))
    w_down = centred(splits[6], (N_EXPERT, HPART, D), HID ** -0.5, 0.21875, ((0, 8),))
    return dict(tokens=tokens, out_grad=out_grad, expert_ids=expert_ids, combine=combine, w_gate=w_gate, w_up=w_up, w_down=w_down)


def reference(tokens, out_grad, expert_ids, combine, w_gate, w_up, w_down):
    blocks = N_EXPERT * N_SEQ
    experts = N_EXPERT // HSPLIT
    slice_width = HID // HSPLIT
    tok_x = tokens.reshape(blocks, TOK_DEV, D)
    tok_g = out_grad.reshape(blocks, TOK_DEV, D)
    chosen_ids = expert_ids.reshape(blocks, TOK_DEV, TOP)
    weights = combine.reshape(blocks, TOK_DEV, TOP)
    slot_ids = jnp.arange(CAP, dtype=jnp.int32)
    places = jnp.arange(TOK_DEV, dtype=jnp.int32)
    block_ids = jnp.arange(blocks, dtype=jnp.int32)
    gate_all = w_gate.reshape(experts, HSPLIT, D, slice_width)
    up_all = w_up.reshape(experts, HSPLIT, D, slice_width)
    down_all = w_down.reshape(experts, HID, D)

    def by_seq(values):
        width = values.shape[-1]
        shaped = values.reshape(N_EXPERT, N_SEQ, CAP, width)
        return jnp.transpose(shaped, (1, 0, 2, 3)).reshape(N_SEQ, N_EXPERT * CAP, width)

    def expert_pass(state_now, expert):
        grad_tok, grad_comb = state_now
        chosen = chosen_ids == expert
        routed = jnp.any(chosen, axis=2).astype(jnp.int32)
        earlier = jnp.cumsum(routed, axis=1, dtype=jnp.int32) - routed
        picker = (earlier[:, None, :] == slot_ids[None, :, None]) & (routed[:, None, :] == 1)
        filled = jnp.any(picker, axis=2)
        where_tok = jnp.sum(jnp.where(picker, places[None, None, :], 0), axis=2).astype(jnp.int32)
        weight_te = jnp.sum(jnp.where(chosen, weights, 0.0), axis=2)
        rows_w = jnp.sum(jnp.where(picker, weight_te[:, None, :], 0.0), axis=2)
        gather_x = jnp.take_along_axis(tok_x, where_tok[:, :, None], axis=1)
        gather_g = jnp.take_along_axis(tok_g, where_tok[:, :, None], axis=1)
        rows_x = jnp.where(filled[:, :, None], gather_x, jnp.zeros_like(gather_x)).astype(jnp.bfloat16)
        rows_g = jnp.where(filled[:, :, None], gather_g, jnp.zeros_like(gather_g)).astype(jnp.bfloat16)
        gate_cols = jnp.transpose(gate_all[expert], (1, 0, 2)).reshape(D, HID)
        up_cols = jnp.transpose(up_all[expert], (1, 0, 2)).reshape(D, HID)
        down_rows = down_all[expert]
        flat_x = rows_x.reshape(-1, D)
        flat_g = rows_g.reshape(-1, D)
        flat_w = rows_w.reshape(-1)
        gate_pre = jnp.dot(flat_x, gate_cols, preferred_element_type=jnp.float32)
        up_pre = jnp.dot(flat_x, up_cols, preferred_element_type=jnp.float32)
        sig_gate = jax.nn.sigmoid(gate_pre)
        act_gate = gate_pre * sig_gate
        hidden = (act_gate * up_pre).astype(jnp.bfloat16)
        expert_out = jnp.dot(hidden, down_rows, preferred_element_type=jnp.float32)
        comb_rows = jnp.sum(flat_g.astype(jnp.float32) * expert_out, axis=1)
        scaled = (flat_w[:, None] * flat_g.astype(jnp.float32)).astype(jnp.bfloat16)
        hidden_grad = jnp.dot(scaled, down_rows.T, preferred_element_type=jnp.float32)
        grad_gate = (hidden_grad * up_pre * sig_gate * (1.0 + gate_pre * (1.0 - sig_gate))).astype(jnp.bfloat16)
        grad_up = (hidden_grad * act_gate).astype(jnp.bfloat16)
        contrib = jnp.zeros((flat_x.shape[0], D), jnp.float32)
        for slice_no in range(HSPLIT):
            lo_col = slice_no * slice_width
            hi_col = lo_col + slice_width
            piece = jnp.dot(grad_gate[:, lo_col:hi_col], gate_cols[:, lo_col:hi_col].T, preferred_element_type=jnp.float32)
            piece = piece + jnp.dot(grad_up[:, lo_col:hi_col], up_cols[:, lo_col:hi_col].T, preferred_element_type=jnp.float32)
            rounded = lax.optimization_barrier(piece.astype(jnp.bfloat16))
            contrib = contrib + rounded.astype(jnp.float32)
        contrib = contrib.reshape(blocks, CAP, D)
        contrib = jnp.where(filled[:, :, None], contrib, 0.0)
        grad_tok = grad_tok.at[block_ids[:, None], where_tok].add(contrib)
        comb_te = jnp.sum(jnp.where(picker, comb_rows.reshape(blocks, CAP)[:, :, None], 0.0), axis=1)
        grad_comb = grad_comb + jnp.where(chosen, comb_te[:, :, None], 0.0)

        def per_seq(running, pieces):
            piece_x, piece_gate, piece_up, piece_scaled, piece_hidden = pieces
            term_gate = jnp.dot(piece_x.T, piece_gate, preferred_element_type=jnp.float32)
            term_up = jnp.dot(piece_x.T, piece_up, preferred_element_type=jnp.float32)
            term_down = jnp.dot(piece_scaled.T, piece_hidden, preferred_element_type=jnp.float32)
            term_all = lax.optimization_barrier(jnp.stack([term_gate, term_up, term_down]).astype(jnp.bfloat16))
            return running + term_all.astype(jnp.float32), None

        summed, _ = lax.scan(per_seq, jnp.zeros((3, D, HID), jnp.float32),
                             (by_seq(flat_x), by_seq(grad_gate), by_seq(grad_up), by_seq(scaled), by_seq(hidden)))
        grads = summed.astype(jnp.bfloat16).reshape(3, D, HSPLIT, slice_width)
        grads = jnp.transpose(grads, (2, 1, 0, 3))
        return (grad_tok, grad_comb), grads

    start = (jnp.zeros((blocks, TOK_DEV, D), jnp.float32), jnp.zeros((blocks, TOK_DEV, TOP), jnp.float32))
    (grad_tok, grad_comb), grads = lax.scan(expert_pass, start, jnp.arange(experts, dtype=jnp.int32))
    grad_tokens = grad_tok.reshape(blocks * TOK_DEV, D).astype(jnp.bfloat16)
    grad_combine = grad_comb.reshape(blocks * TOK_DEV, TOP)
    weight_grads = grads.reshape(N_EXPERT, D, 3, slice_width)
    return (grad_tokens, grad_combine, weight_grads)
```

```python
import functools

import jax
import jax.numpy as jnp
from jax import lax
from jax.experimental import pallas as pl
from jax.experimental.pallas import tpu as pltpu
from jax.sharding import PartitionSpec as P

D = 2048
HSPLIT = 4
CAP = 12
ROWS = 16
LANES = 128
MESH = pl.DeviceIdType.MESH
F32 = jnp.float32
BF16 = jnp.bfloat16


def contract_rows(left, right):
    return lax.dot_general(
        left, right, (((0,), (0,)), ((), ())), preferred_element_type=jnp.float32
    )


def contract_cols(left, right):
    return lax.dot_general(
        left, right, (((1,), (1,)), ((), ())), preferred_element_type=jnp.float32
    )


def local(tokens, out_grad, expert_ids, combine, w_gate, w_up, w_down):
    n_expert = lax.axis_size("expert")
    experts = n_expert // HSPLIT
    tok_dev = tokens.shape[0]
    slice_width = w_gate.shape[2]
    wanted = lax.broadcasted_iota(jnp.int32, (1, 1, experts), 2)
    chosen = expert_ids[:, :, None] == wanted
    routed = jnp.any(chosen, axis=1).astype(jnp.int32)
    earlier = jnp.cumsum(routed, axis=0, dtype=jnp.int32) - routed
    slot_ids = lax.broadcasted_iota(jnp.int32, (1, CAP, 1), 1)
    picker = (earlier.T[:, None, :] == slot_ids) & (routed.T[:, None, :] == 1)
    picker_bf = picker.astype(jnp.bfloat16)
    weight_te = jnp.sum(jnp.where(chosen, combine[:, :, None], 0.0), axis=1)
    send_x = jnp.einsum(
        "ect,td->ecd", picker_bf, tokens, preferred_element_type=jnp.float32
    ).astype(jnp.bfloat16)
    send_g = jnp.einsum(
        "ect,td->ecd", picker_bf, out_grad, preferred_element_type=jnp.float32
    ).astype(jnp.bfloat16)
    send_w = jnp.sum(jnp.where(picker, weight_te.T[:, None, :], 0.0), axis=2)
    out_x = jnp.repeat(send_x, HSPLIT, axis=0)
    out_g = jnp.repeat(send_g, HSPLIT, axis=0)
    out_w = jnp.repeat(send_w, HSPLIT, axis=0)
    rows_x = lax.all_to_all(out_x, "expert", split_axis=0, concat_axis=0, tiled=True)
    rows_g, rows_w = (
        lax.all_to_all(out_g, "expert", split_axis=0, concat_axis=0, tiled=True),
        lax.all_to_all(
            out_w.astype(jnp.bfloat16), "expert", split_axis=0, concat_axis=0, tiled=True
        ).astype(out_w.dtype),
    )
    flat_x = rows_x.reshape(-1, D)
    flat_g = rows_g.reshape(-1, D)
    flat_w = rows_w.reshape(-1)
    gate_cols = w_gate[0]
    up_cols = w_up[0]
    down_rows = w_down[0]
    gate_pre = jnp.dot(flat_x, gate_cols, preferred_element_type=jnp.float32)
    up_pre = jnp.dot(flat_x, up_cols, preferred_element_type=jnp.float32)
    sig_gate = jax.nn.sigmoid(gate_pre)
    act_gate = gate_pre * sig_gate
    hidden = (act_gate * up_pre).astype(jnp.bfloat16)
    expert_out = jnp.dot(hidden, down_rows, preferred_element_type=jnp.float32)
    comb_part = jnp.sum(flat_g.astype(jnp.float32) * expert_out, axis=1)
    scaled = (flat_w[:, None] * flat_g.astype(jnp.float32)).astype(jnp.bfloat16)
    hidden_grad = contract_cols(scaled, down_rows)
    grad_gate = (hidden_grad * up_pre * sig_gate * (1.0 + gate_pre * (1.0 - sig_gate))).astype(
        jnp.bfloat16
    )
    grad_up = (hidden_grad * act_gate).astype(jnp.bfloat16)
    back_rows = (contract_cols(grad_gate, gate_cols) + contract_cols(grad_up, up_cols)).astype(
        jnp.bfloat16
    )
    both_grads = jnp.concatenate([grad_gate, grad_up], axis=1)
    terms = jnp.concatenate(
        [contract_rows(flat_x, both_grads), contract_rows(scaled, hidden)], axis=1
    )
    summed = lax.psum_scatter(
        terms.astype(jnp.bfloat16), "seq", scatter_dimension=0, tiled=True
    ).astype(jnp.float32)
    weight_grads = summed.astype(jnp.bfloat16).reshape(1, summed.shape[0], 3, slice_width)
    ret_x, ret_c = (
        lax.all_to_all(
            back_rows.reshape(n_expert, CAP, D), "expert", split_axis=0, concat_axis=0, tiled=True
        ),
        lax.all_to_all(
            comb_part.reshape(n_expert, CAP).astype(jnp.bfloat16),
            "expert",
            split_axis=0,
            concat_axis=0,
            tiled=True,
        ).astype(jnp.float32),
    )
    spread = jnp.repeat(picker_bf, HSPLIT, axis=0).reshape(n_expert * CAP, tok_dev)
    grad_tokens = contract_rows(spread, ret_x.reshape(-1, D)).astype(jnp.bfloat16)
    comb_slots = jnp.sum(ret_c.reshape(experts, HSPLIT, CAP), axis=1)
    comb_te = jnp.sum(jnp.where(picker, comb_slots[:, :, None], 0.0), axis=1)
    grad_combine = jnp.sum(jnp.where(chosen, comb_te.T[:, None, :], 0.0), axis=2)
    return (grad_tokens, grad_combine, weight_grads)


def fused(n_e, n_s, tok_ref, og_ref, ids_ref, comb_ref, wg_hbm, wu_hbm, wd_hbm,
          gt_ref, gc_ref, wgr_ref,
          wg, wu, wd, outx, outs, xs, ss, xa, sa, ga, back, ret,
          w_sem, s1_send, s2_send, x_recv, s_recv, q_send, xq_recv, sq_recv, gq_recv,
          b_send, b_recv):
    me = lax.axis_index("expert")
    sq = lax.axis_index("seq")
    groups = n_e // HSPLIT
    grp = me // HSPLIT
    part = lax.rem(me, HSPLIT)
    rows = n_e * ROWS
    width = wd.shape[0]
    share = tok_ref.shape[1] // n_s
    feats = tok_ref.shape[1]

    loads = [
        pltpu.make_async_copy(src.at[0], dst, w_sem.at[i])
        for i, (src, dst) in enumerate(((wg_hbm, wg), (wu_hbm, wu), (wd_hbm, wd)))
    ]
    for load in loads:
        load.start()

    barrier = pltpu.get_barrier_semaphore()
    for step in range(1, n_e):
        pl.semaphore_signal(
            barrier, inc=1, device_id=(lax.rem(me + step, n_e), sq), device_id_type=MESH
        )
    for step in range(1, n_s):
        pl.semaphore_signal(
            barrier, inc=1, device_id=(me, lax.rem(sq + step, n_s)), device_id_type=MESH
        )

    ids = ids_ref[...]
    comb = comb_ref[...]
    toks = ids.shape[0]
    top = ids.shape[1]
    lane = lax.broadcasted_iota(jnp.int32, (toks, LANES), 1)
    e_lane = lane // ROWS
    c_lane = lax.rem(lane, ROWS)
    routed = jnp.zeros((toks, LANES), F32)
    weight = jnp.zeros((toks, LANES), F32)
    for k in range(top):
        hit = ids[:, k : k + 1] == e_lane
        routed = jnp.where(hit, 1.0, routed)
        weight = jnp.where(hit, comb[:, k : k + 1], weight)
    tri = (
        lax.broadcasted_iota(jnp.int32, (toks, toks), 1)
        < lax.broadcasted_iota(jnp.int32, (toks, toks), 0)
    ).astype(F32).astype(BF16)
    earlier = jnp.dot(tri, routed.astype(BF16), preferred_element_type=F32)
    pick = jnp.where(earlier == c_lane.astype(F32), routed, 0.0)
    pick_t = pick.T
    row_w = jnp.sum((pick * weight).T, axis=1, keepdims=True)
    used = groups * ROWS
    pick_rows = pick_t[:used].astype(BF16)
    outx[...] = jnp.dot(pick_rows, tok_ref[...], preferred_element_type=F32).astype(BF16)
    picked_g = jnp.dot(pick_rows, og_ref[...], preferred_element_type=F32)
    outs[...] = (row_w[:used] * picked_g).astype(BF16)

    def block(ref, i):
        return ref.at[pl.ds(pl.multiple_of(i * ROWS, ROWS), ROWS), :]

    xs[pl.ds(pl.multiple_of(me * ROWS, ROWS), ROWS), :] = outx[
        pl.ds(pl.multiple_of(grp * ROWS, ROWS), ROWS), :]
    ss[pl.ds(pl.multiple_of(me * ROWS, ROWS), ROWS), :] = outs[
        pl.ds(pl.multiple_of(grp * ROWS, ROWS), ROWS), :]

    pl.semaphore_wait(barrier, n_e - 1 + n_s - 1)

    def first(a, step):
        out, dst, recv = ((outx, xs, x_recv), (outs, ss, s_recv))[a]
        to = lax.rem(grp + step, groups)
        return pltpu.make_async_remote_copy(
            src_ref=block(out, to), dst_ref=block(dst, me),
            send_sem=s1_send.at[a, step - 1], recv_sem=recv.at[me],
            device_id=(to * HSPLIT + part, sq), device_id_type=MESH)

    def spread(a, source, index, step):
        dst, recv = ((xs, x_recv), (ss, s_recv))[a]
        return pltpu.make_async_remote_copy(
            src_ref=block(dst, source), dst_ref=block(dst, source),
            send_sem=s2_send.at[a, index, step - 1], recv_sem=recv.at[source],
            device_id=(grp * HSPLIT + lax.rem(part + step, HSPLIT), sq), device_id_type=MESH)

    def arrived(ref, recv, i):
        pltpu.make_async_copy(block(ref, i), block(ref, i), recv.at[i]).wait()

    sends = []

    def go(copy):
        copy.start()
        sends.append(copy)

    both = ((xs, x_recv), (ss, s_recv))
    for a in range(2):
        for step in range(1, groups):
            go(first(a, step))
        for step in range(1, HSPLIT):
            go(spread(a, me, 0, step))
    for a in range(2):
        for gstep in range(1, groups):
            source = lax.rem(grp + gstep, groups) * HSPLIT + part
            arrived(*both[a], source)
            for step in range(1, HSPLIT):
                go(spread(a, source, gstep, step))

    def to_seq(kind, src, dst, recv, step):
        peer = lax.rem(sq + step, n_s)
        return pltpu.make_async_remote_copy(
            src_ref=src(peer), dst_ref=dst.at[sq], send_sem=q_send.at[kind, step - 1],
            recv_sem=recv.at[sq], device_id=(me, peer), device_id_type=MESH)

    def columns(ref):
        return lambda peer: ref.at[:, pl.ds(pl.multiple_of(peer * share, LANES), share)]

    def rest(a):
        for step in range(1, HSPLIT):
            other = lax.rem(part + step, HSPLIT)
            for g in range(groups):
                arrived(*both[a], g * HSPLIT + other)

    rest(0)
    for step in range(1, n_s):
        go(to_seq(0, columns(xs), xa, xq_recv, step))
    loads[0].wait()
    loads[1].wait()
    x_all = xs[...]
    gate = jnp.dot(x_all, wg[...], preferred_element_type=F32)
    up = jnp.dot(x_all, wu[...], preferred_element_type=F32)
    sig = 1.0 / (1.0 + jnp.exp(-gate))
    act = gate * sig
    hidden = (act * up).astype(BF16)
    d_gate = up * sig * (1.0 + gate * (1.0 - sig))
    rest(1)
    for step in range(1, n_s):
        go(to_seq(1, columns(ss), sa, sq_recv, step))
    loads[2].wait()
    hgrad = lax.dot_general(
        ss[...], wd[...], (((1,), (1,)), ((), ())), preferred_element_type=F32)
    g_gate = (hgrad * d_gate).astype(BF16)
    g_up = (hgrad * act).astype(BF16)
    ga[sq, :, 0:width] = g_gate
    ga[sq, :, width : 2 * width] = g_up
    ga[sq, :, 2 * width : 3 * width] = hidden
    for step in range(1, n_s):
        go(to_seq(2, lambda peer: ga.at[sq], ga, gq_recv, step))

    row_part = jnp.sum(hidden.astype(F32) * hgrad, axis=1, keepdims=True)
    at_row = lax.broadcasted_iota(jnp.int32, (rows, LANES), 0)
    at_lane = lax.broadcasted_iota(jnp.int32, (rows, LANES), 1)
    diag = jnp.where(
        at_lane == grp * ROWS + lax.rem(at_row, ROWS), row_part, 0.0).astype(BF16)
    to_row = lax.broadcasted_iota(jnp.int32, (rows, rows), 0)
    of_row = lax.broadcasted_iota(jnp.int32, (rows, rows), 1)
    fold = ((to_row // ROWS == of_row // ROWS) & (lax.rem(to_row, ROWS) == CAP))
    folded = jnp.dot(fold.astype(F32).astype(BF16), diag, preferred_element_type=F32)

    contract = (((1,), (1,)), ((), ()))
    back[...] = (
        lax.dot_general(g_gate, wg[...], contract, preferred_element_type=F32)
        + lax.dot_general(g_up, wu[...], contract, preferred_element_type=F32)
    ).astype(BF16)
    back[:, 0:LANES] = jnp.where(
        lax.rem(at_row, ROWS) < CAP, back[:, 0:LANES].astype(F32), folded).astype(BF16)
    for step in range(1, n_e):
        to = lax.rem(me + step, n_e)
        go(pltpu.make_async_remote_copy(
            src_ref=block(back, to), dst_ref=block(ret, me), send_sem=b_send.at[step - 1],
            recv_sem=b_recv.at[me], device_id=(to, sq), device_id_type=MESH))
    ret[pl.ds(pl.multiple_of(me * ROWS, ROWS), ROWS), :] = back[
        pl.ds(pl.multiple_of(me * ROWS, ROWS), ROWS), :]

    xa[sq] = xs[:, pl.ds(pl.multiple_of(sq * share, LANES), share)]
    sa[sq] = ss[:, pl.ds(pl.multiple_of(sq * share, LANES), share)]
    for step in range(1, n_s):
        peer = lax.rem(sq + step, n_s)
        for ref, recv in ((xa, xq_recv), (sa, sq_recv), (ga, gq_recv)):
            pltpu.make_async_copy(ref.at[peer], ref.at[peer], recv.at[peer]).wait()
    down = (((0,), (0,)), ((), ()))
    every = n_s * rows
    grads = ga[...].reshape(every, 3 * width)
    wgr_ref[:, 0 : 2 * width] = lax.dot_general(
        xa[...].reshape(every, share), grads[:, 0 : 2 * width], down,
        preferred_element_type=F32).astype(BF16)
    wgr_ref[:, 2 * width : 3 * width] = lax.dot_general(
        sa[...].reshape(every, share), grads[:, 2 * width : 3 * width], down,
        preferred_element_type=F32).astype(BF16)

    lane_r = lax.broadcasted_iota(jnp.int32, (LANES, rows), 0)
    lane_c = lax.broadcasted_iota(jnp.int32, (LANES, rows), 1)
    widen = (lane_r == (lane_c // ROWS // HSPLIT) * ROWS + lax.rem(lane_c, ROWS))
    home = jnp.dot(
        pick.astype(BF16), widen.astype(F32).astype(BF16), preferred_element_type=F32
    ).astype(BF16)
    for step in range(1, n_e):
        arrived(ret, b_recv, lax.rem(me + step, n_e))
    gt_ref[...] = jnp.dot(home, ret[...], preferred_element_type=F32).astype(BF16)
    sums = jnp.sum(
        jnp.where(lax.rem(at_row, ROWS) == CAP, ret[:, 0:LANES].astype(F32), 0.0),
        axis=0, keepdims=True)
    per_lane = pick * sums
    cols = [
        jnp.sum(jnp.where(ids[:, k : k + 1] == e_lane, per_lane, 0.0), axis=1, keepdims=True)
        for k in range(top)
    ]
    total = jnp.zeros((toks, top), F32)
    at_k = lax.broadcasted_iota(jnp.int32, (toks, top), 1)
    for k in range(top):
        total = jnp.where(at_k == k, cols[k], total)
    gc_ref[...] = total / comb
    for copy in sends:
        copy.wait_send()


def local_fused(n_e, n_s, tokens, out_grad, expert_ids, combine, w_gate, w_up, w_down):
    toks, feats = tokens.shape
    width = w_gate.shape[2]
    share = feats // n_s
    groups = n_e // HSPLIT
    rows = n_e * ROWS
    dma = pltpu.SemaphoreType.DMA
    vmem = pl.BlockSpec(memory_space=pltpu.VMEM)
    hbm = pl.BlockSpec(memory_space=pl.ANY)
    grad_tokens, grad_combine, flat = pl.pallas_call(
        functools.partial(fused, n_e, n_s),
        out_shape=(
            jax.ShapeDtypeStruct((toks, feats), BF16),
            jax.ShapeDtypeStruct(combine.shape, F32),
            jax.ShapeDtypeStruct((share, 3 * width), BF16),
        ),
        in_specs=[vmem] * 4 + [hbm] * 3,
        out_specs=(vmem,) * 3,
        scratch_shapes=[
            pltpu.VMEM((feats, width), BF16),
            pltpu.VMEM((feats, width), BF16),
            pltpu.VMEM((width, feats), BF16),
            pltpu.VMEM((groups * ROWS, feats), BF16),
            pltpu.VMEM((groups * ROWS, feats), BF16),
            pltpu.VMEM((rows, feats), BF16),
            pltpu.VMEM((rows, feats), BF16),
            pltpu.VMEM((n_s, rows, share), BF16),
            pltpu.VMEM((n_s, rows, share), BF16),
            pltpu.VMEM((n_s, rows, 3 * width), BF16),
            pltpu.VMEM((rows, feats), BF16),
            pltpu.VMEM((rows, feats), BF16),
            dma((3,)),
            dma((2, max(1, groups - 1))),
            dma((2, groups, HSPLIT - 1)),
            dma((n_e,)),
            dma((n_e,)),
            dma((3, n_s - 1)),
            dma((n_s,)),
            dma((n_s,)),
            dma((n_s,)),
            dma((n_e - 1,)),
            dma((n_e,)),
        ],
        compiler_params=pltpu.CompilerParams(
            collective_id=0, has_side_effects=True, vmem_limit_bytes=50 * 1024 * 1024),
        cost_estimate=pl.CostEstimate(
            flops=18 * rows * feats * width, bytes_accessed=8 * feats * width,
            transcendentals=rows * width),
    )(tokens, out_grad, expert_ids, combine, w_gate, w_up, w_down)
    return grad_tokens, grad_combine, flat.reshape(1, share, 3, width)


def solution(mesh):
    in_specs = (
        P(("expert", "seq"), None),
        P(("expert", "seq"), None),
        P(("expert", "seq"), None),
        P(("expert", "seq"), None),
        P("expert", None, None),
        P("expert", None, None),
        P("expert", None, None),
    )
    out_specs = (
        P(("expert", "seq"), None),
        P(("expert", "seq"), None),
        P("expert", "seq", None, None),
    )
    n_e, n_s = mesh.shape["expert"], mesh.shape["seq"]
    fits = n_s > 1 and D % (n_s * LANES) == 0 and n_e // HSPLIT * ROWS <= LANES
    body = functools.partial(local_fused, n_e, n_s) if fits else local
    return jax.shard_map(body, mesh=mesh, in_specs=in_specs, out_specs=out_specs, check_vma=False)
```

```python
import functools

import jax
import jax.numpy as jnp
from jax import lax
from jax.experimental import pallas as pl
from jax.experimental.pallas import tpu as pltpu
from jax.sharding import PartitionSpec as P

D = 2048
HSPLIT = 4
CAP = 12
ROWS = 16
EXTRA = ROWS - CAP
CHUNKS = CAP // EXTRA
LANES = 128
MESH = pl.DeviceIdType.MESH
F32 = jnp.float32
BF16 = jnp.bfloat16


def contract_rows(left, right):
    return lax.dot_general(
        left, right, (((0,), (0,)), ((), ())), preferred_element_type=jnp.float32
    )


def contract_cols(left, right):
    return lax.dot_general(
        left, right, (((1,), (1,)), ((), ())), preferred_element_type=jnp.float32
    )


def local(tokens, out_grad, expert_ids, combine, w_gate, w_up, w_down):
    n_expert = lax.axis_size("expert")
    experts = n_expert // HSPLIT
    tok_dev = tokens.shape[0]
    slice_width = w_gate.shape[2]
    wanted = lax.broadcasted_iota(jnp.int32, (1, 1, experts), 2)
    chosen = expert_ids[:, :, None] == wanted
    routed = jnp.any(chosen, axis=1).astype(jnp.int32)
    earlier = jnp.cumsum(routed, axis=0, dtype=jnp.int32) - routed
    slot_ids = lax.broadcasted_iota(jnp.int32, (1, CAP, 1), 1)
    picker = (earlier.T[:, None, :] == slot_ids) & (routed.T[:, None, :] == 1)
    picker_bf = picker.astype(jnp.bfloat16)
    weight_te = jnp.sum(jnp.where(chosen, combine[:, :, None], 0.0), axis=1)
    send_x = jnp.einsum(
        "ect,td->ecd", picker_bf, tokens, preferred_element_type=jnp.float32
    ).astype(jnp.bfloat16)
    send_g = jnp.einsum(
        "ect,td->ecd", picker_bf, out_grad, preferred_element_type=jnp.float32
    ).astype(jnp.bfloat16)
    send_w = jnp.sum(jnp.where(picker, weight_te.T[:, None, :], 0.0), axis=2)
    out_x = jnp.repeat(send_x, HSPLIT, axis=0)
    out_g = jnp.repeat(send_g, HSPLIT, axis=0)
    out_w = jnp.repeat(send_w, HSPLIT, axis=0)
    rows_x = lax.all_to_all(out_x, "expert", split_axis=0, concat_axis=0, tiled=True)
    rows_g, rows_w = (
        lax.all_to_all(out_g, "expert", split_axis=0, concat_axis=0, tiled=True),
        lax.all_to_all(
            out_w.astype(jnp.bfloat16), "expert", split_axis=0, concat_axis=0, tiled=True
        ).astype(out_w.dtype),
    )
    flat_x = rows_x.reshape(-1, D)
    flat_g = rows_g.reshape(-1, D)
    flat_w = rows_w.reshape(-1)
    gate_cols = w_gate[0]
    up_cols = w_up[0]
    down_rows = w_down[0]
    gate_pre = jnp.dot(flat_x, gate_cols, preferred_element_type=jnp.float32)
    up_pre = jnp.dot(flat_x, up_cols, preferred_element_type=jnp.float32)
    sig_gate = jax.nn.sigmoid(gate_pre)
    act_gate = gate_pre * sig_gate
    hidden = (act_gate * up_pre).astype(jnp.bfloat16)
    expert_out = jnp.dot(hidden, down_rows, preferred_element_type=jnp.float32)
    comb_part = jnp.sum(flat_g.astype(jnp.float32) * expert_out, axis=1)
    scaled = (flat_w[:, None] * flat_g.astype(jnp.float32)).astype(jnp.bfloat16)
    hidden_grad = contract_cols(scaled, down_rows)
    grad_gate = (hidden_grad * up_pre * sig_gate * (1.0 + gate_pre * (1.0 - sig_gate))).astype(
        jnp.bfloat16
    )
    grad_up = (hidden_grad * act_gate).astype(jnp.bfloat16)
    back_rows = (contract_cols(grad_gate, gate_cols) + contract_cols(grad_up, up_cols)).astype(
        jnp.bfloat16
    )
    both_grads = jnp.concatenate([grad_gate, grad_up], axis=1)
    terms = jnp.concatenate(
        [contract_rows(flat_x, both_grads), contract_rows(scaled, hidden)], axis=1
    )
    summed = lax.psum_scatter(
        terms.astype(jnp.bfloat16), "seq", scatter_dimension=0, tiled=True
    ).astype(jnp.float32)
    weight_grads = summed.astype(jnp.bfloat16).reshape(1, summed.shape[0], 3, slice_width)
    ret_x, ret_c = (
        lax.all_to_all(
            back_rows.reshape(n_expert, CAP, D), "expert", split_axis=0, concat_axis=0, tiled=True
        ),
        lax.all_to_all(
            comb_part.reshape(n_expert, CAP).astype(jnp.bfloat16),
            "expert",
            split_axis=0,
            concat_axis=0,
            tiled=True,
        ).astype(jnp.float32),
    )
    spread = jnp.repeat(picker_bf, HSPLIT, axis=0).reshape(n_expert * CAP, tok_dev)
    grad_tokens = contract_rows(spread, ret_x.reshape(-1, D)).astype(jnp.bfloat16)
    comb_slots = jnp.sum(ret_c.reshape(experts, HSPLIT, CAP), axis=1)
    comb_te = jnp.sum(jnp.where(picker, comb_slots[:, :, None], 0.0), axis=1)
    grad_combine = jnp.sum(jnp.where(chosen, comb_te.T[:, None, :], 0.0), axis=2)
    return (grad_tokens, grad_combine, weight_grads)


def fused(n_e, n_s, tok_ref, og_ref, ids_ref, comb_ref, wg_hbm, wu_hbm, wd_hbm,
          gt_ref, gc_ref, wgr_ref,
          wg, wu, wd, outx, outs, xs, ss, xa, sa, ga, back, ret,
          w_sem, out_send, near_send, half_send, recv, half_recv,
          q_send, q_recv, b_send, b_recv):
    me = lax.axis_index("expert")
    sq = lax.axis_index("seq")
    groups = n_e // HSPLIT
    grp = me // HSPLIT
    part = lax.rem(me, HSPLIT)
    near = (part + 1 - 2 * lax.rem(part, 2), lax.rem(part + 2, HSPLIT))
    rows = n_e * ROWS
    used = groups * ROWS
    width = wd.shape[0]
    toks, feats = tok_ref.shape
    top = ids_ref.shape[0]
    share = feats // n_s
    piece = feats * EXTRA // ROWS
    packed = CHUNKS * piece
    chunk = [slice(m * piece, (m + 1) * piece) for m in range(CHUNKS)]
    last = slice(packed, feats)
    halves = (slice(0, packed // 2), slice(packed // 2, packed))

    loads = [
        pltpu.make_async_copy(src.at[0], dst, w_sem.at[i])
        for i, (src, dst) in enumerate(((wg_hbm, wg), (wu_hbm, wu), (wd_hbm, wd)))
    ]
    for load in loads:
        load.start()

    barrier = pltpu.get_barrier_semaphore()
    for step in range(1, n_e):
        pl.semaphore_signal(
            barrier, inc=1, device_id=(lax.rem(me + step, n_e), sq), device_id_type=MESH
        )
    for step in range(1, n_s):
        pl.semaphore_signal(
            barrier, inc=1, device_id=(me, lax.rem(sq + step, n_s)), device_id_type=MESH
        )

    def iota(shape, dim):
        return lax.broadcasted_iota(jnp.int32, shape, dim)

    def one_hot(mask):
        return mask.astype(F32).astype(BF16)

    def mm(left, right):
        return jnp.dot(left, right, preferred_element_type=F32)

    ids = ids_ref[...]
    comb = comb_ref[...]
    e_row = iota((used, toks), 0) // ROWS
    c_row = lax.rem(iota((used, toks), 0), ROWS)
    routed = jnp.zeros((used, toks), F32)
    weight = jnp.zeros((used, toks), F32)
    for k in range(top):
        hit = ids[k : k + 1, :] == e_row
        routed = jnp.where(hit, 1.0, routed)
        weight = jnp.where(hit, comb[k : k + 1, :], weight)
    earlier = mm(routed.astype(BF16), one_hot(iota((toks, toks), 0) < iota((toks, toks), 1)))

    def picked(slot, mask):
        return jnp.where(mask & (earlier == slot.astype(F32)), routed, 0.0)

    base = picked(c_row, c_row < CAP)
    tails = [picked(c_row - CAP + EXTRA * m, c_row >= CAP) for m in range(CHUNKS)]
    base_bf = base.astype(BF16)
    tails_bf = [tail.astype(BF16) for tail in tails]

    def gathered(ref, m):
        return mm(base_bf, ref[:, chunk[m]]) + mm(tails_bf[m], ref[:, last])

    def at(i):
        return pl.ds(pl.multiple_of(i * ROWS, ROWS), ROWS)

    sends = []

    def send(src, dst, send_sem, recv_sem, device):
        copy = pltpu.make_async_remote_copy(
            src_ref=src, dst_ref=dst, send_sem=send_sem, recv_sem=recv_sem,
            device_id=device, device_id_type=MESH)
        copy.start()
        sends.append(copy)

    def arrived(ref, sem):
        pltpu.make_async_copy(ref, ref, sem).wait()

    full = slice(0, packed)
    landing = (xs, ss)

    def pass_on(a, src, source, index):
        for n in range(2):
            send(src, landing[a].at[at(source), full], near_send.at[a, index, n],
                 recv.at[a, source], (grp * HSPLIT + near[n], sq))

    def first(a, out):
        for step in range(1, groups):
            to = lax.rem(grp + step, groups)
            send(out.at[at(to), :], landing[a].at[at(me), full], out_send.at[a, step - 1],
                 recv.at[a, me], (to * HSPLIT + part, sq))
        pass_on(a, out.at[at(grp), :], me, 0)

    def relay(a, index):
        g = lax.rem(grp + index, groups)
        for n in range(2):
            source = g * HSPLIT + near[n]
            arrived(landing[a].at[at(source), full], recv.at[a, source])
            half = landing[a].at[at(source), halves[n]]
            send(half, half, half_send.at[a, index, n], half_recv.at[a, g, n],
                 (grp * HSPLIT + near[1 - n], sq))

    def enter(a, index):
        source = lax.rem(grp + index, groups) * HSPLIT + part
        block = landing[a].at[at(source), full]
        arrived(block, recv.at[a, source])
        pass_on(a, block, source, index)

    def far(a):
        for g in range(groups):
            source = g * HSPLIT + lax.rem(part + 1 - 2 * lax.rem(part, 2) + 2, HSPLIT)
            for n in range(2):
                arrived(landing[a].at[at(source), halves[n]], half_recv.at[a, g, n])

    for m in range(CHUNKS):
        outx[:, chunk[m]] = gathered(tok_ref, m).astype(BF16)
    pl.semaphore_wait(barrier, n_e - 1 + n_s - 1)
    first(0, outx)
    for m in range(CHUNKS):
        row_w = jnp.sum((base + tails[m]) * weight, axis=1, keepdims=True)
        outs[:, chunk[m]] = (row_w * gathered(og_ref, m)).astype(BF16)
    first(1, outs)
    xs[at(me), full] = outx[at(grp), :]
    ss[at(me), full] = outs[at(grp), :]

    at_r = iota((rows, rows), 0)
    at_c = iota((rows, rows), 1)
    together = at_r // ROWS == at_c // ROWS
    r_slot = lax.rem(at_r, ROWS)
    c_slot = lax.rem(at_c, ROWS)
    unfold = [
        one_hot(together & (c_slot >= CAP) & (c_slot - CAP + EXTRA * m == r_slot))
        for m in range(CHUNKS)
    ]
    fold = [
        one_hot(together & (r_slot >= CAP) & (r_slot - CAP + EXTRA * m == c_slot))
        for m in range(CHUNKS)
    ]
    valid = lax.rem(iota((rows, width), 0), ROWS) < CAP

    def unpack(ref):
        total = mm(unfold[0], ref[:, chunk[0]])
        for m in range(1, CHUNKS):
            total = total + mm(unfold[m], ref[:, chunk[m]])
        ref[:, last] = total.astype(BF16)

    def to_seq(kind, src, dst):
        for step in range(1, n_s):
            peer = lax.rem(sq + step, n_s)
            send(src(peer), dst.at[sq], q_send.at[kind, step - 1], q_recv.at[kind, sq], (me, peer))

    def columns(ref):
        return lambda peer: ref.at[:, pl.ds(pl.multiple_of(peer * share, LANES), share)]

    across = (((1,), (1,)), ((), ()))

    relay(0, 0)
    for index in range(1, groups):
        enter(0, index)
    relay(1, 0)
    for index in range(1, groups):
        relay(0, index)
    for index in range(1, groups):
        enter(1, index)
    far(0)
    unpack(xs)
    to_seq(0, columns(xs), xa)
    loads[0].wait()
    loads[1].wait()
    gate = lax.dot_general(xs[...], wg[...], across, preferred_element_type=F32)
    up = lax.dot_general(xs[...], wu[...], across, preferred_element_type=F32)
    sig = 1.0 / (1.0 + jnp.exp(-gate))
    act = gate * sig
    hidden = jnp.where(valid, act * up, 0.0).astype(BF16)
    d_gate = up * sig * (1.0 + gate * (1.0 - sig))
    for index in range(1, groups):
        relay(1, index)
    far(1)
    unpack(ss)
    to_seq(1, columns(ss), sa)
    loads[2].wait()
    hgrad = jnp.where(
        valid, lax.dot_general(ss[...], wd[...], across, preferred_element_type=F32), 0.0)
    g_gate = (hgrad * d_gate).astype(BF16)
    g_up = (hgrad * act).astype(BF16)
    ga[sq, :, 0:width] = g_gate
    ga[sq, :, width : 2 * width] = g_up
    ga[sq, :, 2 * width : 3 * width] = hidden
    to_seq(2, lambda peer: ga.at[sq], ga)

    row_part = jnp.sum(hidden.astype(F32) * hgrad, axis=1, keepdims=True)
    back[:, packed : packed + LANES] = jnp.broadcast_to(row_part, (rows, LANES)).astype(BF16)
    tail_grad = (mm(g_gate, wg[:, last]) + mm(g_up, wu[:, last])).astype(BF16)
    keep = lax.rem(iota((rows, piece), 0), ROWS) < CAP
    for m in range(CHUNKS):
        whole = mm(g_gate, wg[:, chunk[m]]) + mm(g_up, wu[:, chunk[m]])
        back[:, chunk[m]] = jnp.where(keep, whole, mm(fold[m], tail_grad)).astype(BF16)
    others = [(g, p) for g in range(1, groups) for p in range(HSPLIT)]
    others += [(0, p) for p in range(1, HSPLIT)]
    for count, (g, p) in enumerate(others):
        to = lax.rem(grp + g, groups) * HSPLIT + lax.rem(part + p, HSPLIT)
        send(back.at[at(to), :], ret.at[at(me), :], b_send.at[count], b_recv.at[me], (to, sq))
    ret[at(me), :] = back[at(me), :]

    widen = one_hot(
        (iota((rows, used), 0) // ROWS // HSPLIT == iota((rows, used), 1) // ROWS)
        & (lax.rem(iota((rows, used), 0), ROWS) == lax.rem(iota((rows, used), 1), ROWS)))
    home = mm(widen, base_bf).T.astype(BF16)
    home_tails = [mm(widen, tail).T.astype(BF16) for tail in tails_bf]
    gather = one_hot(
        (iota((used, rows), 1) // ROWS // HSPLIT == iota((used, rows), 0) // ROWS)
        & (lax.rem(iota((used, rows), 1), ROWS) == lax.rem(iota((used, rows), 0), ROWS)))

    xa[sq] = xs[:, pl.ds(pl.multiple_of(sq * share, LANES), share)]
    sa[sq] = ss[:, pl.ds(pl.multiple_of(sq * share, LANES), share)]
    for step in range(1, n_s):
        peer = lax.rem(sq + step, n_s)
        for kind, ref in enumerate((xa, sa, ga)):
            arrived(ref.at[peer], q_recv.at[kind, peer])
    down = (((0,), (0,)), ((), ()))
    every = n_s * rows
    grads = ga[...].reshape(every, 3 * width)
    wgr_ref[0 : 2 * width, :] = lax.dot_general(
        grads[:, 0 : 2 * width], xa[...].reshape(every, share), down,
        preferred_element_type=F32).astype(BF16)
    wgr_ref[2 * width : 3 * width, :] = lax.dot_general(
        grads[:, 2 * width : 3 * width], sa[...].reshape(every, share), down,
        preferred_element_type=F32).astype(BF16)

    for g, p in others:
        source = lax.rem(grp + g, groups) * HSPLIT + lax.rem(part + p, HSPLIT)
        arrived(ret.at[at(source), :], b_recv.at[source])
    tail_sum = jnp.zeros((toks, piece), F32)
    for m in range(CHUNKS):
        gt_ref[:, chunk[m]] = mm(home, ret[:, chunk[m]]).astype(BF16)
        tail_sum = tail_sum + mm(home_tails[m], ret[:, chunk[m]])
    gt_ref[:, last] = tail_sum.astype(BF16)
    per_slot = base * mm(gather, ret[:, packed : packed + LANES])
    at_k = iota((top, toks), 0)
    total = jnp.zeros((top, toks), F32)
    for k in range(top):
        mine = jnp.sum(jnp.where(ids[k : k + 1, :] == e_row, per_slot, 0.0), axis=0, keepdims=True)
        total = jnp.where(at_k == k, mine, total)
    gc_ref[...] = total / comb
    for copy in sends:
        copy.wait_send()


def local_fused(n_e, n_s, tokens, out_grad, expert_ids, combine, w_gate, w_up, w_down):
    toks, feats = tokens.shape
    width = w_gate.shape[2]
    share = feats // n_s
    groups = n_e // HSPLIT
    rows = n_e * ROWS
    packed = feats * CAP // ROWS
    dma = pltpu.SemaphoreType.DMA
    vmem = pl.BlockSpec(memory_space=pltpu.VMEM)
    hbm = pl.BlockSpec(memory_space=pl.ANY)
    grad_tokens, grad_combine, flat = pl.pallas_call(
        functools.partial(fused, n_e, n_s),
        out_shape=(
            jax.ShapeDtypeStruct((toks, feats), BF16),
            jax.ShapeDtypeStruct(combine.shape[::-1], F32),
            jax.ShapeDtypeStruct((3 * width, share), BF16),
        ),
        in_specs=[vmem] * 4 + [hbm] * 3,
        out_specs=(vmem,) * 3,
        scratch_shapes=[
            pltpu.VMEM((width, feats), BF16),
            pltpu.VMEM((width, feats), BF16),
            pltpu.VMEM((width, feats), BF16),
            pltpu.VMEM((groups * ROWS, packed), BF16),
            pltpu.VMEM((groups * ROWS, packed), BF16),
            pltpu.VMEM((rows, feats), BF16),
            pltpu.VMEM((rows, feats), BF16),
            pltpu.VMEM((n_s, rows, share), BF16),
            pltpu.VMEM((n_s, rows, share), BF16),
            pltpu.VMEM((n_s, rows, 3 * width), BF16),
            pltpu.VMEM((rows, packed + LANES), BF16),
            pltpu.VMEM((rows, packed + LANES), BF16),
            dma((3,)),
            dma((2, max(1, groups - 1))),
            dma((2, groups, 2)),
            dma((2, groups, 2)),
            dma((2, n_e)),
            dma((2, groups, 2)),
            dma((3, n_s - 1)),
            dma((3, n_s)),
            dma((n_e - 1,)),
            dma((n_e,)),
        ],
        compiler_params=pltpu.CompilerParams(
            collective_id=0, has_side_effects=True, vmem_limit_bytes=50 * 1024 * 1024),
        cost_estimate=pl.CostEstimate(
            flops=18 * rows * feats * width, bytes_accessed=8 * feats * width,
            transcendentals=rows * width),
    )(
        tokens, out_grad, expert_ids.T, combine.T,
        w_gate.transpose(0, 2, 1), w_up.transpose(0, 2, 1), w_down,
    )
    weight_grads = flat.reshape(1, 3, width, share).transpose(0, 3, 1, 2)
    return grad_tokens, grad_combine.T, weight_grads


def solution(mesh):
    in_specs = (
        P(("expert", "seq"), None),
        P(("expert", "seq"), None),
        P(("expert", "seq"), None),
        P(("expert", "seq"), None),
        P("expert", None, None),
        P("expert", None, None),
        P("expert", None, None),
    )
    out_specs = (
        P(("expert", "seq"), None),
        P(("expert", "seq"), None),
        P("expert", "seq", None, None),
    )
    n_e, n_s = mesh.shape["expert"], mesh.shape["seq"]
    fits = n_s > 1 and D % (n_s * LANES) == 0
    body = functools.partial(local_fused, n_e, n_s) if fits else local
    return jax.shard_map(body, mesh=mesh, in_specs=in_specs, out_specs=out_specs, check_vma=False)
```

```python
import functools

import jax
import jax.numpy as jnp
from jax import lax
from jax.experimental import pallas as pl
from jax.experimental.pallas import tpu as pltpu
from jax.sharding import PartitionSpec as P

D = 2048
HSPLIT = 4
CAP = 12
ROWS = 16
EXTRA = ROWS - CAP
CHUNKS = CAP // EXTRA
LANES = 128
VMEM_BYTES = 63 * 1024 * 1024
MESH = pl.DeviceIdType.MESH
F32 = jnp.float32
BF16 = jnp.bfloat16


def contract_rows(left, right):
    return lax.dot_general(
        left, right, (((0,), (0,)), ((), ())), preferred_element_type=jnp.float32
    )


def contract_cols(left, right):
    return lax.dot_general(
        left, right, (((1,), (1,)), ((), ())), preferred_element_type=jnp.float32
    )


def local(tokens, out_grad, expert_ids, combine, w_gate, w_up, w_down):
    n_expert = lax.axis_size("expert")
    experts = n_expert // HSPLIT
    tok_dev = tokens.shape[0]
    slice_width = w_gate.shape[2]
    wanted = lax.broadcasted_iota(jnp.int32, (1, 1, experts), 2)
    chosen = expert_ids[:, :, None] == wanted
    routed = jnp.any(chosen, axis=1).astype(jnp.int32)
    earlier = jnp.cumsum(routed, axis=0, dtype=jnp.int32) - routed
    slot_ids = lax.broadcasted_iota(jnp.int32, (1, CAP, 1), 1)
    picker = (earlier.T[:, None, :] == slot_ids) & (routed.T[:, None, :] == 1)
    picker_bf = picker.astype(jnp.bfloat16)
    weight_te = jnp.sum(jnp.where(chosen, combine[:, :, None], 0.0), axis=1)
    send_x = jnp.einsum(
        "ect,td->ecd", picker_bf, tokens, preferred_element_type=jnp.float32
    ).astype(jnp.bfloat16)
    send_g = jnp.einsum(
        "ect,td->ecd", picker_bf, out_grad, preferred_element_type=jnp.float32
    ).astype(jnp.bfloat16)
    send_w = jnp.sum(jnp.where(picker, weight_te.T[:, None, :], 0.0), axis=2)
    out_x = jnp.repeat(send_x, HSPLIT, axis=0)
    out_g = jnp.repeat(send_g, HSPLIT, axis=0)
    out_w = jnp.repeat(send_w, HSPLIT, axis=0)
    rows_x = lax.all_to_all(out_x, "expert", split_axis=0, concat_axis=0, tiled=True)
    rows_g, rows_w = (
        lax.all_to_all(out_g, "expert", split_axis=0, concat_axis=0, tiled=True),
        lax.all_to_all(
            out_w.astype(jnp.bfloat16), "expert", split_axis=0, concat_axis=0, tiled=True
        ).astype(out_w.dtype),
    )
    flat_x = rows_x.reshape(-1, D)
    flat_g = rows_g.reshape(-1, D)
    flat_w = rows_w.reshape(-1)
    gate_cols = w_gate[0]
    up_cols = w_up[0]
    down_rows = w_down[0]
    gate_pre = jnp.dot(flat_x, gate_cols, preferred_element_type=jnp.float32)
    up_pre = jnp.dot(flat_x, up_cols, preferred_element_type=jnp.float32)
    sig_gate = jax.nn.sigmoid(gate_pre)
    act_gate = gate_pre * sig_gate
    hidden = (act_gate * up_pre).astype(jnp.bfloat16)
    expert_out = jnp.dot(hidden, down_rows, preferred_element_type=jnp.float32)
    comb_part = jnp.sum(flat_g.astype(jnp.float32) * expert_out, axis=1)
    scaled = (flat_w[:, None] * flat_g.astype(jnp.float32)).astype(jnp.bfloat16)
    hidden_grad = contract_cols(scaled, down_rows)
    grad_gate = (hidden_grad * up_pre * sig_gate * (1.0 + gate_pre * (1.0 - sig_gate))).astype(
        jnp.bfloat16
    )
    grad_up = (hidden_grad * act_gate).astype(jnp.bfloat16)
    back_rows = (contract_cols(grad_gate, gate_cols) + contract_cols(grad_up, up_cols)).astype(
        jnp.bfloat16
    )
    both_grads = jnp.concatenate([grad_gate, grad_up], axis=1)
    terms = jnp.concatenate(
        [contract_rows(flat_x, both_grads), contract_rows(scaled, hidden)], axis=1
    )
    summed = lax.psum_scatter(
        terms.astype(jnp.bfloat16), "seq", scatter_dimension=0, tiled=True
    ).astype(jnp.float32)
    weight_grads = summed.astype(jnp.bfloat16).reshape(1, summed.shape[0], 3, slice_width)
    ret_x, ret_c = (
        lax.all_to_all(
            back_rows.reshape(n_expert, CAP, D), "expert", split_axis=0, concat_axis=0, tiled=True
        ),
        lax.all_to_all(
            comb_part.reshape(n_expert, CAP).astype(jnp.bfloat16),
            "expert",
            split_axis=0,
            concat_axis=0,
            tiled=True,
        ).astype(jnp.float32),
    )
    spread = jnp.repeat(picker_bf, HSPLIT, axis=0).reshape(n_expert * CAP, tok_dev)
    grad_tokens = contract_rows(spread, ret_x.reshape(-1, D)).astype(jnp.bfloat16)
    comb_slots = jnp.sum(ret_c.reshape(experts, HSPLIT, CAP), axis=1)
    comb_te = jnp.sum(jnp.where(picker, comb_slots[:, :, None], 0.0), axis=1)
    grad_combine = jnp.sum(jnp.where(chosen, comb_te.T[:, None, :], 0.0), axis=2)
    return (grad_tokens, grad_combine, weight_grads)


def fused(n_e, n_s, tok_hbm, og_hbm, ids_hbm, comb_hbm, wg_hbm, wu_hbm, wd_hbm,
          gt_ref, gc_ref, wgr_ref,
          tok_ref, og_ref, ids_ref, comb_ref, wgu, wd, outx, outs, xs, ss, xa, sa, ga, back, ret,
          w_sem, out_send, near_send, half_send, recv, half_recv,
          q_send, q_recv, g_send, g_recv, b_send, b_recv):
    me = lax.axis_index("expert")
    sq = lax.axis_index("seq")
    groups = n_e // HSPLIT
    grp = me // HSPLIT
    part = lax.rem(me, HSPLIT)
    near = (part + 1 - 2 * lax.rem(part, 2), lax.rem(part + 2, HSPLIT))
    rows = n_e * ROWS
    used = groups * ROWS
    width = wd.shape[0]
    toks, feats = tok_ref.shape
    top = ids_ref.shape[0]
    share = feats // n_s
    piece = feats * EXTRA // ROWS
    packed = CHUNKS * piece
    chunk = [slice(m * piece, (m + 1) * piece) for m in range(CHUNKS)]
    last = slice(packed, feats)
    halves = (slice(0, packed // 2), slice(packed // 2, packed))

    wg = wgu.at[0:width, :]
    wu = wgu.at[width : 2 * width, :]
    loads = [
        pltpu.make_async_copy(src, dst, w_sem.at[i])
        for i, (src, dst) in enumerate((
            (ids_hbm, ids_ref), (comb_hbm, comb_ref), (tok_hbm, tok_ref), (og_hbm, og_ref),
            (wg_hbm.at[0], wg), (wu_hbm.at[0], wu), (wd_hbm.at[0], wd)))
    ]
    for load in loads:
        load.start()

    barrier = pltpu.get_barrier_semaphore()
    for step in range(1, n_e):
        pl.semaphore_signal(
            barrier, inc=1, device_id=(lax.rem(me + step, n_e), sq), device_id_type=MESH
        )
    for step in range(1, n_s):
        pl.semaphore_signal(
            barrier, inc=1, device_id=(me, lax.rem(sq + step, n_s)), device_id_type=MESH
        )

    def iota(shape, dim):
        return lax.broadcasted_iota(jnp.int32, shape, dim)

    def one_hot(mask):
        return mask.astype(F32).astype(BF16)

    def mm(left, right):
        return jnp.dot(left, right, preferred_element_type=F32)

    loads[0].wait()
    loads[1].wait()
    ids = ids_ref[...]
    comb = comb_ref[...]
    e_row = iota((used, toks), 0) // ROWS
    c_row = lax.rem(iota((used, toks), 0), ROWS)
    routed = jnp.zeros((used, toks), F32)
    weight = jnp.zeros((used, toks), F32)
    for k in range(top):
        hit = ids[k : k + 1, :] == e_row
        routed = jnp.where(hit, 1.0, routed)
        weight = jnp.where(hit, comb[k : k + 1, :], weight)
    earlier = mm(routed.astype(BF16), one_hot(iota((toks, toks), 0) < iota((toks, toks), 1)))

    def picked(slot, mask):
        return jnp.where(mask & (earlier == slot.astype(F32)), routed, 0.0)

    base = picked(c_row, c_row < CAP)
    tails = [picked(c_row - CAP + EXTRA * m, c_row >= CAP) for m in range(CHUNKS)]
    base_bf = base.astype(BF16)
    tails_bf = [tail.astype(BF16) for tail in tails]

    def gathered(ref, m):
        return mm(base_bf, ref[:, chunk[m]]) + mm(tails_bf[m], ref[:, last])

    def at(i):
        return pl.ds(pl.multiple_of(i * ROWS, ROWS), ROWS)

    sends = []

    def send(src, dst, send_sem, recv_sem, device):
        copy = pltpu.make_async_remote_copy(
            src_ref=src, dst_ref=dst, send_sem=send_sem, recv_sem=recv_sem,
            device_id=device, device_id_type=MESH)
        copy.start()
        sends.append(copy)

    def arrived(ref, sem):
        pltpu.make_async_copy(ref, ref, sem).wait()

    full = slice(0, packed)
    landing = (xs, ss)

    def pass_on(a, src, source, index):
        for n in range(2):
            send(src, landing[a].at[at(source), full], near_send.at[a, index, n],
                 recv.at[a, source], (grp * HSPLIT + near[n], sq))

    def first(a, out):
        for step in range(1, groups):
            to = lax.rem(grp + step, groups)
            send(out.at[at(to), :], landing[a].at[at(me), full], out_send.at[a, step - 1],
                 recv.at[a, me], (to * HSPLIT + part, sq))
        pass_on(a, out.at[at(grp), :], me, 0)

    def relay(a, index):
        g = lax.rem(grp + index, groups)
        for n in range(2):
            source = g * HSPLIT + near[n]
            arrived(landing[a].at[at(source), full], recv.at[a, source])
            half = landing[a].at[at(source), halves[n]]
            send(half, half, half_send.at[a, index, n], half_recv.at[a, g, n],
                 (grp * HSPLIT + near[1 - n], sq))

    def enter(a, index):
        source = lax.rem(grp + index, groups) * HSPLIT + part
        block = landing[a].at[at(source), full]
        arrived(block, recv.at[a, source])
        pass_on(a, block, source, index)

    def far(a, index):
        g = lax.rem(grp + index, groups)
        source = g * HSPLIT + lax.rem(near[0] + 2, HSPLIT)
        for n in range(2):
            arrived(landing[a].at[at(source), halves[n]], half_recv.at[a, g, n])

    loads[2].wait()
    for m in range(CHUNKS):
        outx[:, chunk[m]] = gathered(tok_ref, m).astype(BF16)
    pl.semaphore_wait(barrier, n_e - 1 + n_s - 1)
    first(0, outx)
    loads[3].wait()
    for m in range(CHUNKS):
        row_w = jnp.sum((base + tails[m]) * weight, axis=1, keepdims=True)
        outs[:, chunk[m]] = (row_w * gathered(og_ref, m)).astype(BF16)
    first(1, outs)
    xs[at(me), full] = outx[at(grp), :]
    ss[at(me), full] = outs[at(grp), :]

    def slots(count):
        at_r = iota((count, count), 0)
        at_c = iota((count, count), 1)
        return at_r // ROWS == at_c // ROWS, lax.rem(at_r, ROWS), lax.rem(at_c, ROWS)

    quad = HSPLIT * ROWS
    together, r_slot, c_slot = slots(quad)
    unfold = [
        one_hot(together & (c_slot >= CAP) & (c_slot - CAP + EXTRA * m == r_slot))
        for m in range(CHUNKS)
    ]
    together, r_slot, c_slot = slots(rows)
    fold = [
        one_hot(together & (r_slot >= CAP) & (r_slot - CAP + EXTRA * m == c_slot))
        for m in range(CHUNKS)
    ]
    valid = lax.rem(iota((width, rows), 1), ROWS) < CAP
    shares = (xa, sa)

    def group_rows(index):
        return pl.ds(pl.multiple_of(lax.rem(grp + index, groups) * quad, quad), quad)

    def complete(a, index):
        far(a, index)
        ref = landing[a]
        here = group_rows(index)
        total = mm(unfold[0], ref[here, chunk[0]])
        for m in range(1, CHUNKS):
            total = total + mm(unfold[m], ref[here, chunk[m]])
        ref[here, last] = total.astype(BF16)
        for step in range(1, n_s):
            peer = lax.rem(sq + step, n_s)
            mine = pl.ds(pl.multiple_of(peer * share, LANES), share)
            send(ref.at[here, mine], shares[a].at[sq, here, :], q_send.at[a, index, step - 1],
                 q_recv.at[a, sq, index], (me, peer))

    across = (((1,), (1,)), ((), ()))

    relay(0, 0)
    for index in range(1, groups):
        enter(0, index)
    complete(0, 0)
    relay(1, 0)
    for index in range(1, groups):
        relay(0, index)
    for index in range(1, groups):
        enter(1, index)
    complete(1, 0)
    for index in range(1, groups):
        complete(0, index)
    loads[4].wait()
    loads[5].wait()
    gate_up = lax.dot_general(wgu[...], xs[...], across, preferred_element_type=F32)
    gate = gate_up[0:width]
    up = gate_up[width : 2 * width]
    sig = 1.0 / (1.0 + jnp.exp(-gate))
    act = gate * sig
    hidden = jnp.where(valid, act * up, 0.0).astype(BF16)
    d_gate = up * sig * (1.0 + gate * (1.0 - sig))
    for index in range(1, groups):
        relay(1, index)
    for index in range(1, groups):
        complete(1, index)
    loads[6].wait()
    hgrad = jnp.where(
        valid, lax.dot_general(wd[...], ss[...], across, preferred_element_type=F32), 0.0)
    g_gate_t = (hgrad * d_gate).astype(BF16)
    g_up_t = (hgrad * act).astype(BF16)

    def lanes_of(s):
        return pl.ds(pl.multiple_of(s * rows, LANES), rows)

    ga[0:width, lanes_of(sq)] = g_gate_t
    ga[width : 2 * width, lanes_of(sq)] = g_up_t
    ga[2 * width : 3 * width, lanes_of(sq)] = hidden
    pairs = n_s // 2
    core = lax.rem(sq, 2)
    mate = sq + 1 - 2 * core
    peers = [lax.rem(sq // 2 + step, pairs) * 2 + core for step in range(1, pairs)]

    def to_seq(source, count, peer):
        block = ga.at[:, lanes_of(source)]
        send(block, block, g_send.at[count], g_recv.at[source], (me, peer))

    for count, peer in enumerate(peers):
        to_seq(sq, count, peer)
    to_seq(sq, pairs - 1, mate)

    row_part = jnp.sum(hidden.astype(F32) * hgrad, axis=0, keepdims=True)
    back[:, packed : packed + LANES] = jnp.broadcast_to(row_part, (LANES, rows)).T.astype(BF16)
    g_gate = g_gate_t.T
    g_up = g_up_t.T
    tail_grad = (mm(g_gate, wg[:, last]) + mm(g_up, wu[:, last])).astype(BF16)
    keep = lax.rem(iota((rows, piece), 0), ROWS) < CAP
    for m in range(CHUNKS):
        whole = mm(g_gate, wg[:, chunk[m]]) + mm(g_up, wu[:, chunk[m]])
        back[:, chunk[m]] = jnp.where(keep, whole, mm(fold[m], tail_grad)).astype(BF16)
    others = [(g, p) for g in range(1, groups) for p in range(HSPLIT)]
    others += [(0, p) for p in range(1, HSPLIT)]
    for count, (g, p) in enumerate(others):
        to = lax.rem(grp + g, groups) * HSPLIT + lax.rem(part + p, HSPLIT)
        send(back.at[at(to), :], ret.at[at(me), :], b_send.at[count], b_recv.at[me], (to, sq))
    ret[at(me), :] = back[at(me), :]

    widen = one_hot(
        (iota((rows, used), 0) // ROWS // HSPLIT == iota((rows, used), 1) // ROWS)
        & (lax.rem(iota((rows, used), 0), ROWS) == lax.rem(iota((rows, used), 1), ROWS)))
    home = mm(widen, base_bf).T.astype(BF16)
    home_tails = [mm(widen, tail).T.astype(BF16) for tail in tails_bf]
    gather = one_hot(
        (iota((used, rows), 1) // ROWS // HSPLIT == iota((used, rows), 0) // ROWS)
        & (lax.rem(iota((used, rows), 1), ROWS) == lax.rem(iota((used, rows), 0), ROWS)))

    xa[sq] = xs[:, pl.ds(pl.multiple_of(sq * share, LANES), share)]
    sa[sq] = ss[:, pl.ds(pl.multiple_of(sq * share, LANES), share)]
    for count, peer in enumerate(peers):
        arrived(ga.at[:, lanes_of(peer)], g_recv.at[peer])
        to_seq(peer, pairs + count, mate)
    for step in range(1, n_s):
        peer = lax.rem(sq + step, n_s)
        for a, ref in enumerate(shares):
            for index in range(groups):
                arrived(ref.at[peer, group_rows(index), :], q_recv.at[a, peer, index])
    arrived(ga.at[:, lanes_of(mate)], g_recv.at[mate])
    for peer in peers:
        twin = peer + 1 - 2 * core
        arrived(ga.at[:, lanes_of(twin)], g_recv.at[twin])
    every = n_s * rows
    wgr_ref[0 : 2 * width, :] = mm(
        ga[0 : 2 * width, :], xa[...].reshape(every, share)).astype(BF16)
    wgr_ref[2 * width : 3 * width, :] = mm(
        ga[2 * width : 3 * width, :], sa[...].reshape(every, share)).astype(BF16)

    for g, p in others:
        source = lax.rem(grp + g, groups) * HSPLIT + lax.rem(part + p, HSPLIT)
        arrived(ret.at[at(source), :], b_recv.at[source])
    tail_sum = jnp.zeros((toks, piece), F32)
    for m in range(CHUNKS):
        gt_ref[:, chunk[m]] = mm(home, ret[:, chunk[m]]).astype(BF16)
        tail_sum = tail_sum + mm(home_tails[m], ret[:, chunk[m]])
    gt_ref[:, last] = tail_sum.astype(BF16)
    per_slot = base * mm(gather, ret[:, packed : packed + LANES])
    at_k = iota((top, toks), 0)
    total = jnp.zeros((top, toks), F32)
    for k in range(top):
        mine = jnp.sum(jnp.where(ids[k : k + 1, :] == e_row, per_slot, 0.0), axis=0, keepdims=True)
        total = jnp.where(at_k == k, mine, total)
    gc_ref[...] = total / comb
    for copy in sends:
        copy.wait_send()


def local_fused(n_e, n_s, tokens, out_grad, expert_ids, combine, w_gate, w_up, w_down):
    toks, feats = tokens.shape
    width = w_gate.shape[2]
    share = feats // n_s
    groups = n_e // HSPLIT
    rows = n_e * ROWS
    packed = feats * CAP // ROWS
    dma = pltpu.SemaphoreType.DMA
    vmem = pl.BlockSpec(memory_space=pltpu.VMEM)
    hbm = pl.BlockSpec(memory_space=pl.ANY)
    grad_tokens, grad_combine, flat = pl.pallas_call(
        functools.partial(fused, n_e, n_s),
        out_shape=(
            jax.ShapeDtypeStruct((toks, feats), BF16),
            jax.ShapeDtypeStruct(combine.shape[::-1], F32),
            jax.ShapeDtypeStruct((3 * width, share), BF16),
        ),
        in_specs=[hbm] * 7,
        out_specs=(vmem,) * 3,
        scratch_shapes=[
            pltpu.VMEM((toks, feats), BF16),
            pltpu.VMEM((toks, feats), BF16),
            pltpu.VMEM(expert_ids.shape[::-1], jnp.int32),
            pltpu.VMEM(combine.shape[::-1], F32),
            pltpu.VMEM((2 * width, feats), BF16),
            pltpu.VMEM((width, feats), BF16),
            pltpu.VMEM((groups * ROWS, packed), BF16),
            pltpu.VMEM((groups * ROWS, packed), BF16),
            pltpu.VMEM((rows, feats), BF16),
            pltpu.VMEM((rows, feats), BF16),
            pltpu.VMEM((n_s, rows, share), BF16),
            pltpu.VMEM((n_s, rows, share), BF16),
            pltpu.VMEM((3 * width, n_s * rows), BF16),
            pltpu.VMEM((rows, packed + LANES), BF16),
            pltpu.VMEM((rows, packed + LANES), BF16),
            dma((7,)),
            dma((2, max(1, groups - 1))),
            dma((2, groups, 2)),
            dma((2, groups, 2)),
            dma((2, n_e)),
            dma((2, groups, 2)),
            dma((2, groups, n_s - 1)),
            dma((2, n_s, groups)),
            dma((n_s - 1,)),
            dma((n_s,)),
            dma((n_e - 1,)),
            dma((n_e,)),
        ],
        compiler_params=pltpu.CompilerParams(
            collective_id=0, has_side_effects=True, vmem_limit_bytes=VMEM_BYTES),
        cost_estimate=pl.CostEstimate(
            flops=18 * rows * feats * width, bytes_accessed=8 * feats * width,
            transcendentals=rows * width),
    )(
        tokens, out_grad, expert_ids.T, combine.T,
        w_gate.transpose(0, 2, 1), w_up.transpose(0, 2, 1), w_down,
    )
    weight_grads = flat.reshape(1, 3, width, share).transpose(0, 3, 1, 2)
    return grad_tokens, grad_combine.T, weight_grads


def solution(mesh):
    in_specs = (
        P(("expert", "seq"), None),
        P(("expert", "seq"), None),
        P(("expert", "seq"), None),
        P(("expert", "seq"), None),
        P("expert", None, None),
        P("expert", None, None),
        P("expert", None, None),
    )
    out_specs = (
        P(("expert", "seq"), None),
        P(("expert", "seq"), None),
        P("expert", "seq", None, None),
    )
    n_e, n_s = mesh.shape["expert"], mesh.shape["seq"]
    fits = n_s % 2 == 0 and D % (n_s * LANES) == 0
    body = functools.partial(local_fused, n_e, n_s) if fits else local
    return jax.shard_map(body, mesh=mesh, in_specs=in_specs, out_specs=out_specs, check_vma=False)
```

```python
import functools

import jax
import jax.numpy as jnp
from jax import lax
from jax.experimental import pallas as pl
from jax.experimental.pallas import tpu as pltpu
from jax.sharding import PartitionSpec as P

D = 2048
HSPLIT = 4
CAP = 12
ROWS = 16
EXTRA = ROWS - CAP
CHUNKS = CAP // EXTRA
LANES = 128
VMEM_BYTES = 61500 * 1024
MESH = pl.DeviceIdType.MESH
F32 = jnp.float32
BF16 = jnp.bfloat16


def contract_rows(left, right):
    return lax.dot_general(
        left, right, (((0,), (0,)), ((), ())), preferred_element_type=jnp.float32
    )


def contract_cols(left, right):
    return lax.dot_general(
        left, right, (((1,), (1,)), ((), ())), preferred_element_type=jnp.float32
    )


def local(tokens, out_grad, expert_ids, combine, w_gate, w_up, w_down):
    n_expert = lax.axis_size("expert")
    experts = n_expert // HSPLIT
    tok_dev = tokens.shape[0]
    slice_width = w_gate.shape[2]
    wanted = lax.broadcasted_iota(jnp.int32, (1, 1, experts), 2)
    chosen = expert_ids[:, :, None] == wanted
    routed = jnp.any(chosen, axis=1).astype(jnp.int32)
    earlier = jnp.cumsum(routed, axis=0, dtype=jnp.int32) - routed
    slot_ids = lax.broadcasted_iota(jnp.int32, (1, CAP, 1), 1)
    picker = (earlier.T[:, None, :] == slot_ids) & (routed.T[:, None, :] == 1)
    picker_bf = picker.astype(jnp.bfloat16)
    weight_te = jnp.sum(jnp.where(chosen, combine[:, :, None], 0.0), axis=1)
    send_x = jnp.einsum(
        "ect,td->ecd", picker_bf, tokens, preferred_element_type=jnp.float32
    ).astype(jnp.bfloat16)
    send_g = jnp.einsum(
        "ect,td->ecd", picker_bf, out_grad, preferred_element_type=jnp.float32
    ).astype(jnp.bfloat16)
    send_w = jnp.sum(jnp.where(picker, weight_te.T[:, None, :], 0.0), axis=2)
    out_x = jnp.repeat(send_x, HSPLIT, axis=0)
    out_g = jnp.repeat(send_g, HSPLIT, axis=0)
    out_w = jnp.repeat(send_w, HSPLIT, axis=0)
    rows_x = lax.all_to_all(out_x, "expert", split_axis=0, concat_axis=0, tiled=True)
    rows_g, rows_w = (
        lax.all_to_all(out_g, "expert", split_axis=0, concat_axis=0, tiled=True),
        lax.all_to_all(
            out_w.astype(jnp.bfloat16), "expert", split_axis=0, concat_axis=0, tiled=True
        ).astype(out_w.dtype),
    )
    flat_x = rows_x.reshape(-1, D)
    flat_g = rows_g.reshape(-1, D)
    flat_w = rows_w.reshape(-1)
    gate_cols = w_gate[0]
    up_cols = w_up[0]
    down_rows = w_down[0]
    gate_pre = jnp.dot(flat_x, gate_cols, preferred_element_type=jnp.float32)
    up_pre = jnp.dot(flat_x, up_cols, preferred_element_type=jnp.float32)
    sig_gate = jax.nn.sigmoid(gate_pre)
    act_gate = gate_pre * sig_gate
    hidden = (act_gate * up_pre).astype(jnp.bfloat16)
    expert_out = jnp.dot(hidden, down_rows, preferred_element_type=jnp.float32)
    comb_part = jnp.sum(flat_g.astype(jnp.float32) * expert_out, axis=1)
    scaled = (flat_w[:, None] * flat_g.astype(jnp.float32)).astype(jnp.bfloat16)
    hidden_grad = contract_cols(scaled, down_rows)
    grad_gate = (hidden_grad * up_pre * sig_gate * (1.0 + gate_pre * (1.0 - sig_gate))).astype(
        jnp.bfloat16
    )
    grad_up = (hidden_grad * act_gate).astype(jnp.bfloat16)
    back_rows = (contract_cols(grad_gate, gate_cols) + contract_cols(grad_up, up_cols)).astype(
        jnp.bfloat16
    )
    both_grads = jnp.concatenate([grad_gate, grad_up], axis=1)
    terms = jnp.concatenate(
        [contract_rows(flat_x, both_grads), contract_rows(scaled, hidden)], axis=1
    )
    summed = lax.psum_scatter(
        terms.astype(jnp.bfloat16), "seq", scatter_dimension=0, tiled=True
    ).astype(jnp.float32)
    weight_grads = summed.astype(jnp.bfloat16).reshape(1, summed.shape[0], 3, slice_width)
    ret_x, ret_c = (
        lax.all_to_all(
            back_rows.reshape(n_expert, CAP, D), "expert", split_axis=0, concat_axis=0, tiled=True
        ),
        lax.all_to_all(
            comb_part.reshape(n_expert, CAP).astype(jnp.bfloat16),
            "expert",
            split_axis=0,
            concat_axis=0,
            tiled=True,
        ).astype(jnp.float32),
    )
    spread = jnp.repeat(picker_bf, HSPLIT, axis=0).reshape(n_expert * CAP, tok_dev)
    grad_tokens = contract_rows(spread, ret_x.reshape(-1, D)).astype(jnp.bfloat16)
    comb_slots = jnp.sum(ret_c.reshape(experts, HSPLIT, CAP), axis=1)
    comb_te = jnp.sum(jnp.where(picker, comb_slots[:, :, None], 0.0), axis=1)
    grad_combine = jnp.sum(jnp.where(chosen, comb_te.T[:, None, :], 0.0), axis=2)
    return (grad_tokens, grad_combine, weight_grads)


def fused(n_e, n_s, tok_hbm, og_hbm, ids_hbm, comb_hbm, wg_hbm, wu_hbm, wd_hbm,
          gt_ref, gc_ref, wgr_ref,
          tok_ref, og_ref, ids_ref, comb_ref, wgu, wd, outx, outs, xs, ss, xa, sa, ga, back, mid, tot, ret,
          w_sem, out_send, near_send, half_send, recv, half_recv,
          q_send, q_recv, g_send, g_recv,
          b_send, b_recv, m_send, m_recv, t_send, t_recv):
    me = lax.axis_index("expert")
    sq = lax.axis_index("seq")
    groups = n_e // HSPLIT
    grp = me // HSPLIT
    part = lax.rem(me, HSPLIT)
    near = (part + 1 - 2 * lax.rem(part, 2), lax.rem(part + 2, HSPLIT))
    rows = n_e * ROWS
    used = groups * ROWS
    width = wd.shape[0]
    toks, feats = tok_ref.shape
    top = ids_ref.shape[0]
    share = feats // n_s
    piece = feats * EXTRA // ROWS
    packed = CHUNKS * piece
    chunk = [slice(m * piece, (m + 1) * piece) for m in range(CHUNKS)]
    last = slice(packed, feats)
    halves = (slice(0, packed // 2), slice(packed // 2, packed))

    wg = wgu.at[0:width, :]
    wu = wgu.at[width : 2 * width, :]
    loads = [
        pltpu.make_async_copy(src, dst, w_sem.at[i])
        for i, (src, dst) in enumerate((
            (ids_hbm, ids_ref), (comb_hbm, comb_ref), (tok_hbm, tok_ref), (og_hbm, og_ref),
            (wg_hbm.at[0], wg), (wu_hbm.at[0], wu), (wd_hbm.at[0], wd)))
    ]
    for load in loads:
        load.start()

    def holder(g, p):
        return lax.rem(grp + g, groups) * HSPLIT + lax.rem(part + p, HSPLIT)

    met = [(holder(g, 0), sq) for g in range(1, groups)]
    met += [(holder(0, p), sq) for p in range(1, HSPLIT)]
    met += [(me, lax.rem(sq + step, n_s)) for step in range(1, n_s)]
    barrier = pltpu.get_barrier_semaphore()
    for device in met:
        pl.semaphore_signal(barrier, inc=1, device_id=device, device_id_type=MESH)

    def iota(shape, dim):
        return lax.broadcasted_iota(jnp.int32, shape, dim)

    def one_hot(mask):
        return mask.astype(F32).astype(BF16)

    def mm(left, right):
        return jnp.dot(left, right, preferred_element_type=F32)

    loads[0].wait()
    loads[1].wait()
    ids = ids_ref[...]
    comb = comb_ref[...]
    e_row = iota((used, toks), 0) // ROWS
    c_row = lax.rem(iota((used, toks), 0), ROWS)
    routed = jnp.zeros((used, toks), F32)
    weight = jnp.zeros((used, toks), F32)
    for k in range(top):
        hit = ids[k : k + 1, :] == e_row
        routed = jnp.where(hit, 1.0, routed)
        weight = jnp.where(hit, comb[k : k + 1, :], weight)
    earlier = mm(routed.astype(BF16), one_hot(iota((toks, toks), 0) < iota((toks, toks), 1)))

    def picked(slot, mask):
        return jnp.where(mask & (earlier == slot.astype(F32)), routed, 0.0)

    base = picked(c_row, c_row < CAP)
    tails = [picked(c_row - CAP + EXTRA * m, c_row >= CAP) for m in range(CHUNKS)]
    base_bf = base.astype(BF16)
    tails_bf = [tail.astype(BF16) for tail in tails]

    def gathered(ref, m):
        return mm(base_bf, ref[:, chunk[m]]) + mm(tails_bf[m], ref[:, last])

    def at(i):
        return pl.ds(pl.multiple_of(i * ROWS, ROWS), ROWS)

    sends = []

    def send(src, dst, send_sem, recv_sem, device):
        copy = pltpu.make_async_remote_copy(
            src_ref=src, dst_ref=dst, send_sem=send_sem, recv_sem=recv_sem,
            device_id=device, device_id_type=MESH)
        copy.start()
        sends.append(copy)

    def arrived(ref, sem):
        pltpu.make_async_copy(ref, ref, sem).wait()

    full = slice(0, packed)
    landing = (xs, ss)

    def place(index, p):
        return at(index * HSPLIT + p)

    def pass_on(a, src, index):
        for n in range(2):
            send(src, landing[a].at[place(index, part), full], near_send.at[a, index, n],
                 recv.at[a, index, part], (grp * HSPLIT + near[n], sq))

    def first(a, out):
        for step in range(1, groups):
            to = lax.rem(grp + step, groups)
            send(out.at[at(to), :], landing[a].at[place(groups - step, part), full],
                 out_send.at[a, step - 1], recv.at[a, groups - step, part],
                 (to * HSPLIT + part, sq))

    def relay(a, index):
        for n in range(2):
            arrived(landing[a].at[place(index, near[n]), full], recv.at[a, index, near[n]])
            half = landing[a].at[place(index, near[n]), halves[n]]
            send(half, half, half_send.at[a, index, n], half_recv.at[a, index, n],
                 (grp * HSPLIT + near[1 - n], sq))

    def enter(a, index):
        block = landing[a].at[place(index, part), full]
        arrived(block, recv.at[a, index, part])
        pass_on(a, block, index)

    def far(a, index):
        source = lax.rem(near[0] + 2, HSPLIT)
        for n in range(2):
            arrived(landing[a].at[place(index, source), halves[n]], half_recv.at[a, index, n])

    loads[2].wait()
    for m in range(CHUNKS):
        outx[:, chunk[m]] = gathered(tok_ref, m).astype(BF16)
    pl.semaphore_wait(barrier, len(met))
    first(0, outx)
    pass_on(0, outx.at[at(grp), :], 0)
    loads[3].wait()
    for m in range(CHUNKS):
        row_w = jnp.sum((base + tails[m]) * weight, axis=1, keepdims=True)
        outs[:, chunk[m]] = (row_w * gathered(og_ref, m)).astype(BF16)
    first(1, outs)
    xs[place(0, part), full] = outx[at(grp), :]
    ss[place(0, part), full] = outs[at(grp), :]

    def slots(count):
        at_r = iota((count, count), 0)
        at_c = iota((count, count), 1)
        return at_r // ROWS == at_c // ROWS, lax.rem(at_r, ROWS), lax.rem(at_c, ROWS)

    quad = HSPLIT * ROWS
    together, r_slot, c_slot = slots(quad)
    unfold = [
        one_hot(together & (c_slot >= CAP) & (c_slot - CAP + EXTRA * m == r_slot))
        for m in range(CHUNKS)
    ]
    fold = [
        one_hot(together & (r_slot >= CAP) & (r_slot - CAP + EXTRA * m == c_slot))
        for m in range(CHUNKS)
    ]
    valid = lax.rem(iota((width, quad), 1), ROWS) < CAP
    shares = (xa, sa)

    def group_rows(index):
        return slice(index * quad, (index + 1) * quad)

    def complete(a, index):
        far(a, index)
        ref = landing[a]
        here = group_rows(index)
        total = mm(unfold[0], ref[here, chunk[0]])
        for m in range(1, CHUNKS):
            total = total + mm(unfold[m], ref[here, chunk[m]])
        ref[here, last] = total.astype(BF16)
        for step in range(1, n_s):
            peer = lax.rem(sq + step, n_s)
            mine = pl.ds(pl.multiple_of(peer * share, LANES), share)
            send(ref.at[here, mine], shares[a].at[sq, here, :], q_send.at[a, index, step - 1],
                 q_recv.at[a, sq, index], (me, peer))

    across = (((1,), (1,)), ((), ()))

    beyond = range(1, groups)
    for index in beyond:
        enter(0, index)
    relay(0, 0)
    for index in beyond:
        enter(1, index)
    pass_on(1, outs.at[at(grp), :], 0)
    for index in beyond:
        relay(0, index)
    complete(0, 0)
    for index in beyond:
        relay(1, index)
    for index in beyond:
        complete(0, index)
    loads[4].wait()
    loads[5].wait()
    gate_up = lax.dot_general(wgu[...], xs[...], across, preferred_element_type=F32)
    gate_all = gate_up[0:width]
    up_all = gate_up[width : 2 * width]
    sig_all = 1.0 / (1.0 + jnp.exp(-gate_all))
    act_all = gate_all * sig_all
    hidden_all = act_all * up_all
    d_gate_all = up_all * sig_all * (1.0 + gate_all * (1.0 - sig_all))
    relay(1, 0)
    loads[6].wait()
    keep = lax.rem(iota((quad, piece), 0), ROWS) < CAP
    terms = [None] * groups

    def backward(index):
        here = group_rows(index)
        complete(1, index)
        hgrad = jnp.where(
            valid, lax.dot_general(wd[...], ss[here, :], across, preferred_element_type=F32), 0.0)
        hidden = jnp.where(valid, hidden_all[:, here], 0.0).astype(BF16)
        g_gate_t = (hgrad * d_gate_all[:, here]).astype(BF16)
        g_up_t = (hgrad * act_all[:, here]).astype(BF16)
        terms[index] = (g_gate_t, g_up_t, hidden)
        row_part = jnp.sum(hidden.astype(F32) * hgrad, axis=0, keepdims=True)
        back[here, packed : packed + LANES] = jnp.broadcast_to(
            row_part, (LANES, quad)).T.astype(BF16)
        g_gate = g_gate_t.T
        g_up = g_up_t.T
        tail_grad = (mm(g_gate, wg[:, last]) + mm(g_up, wu[:, last])).astype(BF16)
        for m in range(CHUNKS):
            whole = mm(g_gate, wg[:, chunk[m]]) + mm(g_up, wu[:, chunk[m]])
            back[here, chunk[m]] = jnp.where(keep, whole, mm(fold[m], tail_grad)).astype(BF16)

    for index in beyond:
        backward(index)
        for p in range(1, HSPLIT):
            to = lax.rem(part + p, HSPLIT)
            send(back.at[place(index, to), :], mid.at[index - 1, part],
                 m_send.at[index - 1, p - 1], m_recv.at[index - 1, part], (holder(0, p), sq))
    backward(0)

    def lanes_of(s):
        return pl.ds(pl.multiple_of(s * rows, LANES), rows)

    for i in range(3):
        ga[i * width : (i + 1) * width, lanes_of(sq)] = jnp.concatenate(
            [terms[index][i] for index in range(groups)], axis=1)
    pairs = n_s // 2
    core = lax.rem(sq, 2)
    mate = sq + 1 - 2 * core
    peers = [lax.rem(sq // 2 + step, pairs) * 2 + core for step in range(1, pairs)]

    def to_seq(source, count, peer):
        block = ga.at[:, lanes_of(source)]
        send(block, block, g_send.at[count], g_recv.at[source], (me, peer))

    for count, peer in enumerate(peers):
        to_seq(sq, count, peer)
    to_seq(sq, pairs - 1, mate)

    for p in range(1, HSPLIT):
        send(back.at[place(0, lax.rem(part + p, HSPLIT)), :], ret.at[at(part), :],
             b_send.at[p - 1], b_recv.at[part], (holder(0, p), sq))
    ret[at(part), :] = back[place(0, part), :]
    for index in beyond:
        total = back[place(index, part), :].astype(F32)
        for p in range(1, HSPLIT):
            other = lax.rem(part + p, HSPLIT)
            arrived(mid.at[index - 1, other], m_recv.at[index - 1, other])
            total = total + mid[index - 1, other].astype(F32)
        tot[index - 1] = total.astype(BF16)
        send(tot.at[index - 1], ret.at[at(HSPLIT + groups - index - 1), :],
             t_send.at[index - 1], t_recv.at[groups - index - 1], (holder(index, 0), sq))

    landed = (HSPLIT + groups - 1) * ROWS

    def expert_at(block):
        return lax.rem(grp + jnp.maximum(block - HSPLIT + 1, 0), groups)

    def same(shape, ret_dim):
        of_ret = iota(shape, ret_dim)
        of_slot = iota(shape, 1 - ret_dim)
        return one_hot((expert_at(of_ret // ROWS) == of_slot // ROWS)
                       & (lax.rem(of_ret, ROWS) == lax.rem(of_slot, ROWS)))

    widen = same((landed, used), 0)
    home = mm(widen, base_bf).T.astype(BF16)
    home_tails = [mm(widen, tail).T.astype(BF16) for tail in tails_bf]
    gather = same((used, landed), 1)

    xa[sq] = xs[:, pl.ds(pl.multiple_of(sq * share, LANES), share)]
    sa[sq] = ss[:, pl.ds(pl.multiple_of(sq * share, LANES), share)]
    for count, peer in enumerate(peers):
        arrived(ga.at[:, lanes_of(peer)], g_recv.at[peer])
        to_seq(peer, pairs + count, mate)
    for step in range(1, n_s):
        peer = lax.rem(sq + step, n_s)
        for a, ref in enumerate(shares):
            for index in range(groups):
                arrived(ref.at[peer, group_rows(index), :], q_recv.at[a, peer, index])
    arrived(ga.at[:, lanes_of(mate)], g_recv.at[mate])
    for peer in peers:
        twin = peer + 1 - 2 * core
        arrived(ga.at[:, lanes_of(twin)], g_recv.at[twin])
    every = n_s * rows
    wgr_ref[0 : 2 * width, :] = mm(
        ga[0 : 2 * width, :], xa[...].reshape(every, share)).astype(BF16)
    wgr_ref[2 * width : 3 * width, :] = mm(
        ga[2 * width : 3 * width, :], sa[...].reshape(every, share)).astype(BF16)

    for p in range(1, HSPLIT):
        other = lax.rem(part + p, HSPLIT)
        arrived(ret.at[at(other), :], b_recv.at[other])
    for index in beyond:
        arrived(ret.at[at(HSPLIT + index - 1), :], t_recv.at[index - 1])
    tail_sum = jnp.zeros((toks, piece), F32)
    for m in range(CHUNKS):
        gt_ref[:, chunk[m]] = mm(home, ret[:, chunk[m]]).astype(BF16)
        tail_sum = tail_sum + mm(home_tails[m], ret[:, chunk[m]])
    gt_ref[:, last] = tail_sum.astype(BF16)
    per_slot = base * mm(gather, ret[:, packed : packed + LANES])
    at_k = iota((top, toks), 0)
    total = jnp.zeros((top, toks), F32)
    for k in range(top):
        mine = jnp.sum(jnp.where(ids[k : k + 1, :] == e_row, per_slot, 0.0), axis=0, keepdims=True)
        total = jnp.where(at_k == k, mine, total)
    gc_ref[...] = total / comb
    for copy in sends:
        copy.wait_send()


def deliver(*refs):
    count = len(refs) // 2
    sems = refs[-1]
    copies = [
        pltpu.make_async_copy(refs[i], refs[count + i], sems.at[i]) for i in range(count)
    ]
    for copy in copies:
        copy.start()
    for copy in copies:
        copy.wait()


def local_fused(n_e, n_s, tokens, out_grad, expert_ids, combine, w_gate, w_up, w_down):
    toks, feats = tokens.shape
    width = w_gate.shape[2]
    share = feats // n_s
    groups = n_e // HSPLIT
    rows = n_e * ROWS
    packed = feats * CAP // ROWS
    crossing = max(1, groups - 1)
    dma = pltpu.SemaphoreType.DMA
    vmem = pl.BlockSpec(memory_space=pltpu.VMEM)
    hbm = pl.BlockSpec(memory_space=pl.ANY)
    grad_tokens, grad_combine, flat = pl.pallas_call(
        functools.partial(fused, n_e, n_s),
        out_shape=(
            pltpu.VMEM((toks, feats), BF16),
            pltpu.VMEM(combine.shape[::-1], F32),
            pltpu.VMEM((3 * width, share), BF16),
        ),
        in_specs=[hbm] * 7,
        out_specs=(vmem,) * 3,
        scratch_shapes=[
            pltpu.VMEM((toks, feats), BF16),
            pltpu.VMEM((toks, feats), BF16),
            pltpu.VMEM(expert_ids.shape[::-1], jnp.int32),
            pltpu.VMEM(combine.shape[::-1], F32),
            pltpu.VMEM((2 * width, feats), BF16),
            pltpu.VMEM((width, feats), BF16),
            pltpu.VMEM((groups * ROWS, packed), BF16),
            pltpu.VMEM((groups * ROWS, packed), BF16),
            pltpu.VMEM((rows, feats), BF16),
            pltpu.VMEM((rows, feats), BF16),
            pltpu.VMEM((n_s, rows, share), BF16),
            pltpu.VMEM((n_s, rows, share), BF16),
            pltpu.VMEM((3 * width, n_s * rows), BF16),
            pltpu.VMEM((rows, packed + LANES), BF16),
            pltpu.VMEM((crossing, HSPLIT, ROWS, packed + LANES), BF16),
            pltpu.VMEM((crossing, ROWS, packed + LANES), BF16),
            pltpu.VMEM(((HSPLIT + groups - 1) * ROWS, packed + LANES), BF16),
            dma((7,)),
            dma((2, crossing)),
            dma((2, groups, 2)),
            dma((2, groups, 2)),
            dma((2, groups, HSPLIT)),
            dma((2, groups, 2)),
            dma((2, groups, n_s - 1)),
            dma((2, n_s, groups)),
            dma((n_s - 1,)),
            dma((n_s,)),
            dma((HSPLIT - 1,)),
            dma((HSPLIT,)),
            dma((crossing, HSPLIT - 1)),
            dma((crossing, HSPLIT)),
            dma((crossing,)),
            dma((crossing,)),
        ],
        compiler_params=pltpu.CompilerParams(
            collective_id=0, has_side_effects=True, vmem_limit_bytes=VMEM_BYTES),
        cost_estimate=pl.CostEstimate(
            flops=18 * rows * feats * width, bytes_accessed=8 * feats * width,
            transcendentals=rows * width),
    )(
        tokens, out_grad, expert_ids.T, combine.T,
        w_gate.transpose(0, 2, 1), w_up.transpose(0, 2, 1), w_down,
    )
    made = (grad_tokens, grad_combine, flat)
    grad_tokens, grad_combine, flat = pl.pallas_call(
        deliver,
        out_shape=tuple(jax.ShapeDtypeStruct(x.shape, x.dtype) for x in made),
        in_specs=[hbm] * 3,
        out_specs=(hbm,) * 3,
        scratch_shapes=[dma((3,))],
    )(*made)
    weight_grads = flat.reshape(1, 3, width, share).transpose(0, 3, 1, 2)
    return grad_tokens, grad_combine.T, weight_grads


def solution(mesh):
    in_specs = (
        P(("expert", "seq"), None),
        P(("expert", "seq"), None),
        P(("expert", "seq"), None),
        P(("expert", "seq"), None),
        P("expert", None, None),
        P("expert", None, None),
        P("expert", None, None),
    )
    out_specs = (
        P(("expert", "seq"), None),
        P(("expert", "seq"), None),
        P("expert", "seq", None, None),
    )
    n_e, n_s = mesh.shape["expert"], mesh.shape["seq"]
    fits = n_s % 2 == 0 and D % (n_s * LANES) == 0
    body = functools.partial(local_fused, n_e, n_s) if fits else local
    return jax.shard_map(body, mesh=mesh, in_specs=in_specs, out_specs=out_specs, check_vma=False)
```

```python
import functools

import jax
import jax.numpy as jnp
from jax import lax
from jax.experimental import pallas as pl
from jax.experimental.pallas import tpu as pltpu
from jax.sharding import PartitionSpec as P

D = 2048
HSPLIT = 4
CAP = 12
ROWS = 16
EXTRA = ROWS - CAP
CHUNKS = CAP // EXTRA
LANES = 128
VMEM_BYTES = 61500 * 1024
MESH = pl.DeviceIdType.MESH
F32 = jnp.float32
BF16 = jnp.bfloat16


def contract_rows(left, right):
    return lax.dot_general(
        left, right, (((0,), (0,)), ((), ())), preferred_element_type=jnp.float32
    )


def contract_cols(left, right):
    return lax.dot_general(
        left, right, (((1,), (1,)), ((), ())), preferred_element_type=jnp.float32
    )


def local(tokens, out_grad, expert_ids, combine, w_gate, w_up, w_down):
    n_expert = lax.axis_size("expert")
    experts = n_expert // HSPLIT
    tok_dev = tokens.shape[0]
    slice_width = w_gate.shape[2]
    wanted = lax.broadcasted_iota(jnp.int32, (1, 1, experts), 2)
    chosen = expert_ids[:, :, None] == wanted
    routed = jnp.any(chosen, axis=1).astype(jnp.int32)
    earlier = jnp.cumsum(routed, axis=0, dtype=jnp.int32) - routed
    slot_ids = lax.broadcasted_iota(jnp.int32, (1, CAP, 1), 1)
    picker = (earlier.T[:, None, :] == slot_ids) & (routed.T[:, None, :] == 1)
    picker_bf = picker.astype(jnp.bfloat16)
    weight_te = jnp.sum(jnp.where(chosen, combine[:, :, None], 0.0), axis=1)
    send_x = jnp.einsum(
        "ect,td->ecd", picker_bf, tokens, preferred_element_type=jnp.float32
    ).astype(jnp.bfloat16)
    send_g = jnp.einsum(
        "ect,td->ecd", picker_bf, out_grad, preferred_element_type=jnp.float32
    ).astype(jnp.bfloat16)
    send_w = jnp.sum(jnp.where(picker, weight_te.T[:, None, :], 0.0), axis=2)
    out_x = jnp.repeat(send_x, HSPLIT, axis=0)
    out_g = jnp.repeat(send_g, HSPLIT, axis=0)
    out_w = jnp.repeat(send_w, HSPLIT, axis=0)
    rows_x = lax.all_to_all(out_x, "expert", split_axis=0, concat_axis=0, tiled=True)
    rows_g, rows_w = (
        lax.all_to_all(out_g, "expert", split_axis=0, concat_axis=0, tiled=True),
        lax.all_to_all(
            out_w.astype(jnp.bfloat16), "expert", split_axis=0, concat_axis=0, tiled=True
        ).astype(out_w.dtype),
    )
    flat_x = rows_x.reshape(-1, D)
    flat_g = rows_g.reshape(-1, D)
    flat_w = rows_w.reshape(-1)
    gate_cols = w_gate[0]
    up_cols = w_up[0]
    down_rows = w_down[0]
    gate_pre = jnp.dot(flat_x, gate_cols, preferred_element_type=jnp.float32)
    up_pre = jnp.dot(flat_x, up_cols, preferred_element_type=jnp.float32)
    sig_gate = jax.nn.sigmoid(gate_pre)
    act_gate = gate_pre * sig_gate
    hidden = (act_gate * up_pre).astype(jnp.bfloat16)
    expert_out = jnp.dot(hidden, down_rows, preferred_element_type=jnp.float32)
    comb_part = jnp.sum(flat_g.astype(jnp.float32) * expert_out, axis=1)
    scaled = (flat_w[:, None] * flat_g.astype(jnp.float32)).astype(jnp.bfloat16)
    hidden_grad = contract_cols(scaled, down_rows)
    grad_gate = (hidden_grad * up_pre * sig_gate * (1.0 + gate_pre * (1.0 - sig_gate))).astype(
        jnp.bfloat16
    )
    grad_up = (hidden_grad * act_gate).astype(jnp.bfloat16)
    back_rows = (contract_cols(grad_gate, gate_cols) + contract_cols(grad_up, up_cols)).astype(
        jnp.bfloat16
    )
    both_grads = jnp.concatenate([grad_gate, grad_up], axis=1)
    terms = jnp.concatenate(
        [contract_rows(flat_x, both_grads), contract_rows(scaled, hidden)], axis=1
    )
    summed = lax.psum_scatter(
        terms.astype(jnp.bfloat16), "seq", scatter_dimension=0, tiled=True
    ).astype(jnp.float32)
    weight_grads = summed.astype(jnp.bfloat16).reshape(1, summed.shape[0], 3, slice_width)
    ret_x, ret_c = (
        lax.all_to_all(
            back_rows.reshape(n_expert, CAP, D), "expert", split_axis=0, concat_axis=0, tiled=True
        ),
        lax.all_to_all(
            comb_part.reshape(n_expert, CAP).astype(jnp.bfloat16),
            "expert",
            split_axis=0,
            concat_axis=0,
            tiled=True,
        ).astype(jnp.float32),
    )
    spread = jnp.repeat(picker_bf, HSPLIT, axis=0).reshape(n_expert * CAP, tok_dev)
    grad_tokens = contract_rows(spread, ret_x.reshape(-1, D)).astype(jnp.bfloat16)
    comb_slots = jnp.sum(ret_c.reshape(experts, HSPLIT, CAP), axis=1)
    comb_te = jnp.sum(jnp.where(picker, comb_slots[:, :, None], 0.0), axis=1)
    grad_combine = jnp.sum(jnp.where(chosen, comb_te.T[:, None, :], 0.0), axis=2)
    return (grad_tokens, grad_combine, weight_grads)


def fused(n_e, n_s, tok_hbm, og_hbm, ids_hbm, comb_hbm, wg_hbm, wu_hbm, wd_hbm,
          gt_ref, gc_ref, wgr_ref,
          tok_ref, og_ref, ids_ref, comb_ref, wgu, wd, outx, outs, xs, ss, xa, sa, ga, back, mid, tot, ret,
          w_sem, out_send, near_send, half_send, recv, half_recv,
          q_send, q_recv, g_send, g_recv,
          b_send, b_recv, m_send, m_recv, t_send, t_recv):
    me = lax.axis_index("expert")
    sq = lax.axis_index("seq")
    groups = n_e // HSPLIT
    grp = me // HSPLIT
    part = lax.rem(me, HSPLIT)
    near = (part + 1 - 2 * lax.rem(part, 2), lax.rem(part + 2, HSPLIT))
    rows = n_e * ROWS
    used = groups * ROWS
    width = wd.shape[0]
    toks, feats = tok_ref.shape
    top = ids_ref.shape[0]
    share = feats // n_s
    piece = feats * EXTRA // ROWS
    packed = CHUNKS * piece
    chunk = [slice(m * piece, (m + 1) * piece) for m in range(CHUNKS)]
    last = slice(packed, feats)
    halves = (slice(0, packed // 2), slice(packed // 2, packed))

    wg = wgu.at[0:width, :]
    wu = wgu.at[width : 2 * width, :]
    loads = [
        pltpu.make_async_copy(src, dst, w_sem.at[i])
        for i, (src, dst) in enumerate((
            (ids_hbm, ids_ref), (comb_hbm, comb_ref), (tok_hbm, tok_ref), (og_hbm, og_ref),
            (wg_hbm.at[0], wg), (wu_hbm.at[0], wu), (wd_hbm.at[0], wd)))
    ]
    for load in loads:
        load.start()

    def holder(g, p):
        return lax.rem(grp + g, groups) * HSPLIT + lax.rem(part + p, HSPLIT)

    met = [(holder(g, 0), sq) for g in range(1, groups)]
    met += [(holder(0, p), sq) for p in range(1, HSPLIT)]
    met += [(me, lax.rem(sq + step, n_s)) for step in range(1, n_s)]
    barrier = pltpu.get_barrier_semaphore()
    for device in met:
        pl.semaphore_signal(barrier, inc=1, device_id=device, device_id_type=MESH)

    def iota(shape, dim):
        return lax.broadcasted_iota(jnp.int32, shape, dim)

    def one_hot(mask):
        return mask.astype(F32).astype(BF16)

    def mm(left, right):
        return jnp.dot(left, right, preferred_element_type=F32)

    loads[0].wait()
    loads[1].wait()
    ids = ids_ref[...]
    comb = comb_ref[...]
    e_row = iota((used, toks), 0) // ROWS
    c_row = lax.rem(iota((used, toks), 0), ROWS)
    routed = jnp.zeros((used, toks), F32)
    weight = jnp.zeros((used, toks), F32)
    for k in range(top):
        hit = ids[k : k + 1, :] == e_row
        routed = jnp.where(hit, 1.0, routed)
        weight = jnp.where(hit, comb[k : k + 1, :], weight)
    earlier = mm(routed.astype(BF16), one_hot(iota((toks, toks), 0) < iota((toks, toks), 1)))

    def picked(slot, mask):
        return jnp.where(mask & (earlier == slot.astype(F32)), routed, 0.0)

    base = picked(c_row, c_row < CAP)
    tails = [picked(c_row - CAP + EXTRA * m, c_row >= CAP) for m in range(CHUNKS)]
    base_bf = base.astype(BF16)
    tails_bf = [tail.astype(BF16) for tail in tails]

    def gathered(ref, m):
        return mm(base_bf, ref[:, chunk[m]]) + mm(tails_bf[m], ref[:, last])

    def at(i):
        return pl.ds(pl.multiple_of(i * ROWS, ROWS), ROWS)

    sends = []

    def send(src, dst, send_sem, recv_sem, device):
        copy = pltpu.make_async_remote_copy(
            src_ref=src, dst_ref=dst, send_sem=send_sem, recv_sem=recv_sem,
            device_id=device, device_id_type=MESH)
        copy.start()
        sends.append(copy)

    def arrived(ref, sem):
        pltpu.make_async_copy(ref, ref, sem).wait()

    full = slice(0, packed)
    landing = (xs, ss)

    def place(index, p):
        return at(index * HSPLIT + p)

    def pass_on(a, src, index):
        for n in range(2):
            send(src, landing[a].at[place(index, part), full], near_send.at[a, index, n],
                 recv.at[a, index, part], (grp * HSPLIT + near[n], sq))

    def first(a, out):
        for step in range(1, groups):
            to = lax.rem(grp + step, groups)
            send(out.at[at(to), :], landing[a].at[place(groups - step, part), full],
                 out_send.at[a, step - 1], recv.at[a, groups - step, part],
                 (to * HSPLIT + part, sq))

    def relay(a, index):
        for n in range(2):
            arrived(landing[a].at[place(index, near[n]), full], recv.at[a, index, near[n]])
            half = landing[a].at[place(index, near[n]), halves[n]]
            send(half, half, half_send.at[a, index, n], half_recv.at[a, index, n],
                 (grp * HSPLIT + near[1 - n], sq))

    def enter(a, index):
        block = landing[a].at[place(index, part), full]
        arrived(block, recv.at[a, index, part])
        pass_on(a, block, index)

    def far(a, index):
        source = lax.rem(near[0] + 2, HSPLIT)
        for n in range(2):
            arrived(landing[a].at[place(index, source), halves[n]], half_recv.at[a, index, n])

    loads[2].wait()
    for m in range(CHUNKS):
        outx[:, chunk[m]] = gathered(tok_ref, m).astype(BF16)
    pl.semaphore_wait(barrier, len(met))
    first(0, outx)
    pass_on(0, outx.at[at(grp), :], 0)
    loads[3].wait()
    for m in range(CHUNKS):
        row_w = jnp.sum((base + tails[m]) * weight, axis=1, keepdims=True)
        outs[:, chunk[m]] = (row_w * gathered(og_ref, m)).astype(BF16)
    first(1, outs)
    xs[place(0, part), full] = outx[at(grp), :]
    ss[place(0, part), full] = outs[at(grp), :]

    def slots(count):
        at_r = iota((count, count), 0)
        at_c = iota((count, count), 1)
        return at_r // ROWS == at_c // ROWS, lax.rem(at_r, ROWS), lax.rem(at_c, ROWS)

    quad = HSPLIT * ROWS
    together, r_slot, c_slot = slots(quad)
    unfold = [
        one_hot(together & (c_slot >= CAP) & (c_slot - CAP + EXTRA * m == r_slot))
        for m in range(CHUNKS)
    ]
    fold = [
        one_hot(together & (r_slot >= CAP) & (r_slot - CAP + EXTRA * m == c_slot))
        for m in range(CHUNKS)
    ]
    valid = lax.rem(iota((width, quad), 1), ROWS) < CAP
    shares = (xa, sa)

    def group_rows(index):
        return slice(index * quad, (index + 1) * quad)

    def complete(a, index):
        far(a, index)
        ref = landing[a]
        here = group_rows(index)
        total = mm(unfold[0], ref[here, chunk[0]])
        for m in range(1, CHUNKS):
            total = total + mm(unfold[m], ref[here, chunk[m]])
        ref[here, last] = total.astype(BF16)
        for step in range(1, n_s):
            peer = lax.rem(sq + step, n_s)
            mine = pl.ds(pl.multiple_of(peer * share, LANES), share)
            send(ref.at[here, mine], shares[a].at[sq, here, :], q_send.at[a, index, step - 1],
                 q_recv.at[a, sq, index], (me, peer))

    across = (((1,), (1,)), ((), ()))

    beyond = range(1, groups)
    for index in beyond:
        enter(0, index)
    relay(0, 0)
    for index in beyond:
        enter(1, index)
    pass_on(1, outs.at[at(grp), :], 0)
    for index in beyond:
        relay(0, index)
    complete(0, 0)
    for index in beyond:
        relay(1, index)
    for index in beyond:
        complete(0, index)
    loads[4].wait()
    loads[5].wait()
    gate_up = lax.dot_general(wgu[...], xs[...], across, preferred_element_type=F32)
    gate_all = gate_up[0:width]
    up_all = gate_up[width : 2 * width]
    sig_all = 1.0 / (1.0 + jnp.exp(-gate_all))
    act_all = gate_all * sig_all
    hidden_all = act_all * up_all
    d_gate_all = up_all * sig_all * (1.0 + gate_all * (1.0 - sig_all))
    relay(1, 0)
    loads[6].wait()
    keep = lax.rem(iota((quad, piece), 0), ROWS) < CAP
    terms = [None] * groups

    def backward(index):
        here = group_rows(index)
        complete(1, index)
        hgrad = jnp.where(
            valid, lax.dot_general(wd[...], ss[here, :], across, preferred_element_type=F32), 0.0)
        hidden = jnp.where(valid, hidden_all[:, here], 0.0).astype(BF16)
        g_gate_t = (hgrad * d_gate_all[:, here]).astype(BF16)
        g_up_t = (hgrad * act_all[:, here]).astype(BF16)
        terms[index] = (g_gate_t, g_up_t, hidden)
        row_part = jnp.sum(hidden.astype(F32) * hgrad, axis=0, keepdims=True)
        back[here, packed : packed + LANES] = jnp.broadcast_to(
            row_part, (LANES, quad)).T.astype(BF16)
        g_gate = g_gate_t.T
        g_up = g_up_t.T
        tail_grad = (mm(g_gate, wg[:, last]) + mm(g_up, wu[:, last])).astype(BF16)
        for m in range(CHUNKS):
            whole = mm(g_gate, wg[:, chunk[m]]) + mm(g_up, wu[:, chunk[m]])
            back[here, chunk[m]] = jnp.where(keep, whole, mm(fold[m], tail_grad)).astype(BF16)

    for index in beyond:
        backward(index)
        for p in range(1, HSPLIT):
            to = lax.rem(part + p, HSPLIT)
            send(back.at[place(index, to), :], mid.at[index - 1, part],
                 m_send.at[index - 1, p - 1], m_recv.at[index - 1, part], (holder(0, p), sq))
    backward(0)

    def lanes_of(s):
        return pl.ds(pl.multiple_of(s * rows, LANES), rows)

    for i in range(3):
        ga[i * width : (i + 1) * width, lanes_of(sq)] = jnp.concatenate(
            [terms[index][i] for index in range(groups)], axis=1)
    pairs = n_s // 2
    core = lax.rem(sq, 2)
    mate = sq + 1 - 2 * core
    peers = [lax.rem(sq // 2 + step, pairs) * 2 + core for step in range(1, pairs)]

    def to_seq(source, count, peer):
        block = ga.at[:, lanes_of(source)]
        send(block, block, g_send.at[count], g_recv.at[source], (me, peer))

    for count, peer in enumerate(peers):
        to_seq(sq, count, peer)
    to_seq(sq, pairs - 1, mate)

    for p in range(1, HSPLIT):
        send(back.at[place(0, lax.rem(part + p, HSPLIT)), :], ret.at[at(part), :],
             b_send.at[p - 1], b_recv.at[part], (holder(0, p), sq))
    ret[at(part), :] = back[place(0, part), :]
    for index in beyond:
        total = back[place(index, part), :].astype(F32)
        for p in range(1, HSPLIT):
            other = lax.rem(part + p, HSPLIT)
            arrived(mid.at[index - 1, other], m_recv.at[index - 1, other])
            total = total + mid[index - 1, other].astype(F32)
        tot[index - 1] = total.astype(BF16)
        send(tot.at[index - 1], ret.at[at(HSPLIT + groups - index - 1), :],
             t_send.at[index - 1], t_recv.at[groups - index - 1], (holder(index, 0), sq))

    landed = (HSPLIT + groups - 1) * ROWS

    def expert_at(block):
        return lax.rem(grp + jnp.maximum(block - HSPLIT + 1, 0), groups)

    def same(shape, ret_dim):
        of_ret = iota(shape, ret_dim)
        of_slot = iota(shape, 1 - ret_dim)
        return one_hot((expert_at(of_ret // ROWS) == of_slot // ROWS)
                       & (lax.rem(of_ret, ROWS) == lax.rem(of_slot, ROWS)))

    widen = same((landed, used), 0)
    home = mm(widen, base_bf).T.astype(BF16)
    home_tails = [mm(widen, tail).T.astype(BF16) for tail in tails_bf]
    gather = same((used, landed), 1)

    xa[sq] = xs[:, pl.ds(pl.multiple_of(sq * share, LANES), share)]
    sa[sq] = ss[:, pl.ds(pl.multiple_of(sq * share, LANES), share)]
    for count, peer in enumerate(peers):
        arrived(ga.at[:, lanes_of(peer)], g_recv.at[peer])
        to_seq(peer, pairs + count, mate)
    for step in range(1, n_s):
        peer = lax.rem(sq + step, n_s)
        for a, ref in enumerate(shares):
            for index in range(groups):
                arrived(ref.at[peer, group_rows(index), :], q_recv.at[a, peer, index])
    arrived(ga.at[:, lanes_of(mate)], g_recv.at[mate])
    for peer in peers:
        twin = peer + 1 - 2 * core
        arrived(ga.at[:, lanes_of(twin)], g_recv.at[twin])
    every = n_s * rows
    wgr_ref[0 : 2 * width, :] = mm(
        ga[0 : 2 * width, :], xa[...].reshape(every, share)).astype(BF16)
    wgr_ref[2 * width : 3 * width, :] = mm(
        ga[2 * width : 3 * width, :], sa[...].reshape(every, share)).astype(BF16)

    for p in range(1, HSPLIT):
        other = lax.rem(part + p, HSPLIT)
        arrived(ret.at[at(other), :], b_recv.at[other])
    for index in beyond:
        arrived(ret.at[at(HSPLIT + index - 1), :], t_recv.at[index - 1])
    tail_sum = jnp.zeros((toks, piece), F32)
    for m in range(CHUNKS):
        gt_ref[:, chunk[m]] = mm(home, ret[:, chunk[m]]).astype(BF16)
        tail_sum = tail_sum + mm(home_tails[m], ret[:, chunk[m]])
    gt_ref[:, last] = tail_sum.astype(BF16)
    per_slot = base * mm(gather, ret[:, packed : packed + LANES])
    at_k = iota((top, toks), 0)
    total = jnp.zeros((top, toks), F32)
    for k in range(top):
        mine = jnp.sum(jnp.where(ids[k : k + 1, :] == e_row, per_slot, 0.0), axis=0, keepdims=True)
        total = jnp.where(at_k == k, mine, total)
    gc_ref[...] = total / comb
    for copy in sends:
        copy.wait_send()


def local_fused(n_e, n_s, tokens, out_grad, expert_ids, combine, w_gate, w_up, w_down):
    toks, feats = tokens.shape
    width = w_gate.shape[2]
    share = feats // n_s
    groups = n_e // HSPLIT
    rows = n_e * ROWS
    packed = feats * CAP // ROWS
    crossing = max(1, groups - 1)
    dma = pltpu.SemaphoreType.DMA
    vmem = pl.BlockSpec(memory_space=pltpu.VMEM)
    hbm = pl.BlockSpec(memory_space=pl.ANY)
    grad_tokens, grad_combine, flat = pl.pallas_call(
        functools.partial(fused, n_e, n_s),
        out_shape=(
            pltpu.VMEM((toks, feats), BF16),
            pltpu.VMEM(combine.shape[::-1], F32),
            pltpu.VMEM((3 * width, share), BF16),
        ),
        in_specs=[hbm] * 7,
        out_specs=(vmem,) * 3,
        scratch_shapes=[
            pltpu.VMEM((toks, feats), BF16),
            pltpu.VMEM((toks, feats), BF16),
            pltpu.VMEM(expert_ids.shape[::-1], jnp.int32),
            pltpu.VMEM(combine.shape[::-1], F32),
            pltpu.VMEM((2 * width, feats), BF16),
            pltpu.VMEM((width, feats), BF16),
            pltpu.VMEM((groups * ROWS, packed), BF16),
            pltpu.VMEM((groups * ROWS, packed), BF16),
            pltpu.VMEM((rows, feats), BF16),
            pltpu.VMEM((rows, feats), BF16),
            pltpu.VMEM((n_s, rows, share), BF16),
            pltpu.VMEM((n_s, rows, share), BF16),
            pltpu.VMEM((3 * width, n_s * rows), BF16),
            pltpu.VMEM((rows, packed + LANES), BF16),
            pltpu.VMEM((crossing, HSPLIT, ROWS, packed + LANES), BF16),
            pltpu.VMEM((crossing, ROWS, packed + LANES), BF16),
            pltpu.VMEM(((HSPLIT + groups - 1) * ROWS, packed + LANES), BF16),
            dma((7,)),
            dma((2, crossing)),
            dma((2, groups, 2)),
            dma((2, groups, 2)),
            dma((2, groups, HSPLIT)),
            dma((2, groups, 2)),
            dma((2, groups, n_s - 1)),
            dma((2, n_s, groups)),
            dma((n_s - 1,)),
            dma((n_s,)),
            dma((HSPLIT - 1,)),
            dma((HSPLIT,)),
            dma((crossing, HSPLIT - 1)),
            dma((crossing, HSPLIT)),
            dma((crossing,)),
            dma((crossing,)),
        ],
        compiler_params=pltpu.CompilerParams(
            collective_id=0, has_side_effects=True, vmem_limit_bytes=VMEM_BYTES),
        cost_estimate=pl.CostEstimate(
            flops=18 * rows * feats * width, bytes_accessed=8 * feats * width,
            transcendentals=rows * width),
    )(
        tokens, out_grad, expert_ids.T, combine.T,
        w_gate.transpose(0, 2, 1), w_up.transpose(0, 2, 1), w_down,
    )
    weight_grads = flat.reshape(1, 3, width, share).transpose(0, 3, 1, 2)
    return grad_tokens, grad_combine.T, weight_grads


def solution(mesh):
    in_specs = (
        P(("expert", "seq"), None),
        P(("expert", "seq"), None),
        P(("expert", "seq"), None),
        P(("expert", "seq"), None),
        P("expert", None, None),
        P("expert", None, None),
        P("expert", None, None),
    )
    out_specs = (
        P(("expert", "seq"), None),
        P(("expert", "seq"), None),
        P("expert", "seq", None, None),
    )
    n_e, n_s = mesh.shape["expert"], mesh.shape["seq"]
    fits = n_s % 2 == 0 and D % (n_s * LANES) == 0
    body = functools.partial(local_fused, n_e, n_s) if fits else local
    return jax.shard_map(body, mesh=mesh, in_specs=in_specs, out_specs=out_specs, check_vma=False)
```

```python
import functools

import jax
import jax.numpy as jnp
from jax import lax
from jax.experimental import pallas as pl
from jax.experimental.pallas import tpu as pltpu
from jax.sharding import PartitionSpec as P

D = 2048
HSPLIT = 4
CAP = 12
ROWS = 16
EXTRA = ROWS - CAP
CHUNKS = CAP // EXTRA
LANES = 128
VMEM_BYTES = 61500 * 1024
MESH = pl.DeviceIdType.MESH
F32 = jnp.float32
BF16 = jnp.bfloat16


def contract_rows(left, right):
    return lax.dot_general(
        left, right, (((0,), (0,)), ((), ())), preferred_element_type=jnp.float32
    )


def contract_cols(left, right):
    return lax.dot_general(
        left, right, (((1,), (1,)), ((), ())), preferred_element_type=jnp.float32
    )


def local(tokens, out_grad, expert_ids, combine, w_gate, w_up, w_down):
    n_expert = lax.axis_size("expert")
    experts = n_expert // HSPLIT
    tok_dev = tokens.shape[0]
    slice_width = w_gate.shape[2]
    wanted = lax.broadcasted_iota(jnp.int32, (1, 1, experts), 2)
    chosen = expert_ids[:, :, None] == wanted
    routed = jnp.any(chosen, axis=1).astype(jnp.int32)
    earlier = jnp.cumsum(routed, axis=0, dtype=jnp.int32) - routed
    slot_ids = lax.broadcasted_iota(jnp.int32, (1, CAP, 1), 1)
    picker = (earlier.T[:, None, :] == slot_ids) & (routed.T[:, None, :] == 1)
    picker_bf = picker.astype(jnp.bfloat16)
    weight_te = jnp.sum(jnp.where(chosen, combine[:, :, None], 0.0), axis=1)
    send_x = jnp.einsum(
        "ect,td->ecd", picker_bf, tokens, preferred_element_type=jnp.float32
    ).astype(jnp.bfloat16)
    send_g = jnp.einsum(
        "ect,td->ecd", picker_bf, out_grad, preferred_element_type=jnp.float32
    ).astype(jnp.bfloat16)
    send_w = jnp.sum(jnp.where(picker, weight_te.T[:, None, :], 0.0), axis=2)
    out_x = jnp.repeat(send_x, HSPLIT, axis=0)
    out_g = jnp.repeat(send_g, HSPLIT, axis=0)
    out_w = jnp.repeat(send_w, HSPLIT, axis=0)
    rows_x = lax.all_to_all(out_x, "expert", split_axis=0, concat_axis=0, tiled=True)
    rows_g, rows_w = (
        lax.all_to_all(out_g, "expert", split_axis=0, concat_axis=0, tiled=True),
        lax.all_to_all(
            out_w.astype(jnp.bfloat16), "expert", split_axis=0, concat_axis=0, tiled=True
        ).astype(out_w.dtype),
    )
    flat_x = rows_x.reshape(-1, D)
    flat_g = rows_g.reshape(-1, D)
    flat_w = rows_w.reshape(-1)
    gate_cols = w_gate[0]
    up_cols = w_up[0]
    down_rows = w_down[0]
    gate_pre = jnp.dot(flat_x, gate_cols, preferred_element_type=jnp.float32)
    up_pre = jnp.dot(flat_x, up_cols, preferred_element_type=jnp.float32)
    sig_gate = jax.nn.sigmoid(gate_pre)
    act_gate = gate_pre * sig_gate
    hidden = (act_gate * up_pre).astype(jnp.bfloat16)
    expert_out = jnp.dot(hidden, down_rows, preferred_element_type=jnp.float32)
    comb_part = jnp.sum(flat_g.astype(jnp.float32) * expert_out, axis=1)
    scaled = (flat_w[:, None] * flat_g.astype(jnp.float32)).astype(jnp.bfloat16)
    hidden_grad = contract_cols(scaled, down_rows)
    grad_gate = (hidden_grad * up_pre * sig_gate * (1.0 + gate_pre * (1.0 - sig_gate))).astype(
        jnp.bfloat16
    )
    grad_up = (hidden_grad * act_gate).astype(jnp.bfloat16)
    back_rows = (contract_cols(grad_gate, gate_cols) + contract_cols(grad_up, up_cols)).astype(
        jnp.bfloat16
    )
    both_grads = jnp.concatenate([grad_gate, grad_up], axis=1)
    terms = jnp.concatenate(
        [contract_rows(flat_x, both_grads), contract_rows(scaled, hidden)], axis=1
    )
    summed = lax.psum_scatter(
        terms.astype(jnp.bfloat16), "seq", scatter_dimension=0, tiled=True
    ).astype(jnp.float32)
    weight_grads = summed.astype(jnp.bfloat16).reshape(1, summed.shape[0], 3, slice_width)
    ret_x, ret_c = (
        lax.all_to_all(
            back_rows.reshape(n_expert, CAP, D), "expert", split_axis=0, concat_axis=0, tiled=True
        ),
        lax.all_to_all(
            comb_part.reshape(n_expert, CAP).astype(jnp.bfloat16),
            "expert",
            split_axis=0,
            concat_axis=0,
            tiled=True,
        ).astype(jnp.float32),
    )
    spread = jnp.repeat(picker_bf, HSPLIT, axis=0).reshape(n_expert * CAP, tok_dev)
    grad_tokens = contract_rows(spread, ret_x.reshape(-1, D)).astype(jnp.bfloat16)
    comb_slots = jnp.sum(ret_c.reshape(experts, HSPLIT, CAP), axis=1)
    comb_te = jnp.sum(jnp.where(picker, comb_slots[:, :, None], 0.0), axis=1)
    grad_combine = jnp.sum(jnp.where(chosen, comb_te.T[:, None, :], 0.0), axis=2)
    return (grad_tokens, grad_combine, weight_grads)


def fused(n_e, n_s, tok_hbm, og_hbm, ids_hbm, comb_hbm, wg_hbm, wu_hbm, wd_hbm,
          gt_ref, gc_ref, wgr_ref,
          tok_ref, og_ref, ids_ref, comb_ref, wgu, wd, outx, outs, xs, ss, xa, sa, subs, ga, back, mid, tot, ret,
          w_sem, out_send, near_send, half_send, recv, half_recv,
          q_send, q_recv, g_send, g_recv,
          b_send, b_recv, m_send, m_recv, t_send, t_recv):
    me = lax.axis_index("expert")
    sq = lax.axis_index("seq")
    groups = n_e // HSPLIT
    grp = me // HSPLIT
    part = lax.rem(me, HSPLIT)
    near = (part + 1 - 2 * lax.rem(part, 2), lax.rem(part + 2, HSPLIT))
    rows = n_e * ROWS
    used = groups * ROWS
    width = wd.shape[0]
    toks, feats = tok_ref.shape
    top = ids_ref.shape[0]
    share = feats // n_s
    sub = share * EXTRA // ROWS
    head = CHUNKS * sub
    packed = n_s * head
    last = slice(packed, feats)
    halves = (slice(0, packed // 2), slice(packed // 2, packed))

    def lanes(s, m):
        return slice(s * head + m * sub, s * head + (m + 1) * sub)

    def by_share(ref, here, m):
        return jnp.concatenate([ref[here, lanes(s, m)] for s in range(n_s)], axis=1)

    wg = wgu.at[0:width, :]
    wu = wgu.at[width : 2 * width, :]
    pairs_in = [
        (ids_hbm, ids_ref), (comb_hbm, comb_ref), (tok_hbm, tok_ref), (og_hbm, og_ref)]
    for src, dst in ((wg_hbm.at[0], wg), (wu_hbm.at[0], wu), (wd_hbm.at[0], wd)):
        for s in range(n_s):
            pairs_in.append((src.at[:, s * share : s * share + head],
                             dst.at[:, s * head : (s + 1) * head]))
            pairs_in.append((src.at[:, s * share + head : (s + 1) * share],
                             dst.at[:, packed + s * sub : packed + (s + 1) * sub]))
    loads = [
        pltpu.make_async_copy(src, dst, w_sem.at[i]) for i, (src, dst) in enumerate(pairs_in)
    ]
    up_to = 4 + 4 * n_s
    for load in loads:
        load.start()

    def holder(g, p):
        return lax.rem(grp + g, groups) * HSPLIT + lax.rem(part + p, HSPLIT)

    met = [(holder(g, 0), sq) for g in range(1, groups)]
    met += [(holder(0, p), sq) for p in range(1, HSPLIT)]
    met += [(me, lax.rem(sq + step, n_s)) for step in range(1, n_s)]
    barrier = pltpu.get_barrier_semaphore()
    for device in met:
        pl.semaphore_signal(barrier, inc=1, device_id=device, device_id_type=MESH)

    def iota(shape, dim):
        return lax.broadcasted_iota(jnp.int32, shape, dim)

    def one_hot(mask):
        return mask.astype(F32).astype(BF16)

    def mm(left, right):
        return jnp.dot(left, right, preferred_element_type=F32)

    loads[0].wait()
    loads[1].wait()
    ids = ids_ref[...]
    comb = comb_ref[...]
    e_row = iota((used, toks), 0) // ROWS
    c_row = lax.rem(iota((used, toks), 0), ROWS)
    routed = jnp.zeros((used, toks), F32)
    weight = jnp.zeros((used, toks), F32)
    for k in range(top):
        hit = ids[k : k + 1, :] == e_row
        routed = jnp.where(hit, 1.0, routed)
        weight = jnp.where(hit, comb[k : k + 1, :], weight)
    earlier = mm(routed.astype(BF16), one_hot(iota((toks, toks), 0) < iota((toks, toks), 1)))

    def picked(slot, mask):
        return jnp.where(mask & (earlier == slot.astype(F32)), routed, 0.0)

    base = picked(c_row, c_row < CAP)
    tails = [picked(c_row - CAP + EXTRA * m, c_row >= CAP) for m in range(CHUNKS)]
    base_bf = base.astype(BF16)
    tails_bf = [tail.astype(BF16) for tail in tails]
    tails_all = jnp.concatenate(tails, axis=0).astype(BF16)

    def gather_to(out, ref, scales):
        for s in range(n_s):
            main = mm(base_bf, ref[:, s * share : s * share + head])
            tail = mm(tails_all, ref[:, s * share + head : (s + 1) * share])
            for m in range(CHUNKS):
                value = main[:, m * sub : (m + 1) * sub] + tail[m * used : (m + 1) * used]
                if scales is not None:
                    value = scales[m] * value
                out[:, lanes(s, m)] = value.astype(BF16)

    def at(i):
        return pl.ds(pl.multiple_of(i * ROWS, ROWS), ROWS)

    sends = []

    def send(src, dst, send_sem, recv_sem, device):
        copy = pltpu.make_async_remote_copy(
            src_ref=src, dst_ref=dst, send_sem=send_sem, recv_sem=recv_sem,
            device_id=device, device_id_type=MESH)
        copy.start()
        sends.append(copy)

    def arrived(ref, sem):
        pltpu.make_async_copy(ref, ref, sem).wait()

    full = slice(0, packed)
    landing = (xs, ss)

    def place(index, p):
        return at(index * HSPLIT + p)

    def pass_on(a, src, index):
        for n in range(2):
            send(src, landing[a].at[place(index, part), full], near_send.at[a, index, n],
                 recv.at[a, index, part], (grp * HSPLIT + near[n], sq))

    def first(a, out):
        for step in range(1, groups):
            to = lax.rem(grp + step, groups)
            send(out.at[at(to), :], landing[a].at[place(groups - step, part), full],
                 out_send.at[a, step - 1], recv.at[a, groups - step, part],
                 (to * HSPLIT + part, sq))

    def relay(a, index):
        for n in range(2):
            arrived(landing[a].at[place(index, near[n]), full], recv.at[a, index, near[n]])
            half = landing[a].at[place(index, near[n]), halves[n]]
            send(half, half, half_send.at[a, index, n], half_recv.at[a, index, n],
                 (grp * HSPLIT + near[1 - n], sq))

    def enter(a, index):
        block = landing[a].at[place(index, part), full]
        arrived(block, recv.at[a, index, part])
        pass_on(a, block, index)

    def far(a, index):
        source = lax.rem(near[0] + 2, HSPLIT)
        for n in range(2):
            arrived(landing[a].at[place(index, source), halves[n]], half_recv.at[a, index, n])

    loads[2].wait()
    gather_to(outx, tok_ref, None)
    pl.semaphore_wait(barrier, len(met))
    first(0, outx)
    pass_on(0, outx.at[at(grp), :], 0)
    loads[3].wait()
    gather_to(outs, og_ref, [
        jnp.sum((base + tail) * weight, axis=1, keepdims=True) for tail in tails])
    first(1, outs)
    xs[place(0, part), full] = outx[at(grp), :]
    ss[place(0, part), full] = outs[at(grp), :]

    def slots(count):
        at_r = iota((count, count), 0)
        at_c = iota((count, count), 1)
        return at_r // ROWS == at_c // ROWS, lax.rem(at_r, ROWS), lax.rem(at_c, ROWS)

    quad = HSPLIT * ROWS
    together, r_slot, c_slot = slots(quad)
    unfold = [
        one_hot(together & (c_slot >= CAP) & (c_slot - CAP + EXTRA * m == r_slot))
        for m in range(CHUNKS)
    ]
    fold = [
        one_hot(together & (r_slot >= CAP) & (r_slot - CAP + EXTRA * m == c_slot))
        for m in range(CHUNKS)
    ]
    valid = lax.rem(iota((width, quad), 1), ROWS) < CAP
    shares = (xa, sa)

    def group_rows(index):
        return slice(index * quad, (index + 1) * quad)

    def complete(a, index):
        far(a, index)
        ref = landing[a]
        here = group_rows(index)
        for step in range(1, n_s):
            peer = lax.rem(sq + step, n_s)
            mine = pl.ds(pl.multiple_of(peer * head, LANES), head)
            send(ref.at[here, mine], shares[a].at[sq, here, :], q_send.at[a, index, step - 1],
                 q_recv.at[a, sq, index], (me, peer))
        total = mm(unfold[0], by_share(ref, here, 0))
        for m in range(1, CHUNKS):
            total = total + mm(unfold[m], by_share(ref, here, m))
        ref[here, last] = total.astype(BF16)

    across = (((1,), (1,)), ((), ()))

    beyond = range(1, groups)
    for index in beyond:
        enter(0, index)
    relay(0, 0)
    for index in beyond:
        enter(1, index)
    pass_on(1, outs.at[at(grp), :], 0)
    for index in beyond:
        relay(0, index)
    complete(0, 0)
    for index in beyond:
        relay(1, index)
    for index in beyond:
        complete(0, index)
    for load in loads[4:up_to]:
        load.wait()
    gate_up = lax.dot_general(wgu[...], xs[...], across, preferred_element_type=F32)
    gate_all = gate_up[0:width]
    up_all = gate_up[width : 2 * width]
    sig_all = 1.0 / (1.0 + jnp.exp(-gate_all))
    act_all = gate_all * sig_all
    hidden_all = act_all * up_all
    d_gate_all = up_all * sig_all * (1.0 + gate_all * (1.0 - sig_all))
    relay(1, 0)
    for load in loads[up_to:]:
        load.wait()
    keep = lax.rem(iota((quad, sub), 0), ROWS) < CAP
    terms = [None] * groups

    def backward(index):
        here = group_rows(index)
        complete(1, index)
        hgrad = jnp.where(
            valid, lax.dot_general(wd[...], ss[here, :], across, preferred_element_type=F32), 0.0)
        hidden = jnp.where(valid, hidden_all[:, here], 0.0).astype(BF16)
        g_gate_t = (hgrad * d_gate_all[:, here]).astype(BF16)
        g_up_t = (hgrad * act_all[:, here]).astype(BF16)
        terms[index] = (g_gate_t, g_up_t, hidden)
        row_part = jnp.sum(hidden.astype(F32) * hgrad, axis=0, keepdims=True)
        back[here, packed : packed + LANES] = jnp.broadcast_to(
            row_part, (LANES, quad)).T.astype(BF16)
        g_gate = g_gate_t.T
        g_up = g_up_t.T
        tail_grad = (mm(g_gate, wg[:, last]) + mm(g_up, wu[:, last])).astype(BF16)
        folded = [mm(fold[m], tail_grad) for m in range(CHUNKS)]
        for s in range(n_s):
            span = slice(s * head, (s + 1) * head)
            whole = mm(g_gate, wg[:, span]) + mm(g_up, wu[:, span])
            for m in range(CHUNKS):
                back[here, lanes(s, m)] = jnp.where(
                    keep, whole[:, m * sub : (m + 1) * sub], folded[m][:, s * sub : (s + 1) * sub]
                ).astype(BF16)

    for index in beyond:
        backward(index)
        for p in range(1, HSPLIT):
            to = lax.rem(part + p, HSPLIT)
            send(back.at[place(index, to), :], mid.at[index - 1, part],
                 m_send.at[index - 1, p - 1], m_recv.at[index - 1, part], (holder(0, p), sq))
    backward(0)

    def lanes_of(s):
        return pl.ds(pl.multiple_of(s * rows, LANES), rows)

    for i in range(3):
        ga[i * width : (i + 1) * width, lanes_of(sq)] = jnp.concatenate(
            [terms[index][i] for index in range(groups)], axis=1)
    pairs = n_s // 2
    core = lax.rem(sq, 2)
    mate = sq + 1 - 2 * core
    peers = [lax.rem(sq // 2 + step, pairs) * 2 + core for step in range(1, pairs)]

    def to_seq(source, count, peer):
        block = ga.at[:, lanes_of(source)]
        send(block, block, g_send.at[count], g_recv.at[source], (me, peer))

    for count, peer in enumerate(peers):
        to_seq(sq, count, peer)
    to_seq(sq, pairs - 1, mate)

    for p in range(1, HSPLIT):
        send(back.at[place(0, lax.rem(part + p, HSPLIT)), :], ret.at[at(part), :],
             b_send.at[p - 1], b_recv.at[part], (holder(0, p), sq))
    ret[at(part), :] = back[place(0, part), :]
    for index in beyond:
        total = back[place(index, part), :].astype(F32)
        for p in range(1, HSPLIT):
            other = lax.rem(part + p, HSPLIT)
            arrived(mid.at[index - 1, other], m_recv.at[index - 1, other])
            total = total + mid[index - 1, other].astype(F32)
        tot[index - 1] = total.astype(BF16)
        send(tot.at[index - 1], ret.at[at(HSPLIT + groups - index - 1), :],
             t_send.at[index - 1], t_recv.at[groups - index - 1], (holder(index, 0), sq))

    landed = (HSPLIT + groups - 1) * ROWS

    def expert_at(block):
        return lax.rem(grp + jnp.maximum(block - HSPLIT + 1, 0), groups)

    def same(shape, ret_dim):
        of_ret = iota(shape, ret_dim)
        of_slot = iota(shape, 1 - ret_dim)
        return one_hot((expert_at(of_ret // ROWS) == of_slot // ROWS)
                       & (lax.rem(of_ret, ROWS) == lax.rem(of_slot, ROWS)))

    widen = same((landed, used), 0)
    home = mm(widen, base_bf).T.astype(BF16)
    home_tails = [mm(widen, tail).T.astype(BF16) for tail in tails_bf]
    gather = same((used, landed), 1)

    mine = pl.ds(pl.multiple_of(sq * head, LANES), head)
    xa[sq] = xs[:, mine]
    sa[sq] = ss[:, mine]
    for a, ref in enumerate(shares):
        for step in range(1, n_s):
            peer = lax.rem(sq + step, n_s)
            for index in range(groups):
                arrived(ref.at[peer, group_rows(index), :], q_recv.at[a, peer, index])
        found = jnp.zeros((quad, n_s * groups * sub), F32)
        for m in range(CHUNKS):
            found = found + mm(unfold[m], jnp.concatenate(
                [ref[s, group_rows(index), m * sub : (m + 1) * sub]
                 for s in range(n_s) for index in range(groups)], axis=1))
        for s in range(n_s):
            for index in range(groups):
                spot = s * groups + index
                subs[a, s, group_rows(index), :] = found[
                    :, spot * sub : (spot + 1) * sub].astype(BF16)
    for count, peer in enumerate(peers):
        arrived(ga.at[:, lanes_of(peer)], g_recv.at[peer])
        to_seq(peer, pairs + count, mate)
    arrived(ga.at[:, lanes_of(mate)], g_recv.at[mate])
    for peer in peers:
        twin = peer + 1 - 2 * core
        arrived(ga.at[:, lanes_of(twin)], g_recv.at[twin])
    every = n_s * rows
    for a, units in enumerate((slice(0, 2 * width), slice(2 * width, 3 * width))):
        wgr_ref[units, 0:head] = mm(
            ga[units, :], shares[a][...].reshape(every, head)).astype(BF16)
        wgr_ref[units, head:share] = mm(
            ga[units, :], subs[a].reshape(every, sub)).astype(BF16)

    for p in range(1, HSPLIT):
        other = lax.rem(part + p, HSPLIT)
        arrived(ret.at[at(other), :], b_recv.at[other])
    for index in beyond:
        arrived(ret.at[at(HSPLIT + index - 1), :], t_recv.at[index - 1])
    whole_ret = slice(0, landed)
    tail_sum = jnp.zeros((toks, n_s * sub), F32)
    for m in range(CHUNKS):
        tail_sum = tail_sum + mm(home_tails[m], by_share(ret, whole_ret, m))
    for s in range(n_s):
        gt_ref[:, s * share : s * share + head] = mm(
            home, ret[:, s * head : (s + 1) * head]).astype(BF16)
        gt_ref[:, s * share + head : (s + 1) * share] = tail_sum[
            :, s * sub : (s + 1) * sub].astype(BF16)
    per_slot = base * mm(gather, ret[:, packed : packed + LANES])
    at_k = iota((top, toks), 0)
    total = jnp.zeros((top, toks), F32)
    for k in range(top):
        mine = jnp.sum(jnp.where(ids[k : k + 1, :] == e_row, per_slot, 0.0), axis=0, keepdims=True)
        total = jnp.where(at_k == k, mine, total)
    gc_ref[...] = total / comb
    for copy in sends:
        copy.wait_send()


def local_fused(n_e, n_s, tokens, out_grad, expert_ids, combine, w_gate, w_up, w_down):
    toks, feats = tokens.shape
    width = w_gate.shape[2]
    share = feats // n_s
    groups = n_e // HSPLIT
    rows = n_e * ROWS
    packed = feats * CAP // ROWS
    crossing = max(1, groups - 1)
    dma = pltpu.SemaphoreType.DMA
    vmem = pl.BlockSpec(memory_space=pltpu.VMEM)
    hbm = pl.BlockSpec(memory_space=pl.ANY)
    grad_tokens, grad_combine, flat = pl.pallas_call(
        functools.partial(fused, n_e, n_s),
        out_shape=(
            pltpu.VMEM((toks, feats), BF16),
            pltpu.VMEM(combine.shape[::-1], F32),
            pltpu.VMEM((3 * width, share), BF16),
        ),
        in_specs=[hbm] * 7,
        out_specs=(vmem,) * 3,
        scratch_shapes=[
            pltpu.VMEM((toks, feats), BF16),
            pltpu.VMEM((toks, feats), BF16),
            pltpu.VMEM(expert_ids.shape[::-1], jnp.int32),
            pltpu.VMEM(combine.shape[::-1], F32),
            pltpu.VMEM((2 * width, feats), BF16),
            pltpu.VMEM((width, feats), BF16),
            pltpu.VMEM((groups * ROWS, packed), BF16),
            pltpu.VMEM((groups * ROWS, packed), BF16),
            pltpu.VMEM((rows, feats), BF16),
            pltpu.VMEM((rows, feats), BF16),
            pltpu.VMEM((n_s, rows, share * CAP // ROWS), BF16),
            pltpu.VMEM((n_s, rows, share * CAP // ROWS), BF16),
            pltpu.VMEM((2, n_s, rows, share * EXTRA // ROWS), BF16),
            pltpu.VMEM((3 * width, n_s * rows), BF16),
            pltpu.VMEM((rows, packed + LANES), BF16),
            pltpu.VMEM((crossing, HSPLIT, ROWS, packed + LANES), BF16),
            pltpu.VMEM((crossing, ROWS, packed + LANES), BF16),
            pltpu.VMEM(((HSPLIT + groups - 1) * ROWS, packed + LANES), BF16),
            dma((4 + 6 * n_s,)),
            dma((2, crossing)),
            dma((2, groups, 2)),
            dma((2, groups, 2)),
            dma((2, groups, HSPLIT)),
            dma((2, groups, 2)),
            dma((2, groups, n_s - 1)),
            dma((2, n_s, groups)),
            dma((n_s - 1,)),
            dma((n_s,)),
            dma((HSPLIT - 1,)),
            dma((HSPLIT,)),
            dma((crossing, HSPLIT - 1)),
            dma((crossing, HSPLIT)),
            dma((crossing,)),
            dma((crossing,)),
        ],
        compiler_params=pltpu.CompilerParams(
            collective_id=0, has_side_effects=True, vmem_limit_bytes=VMEM_BYTES),
        cost_estimate=pl.CostEstimate(
            flops=18 * rows * feats * width, bytes_accessed=8 * feats * width,
            transcendentals=rows * width),
    )(
        tokens, out_grad, expert_ids.T, combine.T,
        w_gate.transpose(0, 2, 1), w_up.transpose(0, 2, 1), w_down,
    )
    weight_grads = flat.reshape(1, 3, width, share).transpose(0, 3, 1, 2)
    return grad_tokens, grad_combine.T, weight_grads


def solution(mesh):
    in_specs = (
        P(("expert", "seq"), None),
        P(("expert", "seq"), None),
        P(("expert", "seq"), None),
        P(("expert", "seq"), None),
        P("expert", None, None),
        P("expert", None, None),
        P("expert", None, None),
    )
    out_specs = (
        P(("expert", "seq"), None),
        P(("expert", "seq"), None),
        P("expert", "seq", None, None),
    )
    n_e, n_s = mesh.shape["expert"], mesh.shape["seq"]
    fits = n_s % 2 == 0 and D * EXTRA // ROWS % (n_s * LANES) == 0
    body = functools.partial(local_fused, n_e, n_s) if fits else local
    return jax.shard_map(body, mesh=mesh, in_specs=in_specs, out_specs=out_specs, check_vma=False)
```

```python
import functools

import jax
import jax.numpy as jnp
from jax import lax
from jax.experimental import pallas as pl
from jax.experimental.pallas import tpu as pltpu
from jax.sharding import PartitionSpec as P

D = 2048
HSPLIT = 4
CAP = 12
ROWS = 16
EXTRA = ROWS - CAP
CHUNKS = CAP // EXTRA
LANES = 128
VMEM_BYTES = 61500 * 1024
MESH = pl.DeviceIdType.MESH
F32 = jnp.float32
BF16 = jnp.bfloat16


def contract_rows(left, right):
    return lax.dot_general(
        left, right, (((0,), (0,)), ((), ())), preferred_element_type=jnp.float32
    )


def contract_cols(left, right):
    return lax.dot_general(
        left, right, (((1,), (1,)), ((), ())), preferred_element_type=jnp.float32
    )


def local(tokens, out_grad, expert_ids, combine, w_gate, w_up, w_down):
    n_expert = lax.axis_size("expert")
    experts = n_expert // HSPLIT
    tok_dev = tokens.shape[0]
    slice_width = w_gate.shape[2]
    wanted = lax.broadcasted_iota(jnp.int32, (1, 1, experts), 2)
    chosen = expert_ids[:, :, None] == wanted
    routed = jnp.any(chosen, axis=1).astype(jnp.int32)
    earlier = jnp.cumsum(routed, axis=0, dtype=jnp.int32) - routed
    slot_ids = lax.broadcasted_iota(jnp.int32, (1, CAP, 1), 1)
    picker = (earlier.T[:, None, :] == slot_ids) & (routed.T[:, None, :] == 1)
    picker_bf = picker.astype(jnp.bfloat16)
    weight_te = jnp.sum(jnp.where(chosen, combine[:, :, None], 0.0), axis=1)
    send_x = jnp.einsum(
        "ect,td->ecd", picker_bf, tokens, preferred_element_type=jnp.float32
    ).astype(jnp.bfloat16)
    send_g = jnp.einsum(
        "ect,td->ecd", picker_bf, out_grad, preferred_element_type=jnp.float32
    ).astype(jnp.bfloat16)
    send_w = jnp.sum(jnp.where(picker, weight_te.T[:, None, :], 0.0), axis=2)
    out_x = jnp.repeat(send_x, HSPLIT, axis=0)
    out_g = jnp.repeat(send_g, HSPLIT, axis=0)
    out_w = jnp.repeat(send_w, HSPLIT, axis=0)
    rows_x = lax.all_to_all(out_x, "expert", split_axis=0, concat_axis=0, tiled=True)
    rows_g, rows_w = (
        lax.all_to_all(out_g, "expert", split_axis=0, concat_axis=0, tiled=True),
        lax.all_to_all(
            out_w.astype(jnp.bfloat16), "expert", split_axis=0, concat_axis=0, tiled=True
        ).astype(out_w.dtype),
    )
    flat_x = rows_x.reshape(-1, D)
    flat_g = rows_g.reshape(-1, D)
    flat_w = rows_w.reshape(-1)
    gate_cols = w_gate[0]
    up_cols = w_up[0]
    down_rows = w_down[0]
    gate_pre = jnp.dot(flat_x, gate_cols, preferred_element_type=jnp.float32)
    up_pre = jnp.dot(flat_x, up_cols, preferred_element_type=jnp.float32)
    sig_gate = jax.nn.sigmoid(gate_pre)
    act_gate = gate_pre * sig_gate
    hidden = (act_gate * up_pre).astype(jnp.bfloat16)
    expert_out = jnp.dot(hidden, down_rows, preferred_element_type=jnp.float32)
    comb_part = jnp.sum(flat_g.astype(jnp.float32) * expert_out, axis=1)
    scaled = (flat_w[:, None] * flat_g.astype(jnp.float32)).astype(jnp.bfloat16)
    hidden_grad = contract_cols(scaled, down_rows)
    grad_gate = (hidden_grad * up_pre * sig_gate * (1.0 + gate_pre * (1.0 - sig_gate))).astype(
        jnp.bfloat16
    )
    grad_up = (hidden_grad * act_gate).astype(jnp.bfloat16)
    back_rows = (contract_cols(grad_gate, gate_cols) + contract_cols(grad_up, up_cols)).astype(
        jnp.bfloat16
    )
    both_grads = jnp.concatenate([grad_gate, grad_up], axis=1)
    terms = jnp.concatenate(
        [contract_rows(flat_x, both_grads), contract_rows(scaled, hidden)], axis=1
    )
    summed = lax.psum_scatter(
        terms.astype(jnp.bfloat16), "seq", scatter_dimension=0, tiled=True
    ).astype(jnp.float32)
    weight_grads = summed.astype(jnp.bfloat16).reshape(1, summed.shape[0], 3, slice_width)
    ret_x, ret_c = (
        lax.all_to_all(
            back_rows.reshape(n_expert, CAP, D), "expert", split_axis=0, concat_axis=0, tiled=True
        ),
        lax.all_to_all(
            comb_part.reshape(n_expert, CAP).astype(jnp.bfloat16),
            "expert",
            split_axis=0,
            concat_axis=0,
            tiled=True,
        ).astype(jnp.float32),
    )
    spread = jnp.repeat(picker_bf, HSPLIT, axis=0).reshape(n_expert * CAP, tok_dev)
    grad_tokens = contract_rows(spread, ret_x.reshape(-1, D)).astype(jnp.bfloat16)
    comb_slots = jnp.sum(ret_c.reshape(experts, HSPLIT, CAP), axis=1)
    comb_te = jnp.sum(jnp.where(picker, comb_slots[:, :, None], 0.0), axis=1)
    grad_combine = jnp.sum(jnp.where(chosen, comb_te.T[:, None, :], 0.0), axis=2)
    return (grad_tokens, grad_combine, weight_grads)


def fused(n_e, n_s, tok_hbm, og_hbm, ids_hbm, comb_hbm, wg_hbm, wu_hbm, wd_hbm,
          gt_ref, gc_ref, wgr_ref,
          tok_ref, og_ref, ids_ref, comb_ref, wgu, wd, outx, outs, xs, ss, xa, sa, subs, ga, back, mid, tot, ret,
          w_sem, out_send, near_send, half_send, recv, half_recv,
          q_send, q_recv, g_send, g_recv,
          b_send, b_recv, m_send, m_recv, t_send, t_recv):
    me = lax.axis_index("expert")
    sq = lax.axis_index("seq")
    groups = n_e // HSPLIT
    grp = me // HSPLIT
    part = lax.rem(me, HSPLIT)
    near = (part + 1 - 2 * lax.rem(part, 2), lax.rem(part + 2, HSPLIT))
    rows = n_e * ROWS
    used = groups * ROWS
    width = wd.shape[0]
    toks, feats = tok_ref.shape
    top = ids_ref.shape[0]
    share = feats // n_s
    sub = share * EXTRA // ROWS
    head = CHUNKS * sub
    packed = n_s * head
    last = slice(packed, feats)
    halves = (slice(0, packed // 2), slice(packed // 2, packed))

    def lanes(s, m):
        return slice(s * head + m * sub, s * head + (m + 1) * sub)

    def by_share(ref, here, m):
        return jnp.concatenate([ref[here, lanes(s, m)] for s in range(n_s)], axis=1)

    wg = wgu.at[0:width, :]
    wu = wgu.at[width : 2 * width, :]
    pairs_in = [
        (ids_hbm, ids_ref), (comb_hbm, comb_ref), (tok_hbm, tok_ref), (og_hbm, og_ref)]
    for src, dst in ((wg_hbm.at[0], wg), (wu_hbm.at[0], wu), (wd_hbm.at[0], wd)):
        for s in range(n_s):
            pairs_in.append((src.at[:, s * share : s * share + head],
                             dst.at[:, s * head : (s + 1) * head]))
            pairs_in.append((src.at[:, s * share + head : (s + 1) * share],
                             dst.at[:, packed + s * sub : packed + (s + 1) * sub]))
    loads = [
        pltpu.make_async_copy(src, dst, w_sem.at[i]) for i, (src, dst) in enumerate(pairs_in)
    ]
    up_to = 4 + 4 * n_s
    for load in loads:
        load.start()

    def holder(g, p):
        return lax.rem(grp + g, groups) * HSPLIT + lax.rem(part + p, HSPLIT)

    met = [(holder(g, 0), sq) for g in range(1, groups)]
    met += [(holder(0, p), sq) for p in range(1, HSPLIT)]
    met += [(me, lax.rem(sq + step, n_s)) for step in range(1, n_s)]
    barrier = pltpu.get_barrier_semaphore()
    for device in met:
        pl.semaphore_signal(barrier, inc=1, device_id=device, device_id_type=MESH)

    def iota(shape, dim):
        return lax.broadcasted_iota(jnp.int32, shape, dim)

    def one_hot(mask):
        return mask.astype(F32).astype(BF16)

    def mm(left, right):
        return jnp.dot(left, right, preferred_element_type=F32)

    loads[0].wait()
    loads[1].wait()
    ids = ids_ref[...]
    comb = comb_ref[...]
    e_row = iota((used, toks), 0) // ROWS
    c_row = lax.rem(iota((used, toks), 0), ROWS)
    routed = jnp.zeros((used, toks), F32)
    weight = jnp.zeros((used, toks), F32)
    for k in range(top):
        hit = ids[k : k + 1, :] == e_row
        routed = jnp.where(hit, 1.0, routed)
        weight = jnp.where(hit, comb[k : k + 1, :], weight)
    earlier = mm(routed.astype(BF16), one_hot(iota((toks, toks), 0) < iota((toks, toks), 1)))

    def picked(slot, mask):
        return jnp.where(mask & (earlier == slot.astype(F32)), routed, 0.0)

    base = picked(c_row, c_row < CAP)
    tails = [picked(c_row - CAP + EXTRA * m, c_row >= CAP) for m in range(CHUNKS)]
    base_bf = base.astype(BF16)
    tails_bf = [tail.astype(BF16) for tail in tails]
    tails_all = jnp.concatenate(tails, axis=0).astype(BF16)

    def gather_to(out, ref, scales):
        for s in range(n_s):
            main = mm(base_bf, ref[:, s * share : s * share + head])
            tail = mm(tails_all, ref[:, s * share + head : (s + 1) * share])
            for m in range(CHUNKS):
                value = main[:, m * sub : (m + 1) * sub] + tail[m * used : (m + 1) * used]
                if scales is not None:
                    value = scales[m] * value
                out[:, lanes(s, m)] = value.astype(BF16)

    def at(i):
        return pl.ds(pl.multiple_of(i * ROWS, ROWS), ROWS)

    sends = []

    def send(src, dst, send_sem, recv_sem, device):
        copy = pltpu.make_async_remote_copy(
            src_ref=src, dst_ref=dst, send_sem=send_sem, recv_sem=recv_sem,
            device_id=device, device_id_type=MESH)
        copy.start()
        sends.append(copy)

    def arrived(ref, sem):
        pltpu.make_async_copy(ref, ref, sem).wait()

    full = slice(0, packed)
    landing = (xs, ss)

    def place(index, p):
        return at(index * HSPLIT + p)

    opposite = lax.rem(near[0] + 2, HSPLIT)

    def to_peers(a, slot, src, src_rows, dst_rows):
        for step in range(1, n_s):
            peer = lax.rem(sq + step, n_s)
            mine = pl.ds(pl.multiple_of(peer * head, LANES), head)
            send(src.at[src_rows, mine], (xa, sa)[a].at[sq, dst_rows, :],
                 q_send.at[a, slot, step - 1], q_recv.at[a, sq, slot], (me, peer))

    def pass_on(a, src, index):
        for n in range(2):
            send(src, landing[a].at[place(index, part), full], near_send.at[a, index, n],
                 recv.at[a, index, part], (grp * HSPLIT + near[n], sq))

    def first(a, out):
        for step in range(1, groups):
            to = lax.rem(grp + step, groups)
            send(out.at[at(to), :], landing[a].at[place(groups - step, part), full],
                 out_send.at[a, step - 1], recv.at[a, groups - step, part],
                 (to * HSPLIT + part, sq))

    def relay(a, index):
        for n in range(2):
            arrived(landing[a].at[place(index, near[n]), full], recv.at[a, index, near[n]])
            half = landing[a].at[place(index, near[n]), halves[n]]
            send(half, half, half_send.at[a, index, n], half_recv.at[a, index, n],
                 (grp * HSPLIT + near[1 - n], sq))
            if index == 0:
                to_peers(a, 1 + n, landing[a], place(0, near[n]), place(0, near[n]))

    def enter(a, index):
        block = landing[a].at[place(index, part), full]
        arrived(block, recv.at[a, index, part])
        pass_on(a, block, index)

    def far(a, index):
        source = lax.rem(near[0] + 2, HSPLIT)
        for n in range(2):
            arrived(landing[a].at[place(index, source), halves[n]], half_recv.at[a, index, n])

    loads[2].wait()
    gather_to(outx, tok_ref, None)
    pl.semaphore_wait(barrier, len(met))
    first(0, outx)
    pass_on(0, outx.at[at(grp), :], 0)
    to_peers(0, 0, outx, at(grp), place(0, part))
    loads[3].wait()
    gather_to(outs, og_ref, [
        jnp.sum((base + tail) * weight, axis=1, keepdims=True) for tail in tails])
    first(1, outs)
    to_peers(1, 0, outs, at(grp), place(0, part))
    xs[place(0, part), full] = outx[at(grp), :]
    ss[place(0, part), full] = outs[at(grp), :]

    def slots(count):
        at_r = iota((count, count), 0)
        at_c = iota((count, count), 1)
        return at_r // ROWS == at_c // ROWS, lax.rem(at_r, ROWS), lax.rem(at_c, ROWS)

    quad = HSPLIT * ROWS
    together, r_slot, c_slot = slots(quad)
    unfold = [
        one_hot(together & (c_slot >= CAP) & (c_slot - CAP + EXTRA * m == r_slot))
        for m in range(CHUNKS)
    ]
    fold = [
        one_hot(together & (r_slot >= CAP) & (r_slot - CAP + EXTRA * m == c_slot))
        for m in range(CHUNKS)
    ]
    valid = lax.rem(iota((width, quad), 1), ROWS) < CAP
    shares = (xa, sa)

    def group_rows(index):
        return slice(index * quad, (index + 1) * quad)

    def complete(a, index):
        far(a, index)
        ref = landing[a]
        here = group_rows(index)
        if index:
            to_peers(a, HSPLIT - 1 + index, ref, here, here)
        else:
            to_peers(a, HSPLIT - 1, ref, place(0, opposite), place(0, opposite))
        total = mm(unfold[0], by_share(ref, here, 0))
        for m in range(1, CHUNKS):
            total = total + mm(unfold[m], by_share(ref, here, m))
        ref[here, last] = total.astype(BF16)

    across = (((1,), (1,)), ((), ()))

    beyond = range(1, groups)
    for index in beyond:
        enter(0, index)
    relay(0, 0)
    for index in beyond:
        enter(1, index)
    pass_on(1, outs.at[at(grp), :], 0)
    for index in beyond:
        relay(0, index)
    complete(0, 0)
    for index in beyond:
        relay(1, index)
    for index in beyond:
        complete(0, index)
    for load in loads[4:up_to]:
        load.wait()
    gate_up = lax.dot_general(wgu[...], xs[...], across, preferred_element_type=F32)
    gate_all = gate_up[0:width]
    up_all = gate_up[width : 2 * width]
    sig_all = 1.0 / (1.0 + jnp.exp(-gate_all))
    act_all = gate_all * sig_all
    hidden_all = act_all * up_all
    d_gate_all = up_all * sig_all * (1.0 + gate_all * (1.0 - sig_all))
    relay(1, 0)
    for load in loads[up_to:]:
        load.wait()
    keep = lax.rem(iota((quad, sub), 0), ROWS) < CAP
    terms = [None] * groups

    def unit_grads(index):
        here = group_rows(index)
        complete(1, index)
        hgrad = jnp.where(
            valid, lax.dot_general(wd[...], ss[here, :], across, preferred_element_type=F32), 0.0)
        hidden = jnp.where(valid, hidden_all[:, here], 0.0).astype(BF16)
        g_gate_t = (hgrad * d_gate_all[:, here]).astype(BF16)
        g_up_t = (hgrad * act_all[:, here]).astype(BF16)
        terms[index] = (g_gate_t, g_up_t, hidden, hgrad)

    def row_grads(index):
        here = group_rows(index)
        g_gate_t, g_up_t, hidden, hgrad = terms[index]
        row_part = jnp.sum(hidden.astype(F32) * hgrad, axis=0, keepdims=True)
        back[here, packed : packed + LANES] = jnp.broadcast_to(
            row_part, (LANES, quad)).T.astype(BF16)
        g_gate = g_gate_t.T
        g_up = g_up_t.T
        tail_grad = (mm(g_gate, wg[:, last]) + mm(g_up, wu[:, last])).astype(BF16)
        folded = [mm(fold[m], tail_grad) for m in range(CHUNKS)]
        for s in range(n_s):
            span = slice(s * head, (s + 1) * head)
            whole = mm(g_gate, wg[:, span]) + mm(g_up, wu[:, span])
            for m in range(CHUNKS):
                back[here, lanes(s, m)] = jnp.where(
                    keep, whole[:, m * sub : (m + 1) * sub], folded[m][:, s * sub : (s + 1) * sub]
                ).astype(BF16)

    for index in beyond:
        unit_grads(index)
        row_grads(index)
        for p in range(1, HSPLIT):
            to = lax.rem(part + p, HSPLIT)
            send(back.at[place(index, to), :], mid.at[index - 1, part],
                 m_send.at[index - 1, p - 1], m_recv.at[index - 1, part], (holder(0, p), sq))
    unit_grads(0)

    def lanes_of(s):
        return pl.ds(pl.multiple_of(s * rows, LANES), rows)

    for i in range(3):
        ga[i * width : (i + 1) * width, lanes_of(sq)] = jnp.concatenate(
            [terms[index][i] for index in range(groups)], axis=1)
    pairs = n_s // 2
    core = lax.rem(sq, 2)
    mate = sq + 1 - 2 * core
    peers = [lax.rem(sq // 2 + step, pairs) * 2 + core for step in range(1, pairs)]

    def to_seq(source, count, peer):
        block = ga.at[:, lanes_of(source)]
        send(block, block, g_send.at[count], g_recv.at[source], (me, peer))

    for count, peer in enumerate(peers):
        to_seq(sq, count, peer)
    to_seq(sq, pairs - 1, mate)
    row_grads(0)

    for p in range(1, HSPLIT):
        send(back.at[place(0, lax.rem(part + p, HSPLIT)), :], ret.at[at(part), :],
             b_send.at[p - 1], b_recv.at[part], (holder(0, p), sq))
    ret[at(part), :] = back[place(0, part), :]
    for index in beyond:
        total = back[place(index, part), :].astype(F32)
        for p in range(1, HSPLIT):
            other = lax.rem(part + p, HSPLIT)
            arrived(mid.at[index - 1, other], m_recv.at[index - 1, other])
            total = total + mid[index - 1, other].astype(F32)
        tot[index - 1] = total.astype(BF16)
        send(tot.at[index - 1], ret.at[at(HSPLIT + groups - index - 1), :],
             t_send.at[index - 1], t_recv.at[groups - index - 1], (holder(index, 0), sq))

    landed = (HSPLIT + groups - 1) * ROWS

    def expert_at(block):
        return lax.rem(grp + jnp.maximum(block - HSPLIT + 1, 0), groups)

    def same(shape, ret_dim):
        of_ret = iota(shape, ret_dim)
        of_slot = iota(shape, 1 - ret_dim)
        return one_hot((expert_at(of_ret // ROWS) == of_slot // ROWS)
                       & (lax.rem(of_ret, ROWS) == lax.rem(of_slot, ROWS)))

    widen = same((landed, used), 0)
    home = mm(widen, base_bf).T.astype(BF16)
    home_tails = [mm(widen, tail).T.astype(BF16) for tail in tails_bf]
    gather = same((used, landed), 1)

    mine = pl.ds(pl.multiple_of(sq * head, LANES), head)
    xa[sq] = xs[:, mine]
    sa[sq] = ss[:, mine]
    for a, ref in enumerate(shares):
        for step in range(1, n_s):
            peer = lax.rem(sq + step, n_s)
            own_four = (part, near[0], near[1], opposite)
            arriving = [place(0, p) for p in own_four] + [group_rows(i) for i in beyond]
            for slot, here in enumerate(arriving):
                arrived(ref.at[peer, here, :], q_recv.at[a, peer, slot])
        found = jnp.zeros((quad, n_s * groups * sub), F32)
        for m in range(CHUNKS):
            found = found + mm(unfold[m], jnp.concatenate(
                [ref[s, group_rows(index), m * sub : (m + 1) * sub]
                 for s in range(n_s) for index in range(groups)], axis=1))
        for s in range(n_s):
            for index in range(groups):
                spot = s * groups + index
                subs[a, s, group_rows(index), :] = found[
                    :, spot * sub : (spot + 1) * sub].astype(BF16)
    for count, peer in enumerate(peers):
        arrived(ga.at[:, lanes_of(peer)], g_recv.at[peer])
        to_seq(peer, pairs + count, mate)
    arrived(ga.at[:, lanes_of(mate)], g_recv.at[mate])
    for peer in peers:
        twin = peer + 1 - 2 * core
        arrived(ga.at[:, lanes_of(twin)], g_recv.at[twin])
    every = n_s * rows
    for a, units in enumerate((slice(0, 2 * width), slice(2 * width, 3 * width))):
        wgr_ref[units, 0:head] = mm(
            ga[units, :], shares[a][...].reshape(every, head)).astype(BF16)
        wgr_ref[units, head:share] = mm(
            ga[units, :], subs[a].reshape(every, sub)).astype(BF16)

    for p in range(1, HSPLIT):
        other = lax.rem(part + p, HSPLIT)
        arrived(ret.at[at(other), :], b_recv.at[other])
    for index in beyond:
        arrived(ret.at[at(HSPLIT + index - 1), :], t_recv.at[index - 1])
    whole_ret = slice(0, landed)
    tail_sum = jnp.zeros((toks, n_s * sub), F32)
    for m in range(CHUNKS):
        tail_sum = tail_sum + mm(home_tails[m], by_share(ret, whole_ret, m))
    for s in range(n_s):
        gt_ref[:, s * share : s * share + head] = mm(
            home, ret[:, s * head : (s + 1) * head]).astype(BF16)
        gt_ref[:, s * share + head : (s + 1) * share] = tail_sum[
            :, s * sub : (s + 1) * sub].astype(BF16)
    per_slot = base * mm(gather, ret[:, packed : packed + LANES])
    at_k = iota((top, toks), 0)
    total = jnp.zeros((top, toks), F32)
    for k in range(top):
        mine = jnp.sum(jnp.where(ids[k : k + 1, :] == e_row, per_slot, 0.0), axis=0, keepdims=True)
        total = jnp.where(at_k == k, mine, total)
    gc_ref[...] = total / comb
    for copy in sends:
        copy.wait_send()


def local_fused(n_e, n_s, tokens, out_grad, expert_ids, combine, w_gate, w_up, w_down):
    toks, feats = tokens.shape
    width = w_gate.shape[2]
    share = feats // n_s
    groups = n_e // HSPLIT
    rows = n_e * ROWS
    packed = feats * CAP // ROWS
    crossing = max(1, groups - 1)
    dma = pltpu.SemaphoreType.DMA
    vmem = pl.BlockSpec(memory_space=pltpu.VMEM)
    hbm = pl.BlockSpec(memory_space=pl.ANY)
    grad_tokens, grad_combine, flat = pl.pallas_call(
        functools.partial(fused, n_e, n_s),
        out_shape=(
            pltpu.VMEM((toks, feats), BF16),
            pltpu.VMEM(combine.shape[::-1], F32),
            pltpu.VMEM((3 * width, share), BF16),
        ),
        in_specs=[hbm] * 7,
        out_specs=(vmem,) * 3,
        scratch_shapes=[
            pltpu.VMEM((toks, feats), BF16),
            pltpu.VMEM((toks, feats), BF16),
            pltpu.VMEM(expert_ids.shape[::-1], jnp.int32),
            pltpu.VMEM(combine.shape[::-1], F32),
            pltpu.VMEM((2 * width, feats), BF16),
            pltpu.VMEM((width, feats), BF16),
            pltpu.VMEM((groups * ROWS, packed), BF16),
            pltpu.VMEM((groups * ROWS, packed), BF16),
            pltpu.VMEM((rows, feats), BF16),
            pltpu.VMEM((rows, feats), BF16),
            pltpu.VMEM((n_s, rows, share * CAP // ROWS), BF16),
            pltpu.VMEM((n_s, rows, share * CAP // ROWS), BF16),
            pltpu.VMEM((2, n_s, rows, share * EXTRA // ROWS), BF16),
            pltpu.VMEM((3 * width, n_s * rows), BF16),
            pltpu.VMEM((rows, packed + LANES), BF16),
            pltpu.VMEM((crossing, HSPLIT, ROWS, packed + LANES), BF16),
            pltpu.VMEM((crossing, ROWS, packed + LANES), BF16),
            pltpu.VMEM(((HSPLIT + groups - 1) * ROWS, packed + LANES), BF16),
            dma((4 + 6 * n_s,)),
            dma((2, crossing)),
            dma((2, groups, 2)),
            dma((2, groups, 2)),
            dma((2, groups, HSPLIT)),
            dma((2, groups, 2)),
            dma((2, HSPLIT - 1 + groups, n_s - 1)),
            dma((2, n_s, HSPLIT - 1 + groups)),
            dma((n_s - 1,)),
            dma((n_s,)),
            dma((HSPLIT - 1,)),
            dma((HSPLIT,)),
            dma((crossing, HSPLIT - 1)),
            dma((crossing, HSPLIT)),
            dma((crossing,)),
            dma((crossing,)),
        ],
        compiler_params=pltpu.CompilerParams(
            collective_id=0, has_side_effects=True, vmem_limit_bytes=VMEM_BYTES),
        cost_estimate=pl.CostEstimate(
            flops=18 * rows * feats * width, bytes_accessed=8 * feats * width,
            transcendentals=rows * width),
    )(
        tokens, out_grad, expert_ids.T, combine.T,
        w_gate.transpose(0, 2, 1), w_up.transpose(0, 2, 1), w_down,
    )
    weight_grads = flat.reshape(1, 3, width, share).transpose(0, 3, 1, 2)
    return grad_tokens, grad_combine.T, weight_grads


def solution(mesh):
    in_specs = (
        P(("expert", "seq"), None),
        P(("expert", "seq"), None),
        P(("expert", "seq"), None),
        P(("expert", "seq"), None),
        P("expert", None, None),
        P("expert", None, None),
        P("expert", None, None),
    )
    out_specs = (
        P(("expert", "seq"), None),
        P(("expert", "seq"), None),
        P("expert", "seq", None, None),
    )
    n_e, n_s = mesh.shape["expert"], mesh.shape["seq"]
    fits = n_s % 2 == 0 and D * EXTRA // ROWS % (n_s * LANES) == 0
    body = functools.partial(local_fused, n_e, n_s) if fits else local
    return jax.shard_map(body, mesh=mesh, in_specs=in_specs, out_specs=out_specs, check_vma=False)
```

```python
import functools

import jax
import jax.numpy as jnp
from jax import lax
from jax.experimental import pallas as pl
from jax.experimental.pallas import tpu as pltpu
from jax.sharding import PartitionSpec as P

D = 2048
HSPLIT = 4
CAP = 12
ROWS = 16
EXTRA = ROWS - CAP
CHUNKS = CAP // EXTRA
LANES = 128
VMEM_BYTES = 61500 * 1024
MESH = pl.DeviceIdType.MESH
F32 = jnp.float32
BF16 = jnp.bfloat16


def contract_rows(left, right):
    return lax.dot_general(
        left, right, (((0,), (0,)), ((), ())), preferred_element_type=jnp.float32
    )


def contract_cols(left, right):
    return lax.dot_general(
        left, right, (((1,), (1,)), ((), ())), preferred_element_type=jnp.float32
    )


def local(tokens, out_grad, expert_ids, combine, w_gate, w_up, w_down):
    n_expert = lax.axis_size("expert")
    experts = n_expert // HSPLIT
    tok_dev = tokens.shape[0]
    slice_width = w_gate.shape[2]
    wanted = lax.broadcasted_iota(jnp.int32, (1, 1, experts), 2)
    chosen = expert_ids[:, :, None] == wanted
    routed = jnp.any(chosen, axis=1).astype(jnp.int32)
    earlier = jnp.cumsum(routed, axis=0, dtype=jnp.int32) - routed
    slot_ids = lax.broadcasted_iota(jnp.int32, (1, CAP, 1), 1)
    picker = (earlier.T[:, None, :] == slot_ids) & (routed.T[:, None, :] == 1)
    picker_bf = picker.astype(jnp.bfloat16)
    weight_te = jnp.sum(jnp.where(chosen, combine[:, :, None], 0.0), axis=1)
    send_x = jnp.einsum(
        "ect,td->ecd", picker_bf, tokens, preferred_element_type=jnp.float32
    ).astype(jnp.bfloat16)
    send_g = jnp.einsum(
        "ect,td->ecd", picker_bf, out_grad, preferred_element_type=jnp.float32
    ).astype(jnp.bfloat16)
    send_w = jnp.sum(jnp.where(picker, weight_te.T[:, None, :], 0.0), axis=2)
    out_x = jnp.repeat(send_x, HSPLIT, axis=0)
    out_g = jnp.repeat(send_g, HSPLIT, axis=0)
    out_w = jnp.repeat(send_w, HSPLIT, axis=0)
    rows_x = lax.all_to_all(out_x, "expert", split_axis=0, concat_axis=0, tiled=True)
    rows_g, rows_w = (
        lax.all_to_all(out_g, "expert", split_axis=0, concat_axis=0, tiled=True),
        lax.all_to_all(
            out_w.astype(jnp.bfloat16), "expert", split_axis=0, concat_axis=0, tiled=True
        ).astype(out_w.dtype),
    )
    flat_x = rows_x.reshape(-1, D)
    flat_g = rows_g.reshape(-1, D)
    flat_w = rows_w.reshape(-1)
    gate_cols = w_gate[0]
    up_cols = w_up[0]
    down_rows = w_down[0]
    gate_pre = jnp.dot(flat_x, gate_cols, preferred_element_type=jnp.float32)
    up_pre = jnp.dot(flat_x, up_cols, preferred_element_type=jnp.float32)
    sig_gate = jax.nn.sigmoid(gate_pre)
    act_gate = gate_pre * sig_gate
    hidden = (act_gate * up_pre).astype(jnp.bfloat16)
    expert_out = jnp.dot(hidden, down_rows, preferred_element_type=jnp.float32)
    comb_part = jnp.sum(flat_g.astype(jnp.float32) * expert_out, axis=1)
    scaled = (flat_w[:, None] * flat_g.astype(jnp.float32)).astype(jnp.bfloat16)
    hidden_grad = contract_cols(scaled, down_rows)
    grad_gate = (hidden_grad * up_pre * sig_gate * (1.0 + gate_pre * (1.0 - sig_gate))).astype(
        jnp.bfloat16
    )
    grad_up = (hidden_grad * act_gate).astype(jnp.bfloat16)
    back_rows = (contract_cols(grad_gate, gate_cols) + contract_cols(grad_up, up_cols)).astype(
        jnp.bfloat16
    )
    both_grads = jnp.concatenate([grad_gate, grad_up], axis=1)
    terms = jnp.concatenate(
        [contract_rows(flat_x, both_grads), contract_rows(scaled, hidden)], axis=1
    )
    summed = lax.psum_scatter(
        terms.astype(jnp.bfloat16), "seq", scatter_dimension=0, tiled=True
    ).astype(jnp.float32)
    weight_grads = summed.astype(jnp.bfloat16).reshape(1, summed.shape[0], 3, slice_width)
    ret_x, ret_c = (
        lax.all_to_all(
            back_rows.reshape(n_expert, CAP, D), "expert", split_axis=0, concat_axis=0, tiled=True
        ),
        lax.all_to_all(
            comb_part.reshape(n_expert, CAP).astype(jnp.bfloat16),
            "expert",
            split_axis=0,
            concat_axis=0,
            tiled=True,
        ).astype(jnp.float32),
    )
    spread = jnp.repeat(picker_bf, HSPLIT, axis=0).reshape(n_expert * CAP, tok_dev)
    grad_tokens = contract_rows(spread, ret_x.reshape(-1, D)).astype(jnp.bfloat16)
    comb_slots = jnp.sum(ret_c.reshape(experts, HSPLIT, CAP), axis=1)
    comb_te = jnp.sum(jnp.where(picker, comb_slots[:, :, None], 0.0), axis=1)
    grad_combine = jnp.sum(jnp.where(chosen, comb_te.T[:, None, :], 0.0), axis=2)
    return (grad_tokens, grad_combine, weight_grads)


def fused(n_e, n_s, tok_hbm, og_hbm, ids_hbm, comb_hbm, wg_hbm, wu_hbm, wd_hbm,
          gt_ref, gc_ref, wgr_ref,
          tok_ref, og_ref, ids_ref, comb_ref, wgu, wd, outx, outs, xs, ss, xa, sa, subs, ga, back, mid, tot, ret,
          w_sem, out_send, near_send, half_send, recv, half_recv,
          q_send, q_recv, g_send, g_recv,
          b_send, b_recv, m_send, m_recv, t_send, t_recv):
    me = lax.axis_index("expert")
    sq = lax.axis_index("seq")
    groups = n_e // HSPLIT
    grp = me // HSPLIT
    part = lax.rem(me, HSPLIT)
    near = (part + 1 - 2 * lax.rem(part, 2), lax.rem(part + 2, HSPLIT))
    rows = n_e * ROWS
    used = groups * ROWS
    width = wd.shape[0]
    toks, feats = tok_ref.shape
    top = ids_ref.shape[0]
    share = feats // n_s
    sub = share * EXTRA // ROWS
    head = CHUNKS * sub
    packed = n_s * head
    last = slice(packed, feats)
    halves = (slice(0, packed // 2), slice(packed // 2, packed))

    def lanes(s, m):
        return slice(s * head + m * sub, s * head + (m + 1) * sub)

    def by_share(ref, here, m):
        return jnp.concatenate([ref[here, lanes(s, m)] for s in range(n_s)], axis=1)

    wg = wgu.at[0:width, :]
    wu = wgu.at[width : 2 * width, :]
    pairs_in = [
        (ids_hbm, ids_ref), (comb_hbm, comb_ref), (tok_hbm, tok_ref), (og_hbm, og_ref)]
    for src, dst in ((wg_hbm.at[0], wg), (wu_hbm.at[0], wu), (wd_hbm.at[0], wd)):
        for s in range(n_s):
            pairs_in.append((src.at[:, s * share : s * share + head],
                             dst.at[:, s * head : (s + 1) * head]))
            pairs_in.append((src.at[:, s * share + head : (s + 1) * share],
                             dst.at[:, packed + s * sub : packed + (s + 1) * sub]))
    loads = [
        pltpu.make_async_copy(src, dst, w_sem.at[i]) for i, (src, dst) in enumerate(pairs_in)
    ]
    up_to = 4 + 4 * n_s
    for load in loads[:4]:
        load.start()

    def holder(g, p):
        return lax.rem(grp + g, groups) * HSPLIT + lax.rem(part + p, HSPLIT)

    met = [(holder(g, 0), sq) for g in range(1, groups)]
    met += [(holder(0, p), sq) for p in range(1, HSPLIT)]
    met += [(me, lax.rem(sq + step, n_s)) for step in range(1, n_s)]
    barrier = pltpu.get_barrier_semaphore()
    for device in met:
        pl.semaphore_signal(barrier, inc=1, device_id=device, device_id_type=MESH)

    def iota(shape, dim):
        return lax.broadcasted_iota(jnp.int32, shape, dim)

    def one_hot(mask):
        return mask.astype(F32).astype(BF16)

    def mm(left, right):
        return jnp.dot(left, right, preferred_element_type=F32)

    loads[0].wait()
    loads[1].wait()
    ids = ids_ref[...]
    comb = comb_ref[...]
    e_row = iota((used, toks), 0) // ROWS
    c_row = lax.rem(iota((used, toks), 0), ROWS)
    routed = jnp.zeros((used, toks), F32)
    weight = jnp.zeros((used, toks), F32)
    for k in range(top):
        hit = ids[k : k + 1, :] == e_row
        routed = jnp.where(hit, 1.0, routed)
        weight = jnp.where(hit, comb[k : k + 1, :], weight)
    earlier = mm(routed.astype(BF16), one_hot(iota((toks, toks), 0) < iota((toks, toks), 1)))

    def picked(slot, mask):
        return jnp.where(mask & (earlier == slot.astype(F32)), routed, 0.0)

    base = picked(c_row, c_row < CAP)
    tails = [picked(c_row - CAP + EXTRA * m, c_row >= CAP) for m in range(CHUNKS)]
    base_bf = base.astype(BF16)
    tails_bf = [tail.astype(BF16) for tail in tails]
    tails_all = jnp.concatenate(tails, axis=0).astype(BF16)

    def gather_to(out, ref, scales):
        for s in range(n_s):
            main = mm(base_bf, ref[:, s * share : s * share + head])
            tail = mm(tails_all, ref[:, s * share + head : (s + 1) * share])
            for m in range(CHUNKS):
                value = main[:, m * sub : (m + 1) * sub] + tail[m * used : (m + 1) * used]
                if scales is not None:
                    value = scales[m] * value
                out[:, lanes(s, m)] = value.astype(BF16)

    def at(i):
        return pl.ds(pl.multiple_of(i * ROWS, ROWS), ROWS)

    sends = []

    def send(src, dst, send_sem, recv_sem, device):
        copy = pltpu.make_async_remote_copy(
            src_ref=src, dst_ref=dst, send_sem=send_sem, recv_sem=recv_sem,
            device_id=device, device_id_type=MESH)
        copy.start()
        sends.append(copy)

    def arrived(ref, sem):
        pltpu.make_async_copy(ref, ref, sem).wait()

    full = slice(0, packed)
    landing = (xs, ss)

    def place(index, p):
        return at(index * HSPLIT + p)

    opposite = lax.rem(near[0] + 2, HSPLIT)

    def to_peers(a, slot, src, src_rows, dst_rows):
        for step in range(1, n_s):
            peer = lax.rem(sq + step, n_s)
            mine = pl.ds(pl.multiple_of(peer * head, LANES), head)
            send(src.at[src_rows, mine], (xa, sa)[a].at[sq, dst_rows, :],
                 q_send.at[a, slot, step - 1], q_recv.at[a, sq, slot], (me, peer))

    def pass_on(a, src, index):
        for n in range(2):
            send(src, landing[a].at[place(index, part), full], near_send.at[a, index, n],
                 recv.at[a, index, part], (grp * HSPLIT + near[n], sq))

    def first(a, out):
        for step in range(1, groups):
            to = lax.rem(grp + step, groups)
            send(out.at[at(to), :], landing[a].at[place(groups - step, part), full],
                 out_send.at[a, step - 1], recv.at[a, groups - step, part],
                 (to * HSPLIT + part, sq))

    def relay(a, index):
        for n in range(2):
            arrived(landing[a].at[place(index, near[n]), full], recv.at[a, index, near[n]])
            half = landing[a].at[place(index, near[n]), halves[n]]
            send(half, half, half_send.at[a, index, n], half_recv.at[a, index, n],
                 (grp * HSPLIT + near[1 - n], sq))
            if index == 0:
                to_peers(a, 1 + n, landing[a], place(0, near[n]), place(0, near[n]))

    def enter(a, index):
        block = landing[a].at[place(index, part), full]
        arrived(block, recv.at[a, index, part])
        pass_on(a, block, index)

    def far(a, index):
        source = lax.rem(near[0] + 2, HSPLIT)
        for n in range(2):
            arrived(landing[a].at[place(index, source), halves[n]], half_recv.at[a, index, n])

    loads[2].wait()
    gather_to(outx, tok_ref, None)
    pl.semaphore_wait(barrier, len(met))
    first(0, outx)
    pass_on(0, outx.at[at(grp), :], 0)
    to_peers(0, 0, outx, at(grp), place(0, part))
    loads[3].wait()
    gather_to(outs, og_ref, [
        jnp.sum((base + tail) * weight, axis=1, keepdims=True) for tail in tails])
    first(1, outs)
    to_peers(1, 0, outs, at(grp), place(0, part))
    for load in loads[4:]:
        load.start()
    xs[place(0, part), full] = outx[at(grp), :]
    ss[place(0, part), full] = outs[at(grp), :]

    def slots(count):
        at_r = iota((count, count), 0)
        at_c = iota((count, count), 1)
        return at_r // ROWS == at_c // ROWS, lax.rem(at_r, ROWS), lax.rem(at_c, ROWS)

    quad = HSPLIT * ROWS
    together, r_slot, c_slot = slots(quad)
    unfold = [
        one_hot(together & (c_slot >= CAP) & (c_slot - CAP + EXTRA * m == r_slot))
        for m in range(CHUNKS)
    ]
    fold = [
        one_hot(together & (r_slot >= CAP) & (r_slot - CAP + EXTRA * m == c_slot))
        for m in range(CHUNKS)
    ]
    valid = lax.rem(iota((width, quad), 1), ROWS) < CAP
    shares = (xa, sa)

    def group_rows(index):
        return slice(index * quad, (index + 1) * quad)

    def complete(a, index):
        far(a, index)
        ref = landing[a]
        here = group_rows(index)
        if index:
            to_peers(a, HSPLIT - 1 + index, ref, here, here)
        else:
            to_peers(a, HSPLIT - 1, ref, place(0, opposite), place(0, opposite))
        total = mm(unfold[0], by_share(ref, here, 0))
        for m in range(1, CHUNKS):
            total = total + mm(unfold[m], by_share(ref, here, m))
        ref[here, last] = total.astype(BF16)

    across = (((1,), (1,)), ((), ()))

    beyond = range(1, groups)
    for index in beyond:
        enter(0, index)
    relay(0, 0)
    for index in beyond:
        enter(1, index)
    pass_on(1, outs.at[at(grp), :], 0)
    for index in beyond:
        relay(0, index)
    complete(0, 0)
    for index in beyond:
        relay(1, index)
    for index in beyond:
        complete(0, index)
    for load in loads[4:up_to]:
        load.wait()
    gate_up = lax.dot_general(wgu[...], xs[...], across, preferred_element_type=F32)
    gate_all = gate_up[0:width]
    up_all = gate_up[width : 2 * width]
    sig_all = 1.0 / (1.0 + jnp.exp(-gate_all))
    act_all = gate_all * sig_all
    hidden_all = act_all * up_all
    d_gate_all = up_all * sig_all * (1.0 + gate_all * (1.0 - sig_all))
    relay(1, 0)
    for load in loads[up_to:]:
        load.wait()
    keep = lax.rem(iota((quad, sub), 0), ROWS) < CAP
    terms = [None] * groups

    def unit_grads(index):
        here = group_rows(index)
        complete(1, index)
        hgrad = jnp.where(
            valid, lax.dot_general(wd[...], ss[here, :], across, preferred_element_type=F32), 0.0)
        hidden = jnp.where(valid, hidden_all[:, here], 0.0).astype(BF16)
        g_gate_t = (hgrad * d_gate_all[:, here]).astype(BF16)
        g_up_t = (hgrad * act_all[:, here]).astype(BF16)
        terms[index] = (g_gate_t, g_up_t, hidden, hgrad)

    def row_grads(index):
        here = group_rows(index)
        g_gate_t, g_up_t, hidden, hgrad = terms[index]
        row_part = jnp.sum(hidden.astype(F32) * hgrad, axis=0, keepdims=True)
        back[here, packed : packed + LANES] = jnp.broadcast_to(
            row_part, (LANES, quad)).T.astype(BF16)
        g_gate = g_gate_t.T
        g_up = g_up_t.T
        tail_grad = (mm(g_gate, wg[:, last]) + mm(g_up, wu[:, last])).astype(BF16)
        folded = [mm(fold[m], tail_grad) for m in range(CHUNKS)]
        for s in range(n_s):
            span = slice(s * head, (s + 1) * head)
            whole = mm(g_gate, wg[:, span]) + mm(g_up, wu[:, span])
            for m in range(CHUNKS):
                back[here, lanes(s, m)] = jnp.where(
                    keep, whole[:, m * sub : (m + 1) * sub], folded[m][:, s * sub : (s + 1) * sub]
                ).astype(BF16)

    for index in beyond:
        unit_grads(index)
        row_grads(index)
        for p in range(1, HSPLIT):
            to = lax.rem(part + p, HSPLIT)
            send(back.at[place(index, to), :], mid.at[index - 1, part],
                 m_send.at[index - 1, p - 1], m_recv.at[index - 1, part], (holder(0, p), sq))
    unit_grads(0)

    def lanes_of(s):
        return pl.ds(pl.multiple_of(s * rows, LANES), rows)

    for i in range(3):
        ga[i * width : (i + 1) * width, lanes_of(sq)] = jnp.concatenate(
            [terms[index][i] for index in range(groups)], axis=1)
    pairs = n_s // 2
    core = lax.rem(sq, 2)
    mate = sq + 1 - 2 * core
    peers = [lax.rem(sq // 2 + step, pairs) * 2 + core for step in range(1, pairs)]

    def to_seq(source, count, peer):
        block = ga.at[:, lanes_of(source)]
        send(block, block, g_send.at[count], g_recv.at[source], (me, peer))

    for count, peer in enumerate(peers):
        to_seq(sq, count, peer)
    to_seq(sq, pairs - 1, mate)
    row_grads(0)

    for p in range(1, HSPLIT):
        send(back.at[place(0, lax.rem(part + p, HSPLIT)), :], ret.at[at(part), :],
             b_send.at[p - 1], b_recv.at[part], (holder(0, p), sq))
    ret[at(part), :] = back[place(0, part), :]
    for index in beyond:
        total = back[place(index, part), :].astype(F32)
        for p in range(1, HSPLIT):
            other = lax.rem(part + p, HSPLIT)
            arrived(mid.at[index - 1, other], m_recv.at[index - 1, other])
            total = total + mid[index - 1, other].astype(F32)
        tot[index - 1] = total.astype(BF16)
        send(tot.at[index - 1], ret.at[at(HSPLIT + groups - index - 1), :],
             t_send.at[index - 1], t_recv.at[groups - index - 1], (holder(index, 0), sq))

    landed = (HSPLIT + groups - 1) * ROWS

    def expert_at(block):
        return lax.rem(grp + jnp.maximum(block - HSPLIT + 1, 0), groups)

    def same(shape, ret_dim):
        of_ret = iota(shape, ret_dim)
        of_slot = iota(shape, 1 - ret_dim)
        return one_hot((expert_at(of_ret // ROWS) == of_slot // ROWS)
                       & (lax.rem(of_ret, ROWS) == lax.rem(of_slot, ROWS)))

    widen = same((landed, used), 0)
    home = mm(widen, base_bf).T.astype(BF16)
    home_tails = [mm(widen, tail).T.astype(BF16) for tail in tails_bf]
    gather = same((used, landed), 1)

    mine = pl.ds(pl.multiple_of(sq * head, LANES), head)
    xa[sq] = xs[:, mine]
    sa[sq] = ss[:, mine]
    for a, ref in enumerate(shares):
        for step in range(1, n_s):
            peer = lax.rem(sq + step, n_s)
            own_four = (part, near[0], near[1], opposite)
            arriving = [place(0, p) for p in own_four] + [group_rows(i) for i in beyond]
            for slot, here in enumerate(arriving):
                arrived(ref.at[peer, here, :], q_recv.at[a, peer, slot])
        found = jnp.zeros((quad, n_s * groups * sub), F32)
        for m in range(CHUNKS):
            found = found + mm(unfold[m], jnp.concatenate(
                [ref[s, group_rows(index), m * sub : (m + 1) * sub]
                 for s in range(n_s) for index in range(groups)], axis=1))
        for s in range(n_s):
            for index in range(groups):
                spot = s * groups + index
                subs[a, s, group_rows(index), :] = found[
                    :, spot * sub : (spot + 1) * sub].astype(BF16)
    for count, peer in enumerate(peers):
        arrived(ga.at[:, lanes_of(peer)], g_recv.at[peer])
        to_seq(peer, pairs + count, mate)
    arrived(ga.at[:, lanes_of(mate)], g_recv.at[mate])
    for peer in peers:
        twin = peer + 1 - 2 * core
        arrived(ga.at[:, lanes_of(twin)], g_recv.at[twin])
    every = n_s * rows
    for a, units in enumerate((slice(0, 2 * width), slice(2 * width, 3 * width))):
        wgr_ref[units, 0:head] = mm(
            ga[units, :], shares[a][...].reshape(every, head)).astype(BF16)
        wgr_ref[units, head:share] = mm(
            ga[units, :], subs[a].reshape(every, sub)).astype(BF16)

    for p in range(1, HSPLIT):
        other = lax.rem(part + p, HSPLIT)
        arrived(ret.at[at(other), :], b_recv.at[other])
    for index in beyond:
        arrived(ret.at[at(HSPLIT + index - 1), :], t_recv.at[index - 1])
    whole_ret = slice(0, landed)
    tail_sum = jnp.zeros((toks, n_s * sub), F32)
    for m in range(CHUNKS):
        tail_sum = tail_sum + mm(home_tails[m], by_share(ret, whole_ret, m))
    for s in range(n_s):
        gt_ref[:, s * share : s * share + head] = mm(
            home, ret[:, s * head : (s + 1) * head]).astype(BF16)
        gt_ref[:, s * share + head : (s + 1) * share] = tail_sum[
            :, s * sub : (s + 1) * sub].astype(BF16)
    per_slot = base * mm(gather, ret[:, packed : packed + LANES])
    at_k = iota((top, toks), 0)
    total = jnp.zeros((top, toks), F32)
    for k in range(top):
        mine = jnp.sum(jnp.where(ids[k : k + 1, :] == e_row, per_slot, 0.0), axis=0, keepdims=True)
        total = jnp.where(at_k == k, mine, total)
    gc_ref[...] = total / comb
    for copy in sends:
        copy.wait_send()


def local_fused(n_e, n_s, tokens, out_grad, expert_ids, combine, w_gate, w_up, w_down):
    toks, feats = tokens.shape
    width = w_gate.shape[2]
    share = feats // n_s
    groups = n_e // HSPLIT
    rows = n_e * ROWS
    packed = feats * CAP // ROWS
    crossing = max(1, groups - 1)
    dma = pltpu.SemaphoreType.DMA
    vmem = pl.BlockSpec(memory_space=pltpu.VMEM)
    hbm = pl.BlockSpec(memory_space=pl.ANY)
    grad_tokens, grad_combine, flat = pl.pallas_call(
        functools.partial(fused, n_e, n_s),
        out_shape=(
            pltpu.VMEM((toks, feats), BF16),
            pltpu.VMEM(combine.shape[::-1], F32),
            pltpu.VMEM((3 * width, share), BF16),
        ),
        in_specs=[hbm] * 7,
        out_specs=(vmem,) * 3,
        scratch_shapes=[
            pltpu.VMEM((toks, feats), BF16),
            pltpu.VMEM((toks, feats), BF16),
            pltpu.VMEM(expert_ids.shape[::-1], jnp.int32),
            pltpu.VMEM(combine.shape[::-1], F32),
            pltpu.VMEM((2 * width, feats), BF16),
            pltpu.VMEM((width, feats), BF16),
            pltpu.VMEM((groups * ROWS, packed), BF16),
            pltpu.VMEM((groups * ROWS, packed), BF16),
            pltpu.VMEM((rows, feats), BF16),
            pltpu.VMEM((rows, feats), BF16),
            pltpu.VMEM((n_s, rows, share * CAP // ROWS), BF16),
            pltpu.VMEM((n_s, rows, share * CAP // ROWS), BF16),
            pltpu.VMEM((2, n_s, rows, share * EXTRA // ROWS), BF16),
            pltpu.VMEM((3 * width, n_s * rows), BF16),
            pltpu.VMEM((rows, packed + LANES), BF16),
            pltpu.VMEM((crossing, HSPLIT, ROWS, packed + LANES), BF16),
            pltpu.VMEM((crossing, ROWS, packed + LANES), BF16),
            pltpu.VMEM(((HSPLIT + groups - 1) * ROWS, packed + LANES), BF16),
            dma((4 + 6 * n_s,)),
            dma((2, crossing)),
            dma((2, groups, 2)),
            dma((2, groups, 2)),
            dma((2, groups, HSPLIT)),
            dma((2, groups, 2)),
            dma((2, HSPLIT - 1 + groups, n_s - 1)),
            dma((2, n_s, HSPLIT - 1 + groups)),
            dma((n_s - 1,)),
            dma((n_s,)),
            dma((HSPLIT - 1,)),
            dma((HSPLIT,)),
            dma((crossing, HSPLIT - 1)),
            dma((crossing, HSPLIT)),
            dma((crossing,)),
            dma((crossing,)),
        ],
        compiler_params=pltpu.CompilerParams(
            collective_id=0, has_side_effects=True, vmem_limit_bytes=VMEM_BYTES),
        cost_estimate=pl.CostEstimate(
            flops=18 * rows * feats * width, bytes_accessed=8 * feats * width,
            transcendentals=rows * width),
    )(
        tokens, out_grad, expert_ids.T, combine.T,
        w_gate.transpose(0, 2, 1), w_up.transpose(0, 2, 1), w_down,
    )
    weight_grads = flat.reshape(1, 3, width, share).transpose(0, 3, 1, 2)
    return grad_tokens, grad_combine.T, weight_grads


def solution(mesh):
    in_specs = (
        P(("expert", "seq"), None),
        P(("expert", "seq"), None),
        P(("expert", "seq"), None),
        P(("expert", "seq"), None),
        P("expert", None, None),
        P("expert", None, None),
        P("expert", None, None),
    )
    out_specs = (
        P(("expert", "seq"), None),
        P(("expert", "seq"), None),
        P("expert", "seq", None, None),
    )
    n_e, n_s = mesh.shape["expert"], mesh.shape["seq"]
    fits = n_s % 2 == 0 and D * EXTRA // ROWS % (n_s * LANES) == 0
    body = functools.partial(local_fused, n_e, n_s) if fits else local
    return jax.shard_map(body, mesh=mesh, in_specs=in_specs, out_specs=out_specs, check_vma=False)
```
